128 devices in a mesh: dp: 8 (over y_hi, z), ctx: 16 (over x, y_lo, core).
Axes of the slice: x: 4, y: 4 (y_hi: 2, y_lo: 2; y = y_hi * 2 + y_lo), z: 4, core: 2. Of those that a mesh axis runs over, the one named last changes fastest.
Arguments:
- xs: bfloat16 [8, 3072, 4096], P('dp', 'ctx'), may hold values from -6 to 6
- z_gate: bfloat16 [8, 3072, 4096], P('dp', 'ctx'), may hold values from -6 to 6
- b_proj: bfloat16 [8, 3072, 256], P('dp', 'ctx'), may hold values from -3 to 3
- c_proj: bfloat16 [8, 3072, 256], P('dp', 'ctx'), may hold values from -3 to 3
- dt_raw: bfloat16 [8, 3072, 64], P('dp', 'ctx'), may hold values from -2.5 to 7.5
- a_log: float32 [64], replicated
- dt_bias: float32 [64], replicated, may hold values from -0.5 to 0.5
- d_skip: float32 [64], replicated, may hold values from 0.5 to 1.5
- norm_gain: float32 [4096], replicated, may hold values from 0.25 to 1.75
- w_out: bfloat16 [4096, 2048], P('dp'), may hold values from -0.09375 to 0.09375
- cotangent: bfloat16 [8, 3072, 2048], P('dp', 'ctx'), may hold values from -6 to 6
Outputs:
- layer_out: bfloat16 [8, 3072, 2048], P('dp', 'ctx')
- grad_xs: bfloat16 [8, 3072, 4096], P('dp', 'ctx')
- grad_gate: bfloat16 [8, 3072, 4096], P('dp', 'ctx')
- grad_b: bfloat16 [8, 3072, 256], P('dp', 'ctx')
- grad_c: bfloat16 [8, 3072, 256], P('dp', 'ctx')
- grad_dt: bfloat16 [8, 3072, 64], P('dp', 'ctx')
- grad_w_out: float32 [4096, 2048], P('dp')
The draws below stay inside these ranges and needn't reach their ends.
All inputs are finite; a program needn't handle non-finite values.
Results may differ from the reference program's by a relative error of at most 0.012.
Values may be sent and summed in bfloat16 or wider, within the bound.
A program may use at most 384 MiB of HBM per device.

```python
import math
import jax
import jax.numpy as jnp
from jax import lax

D = 2048
H = 64
P_SIZE = 64
N = 64
G = 4
E = 4096
LEN = 3072
SEQS = 8


def draw_a_log(key, part):
    key = jax.random.fold_in(key, 11)
    selection_key, slow_key, fast_key = jax.random.split(key, 3)
    share = 0.5
    chosen = jax.random.uniform(selection_key, (H,)) < share
    slow = jax.random.uniform(slow_key, (H,), minval=math.log(0.3), maxval=math.log(1.5)) - jnp.log(LEN * 1.0)
    fast = jax.random.uniform(fast_key, (H,), minval=math.log(0.02), maxval=math.log(0.05))
    return jnp.where(chosen, slow, fast).astype(jnp.float32)


def draw_dt_raw(key, part):
    key = jax.random.fold_in(key, 12)
    base_key, spot_key, lift_key = jax.random.split(key, 3)
    starting_value = jnp.clip(0.6 * jax.random.normal(base_key, (SEQS, LEN, H)), -2.5, 2.5)
    chosen_locations = jax.random.randint(spot_key, (SEQS, 3), 0, LEN)
    location_list = jnp.arange(LEN)
    sudden_spread = jnp.any(location_list[None, :, None] == chosen_locations[:, None, :], axis=2)
    raised_copy = jax.random.uniform(lift_key, (SEQS, 1, H), minval=3.0, maxval=5.0)
    return (starting_value + jnp.where(sudden_spread[:, :, None], raised_copy, 0.0)).astype(jnp.bfloat16)


def levels(key, dims, shards, smallest, high):
    def one(axis_at, shards_of):
        draws = jax.random.uniform(jax.random.fold_in(jax.random.fold_in(key, 6), axis_at), (shards_of,), jnp.float32, smallest / len(shards), high / len(shards))
        return jnp.repeat(jnp.exp(draws), dims[axis_at] // shards_of).reshape((-1,) + (1,) * (len(dims) - axis_at - 1))

    level = one(*shards[0])
    for cut in shards[1:]:
        level = level * one(*cut)
    return level


def noise(rng, shape, spread, most, cuts=(), kind=jnp.bfloat16):
    array = jax.random.normal(rng, shape, jnp.float32) * spread
    if len(cuts) > 0:
        array = levels(rng, shape, cuts, -0.22, 0.18) * array
    return jnp.clip(array, min=-most, max=most).astype(kind)


def setup_inputs(seed: int = 0) -> dict:
    key_list = jax.random.split(jax.random.key(seed), 12)
    xs = noise(key_list[0], (SEQS, LEN, E), 1.0, 6.0, ((0, 8), (1, 16)))
    z_gate = noise(key_list[1], (SEQS, LEN, E), 1.0, 6.0, ((0, 8), (1, 16)))
    b_proj = noise(key_list[2], (SEQS, LEN, G * N), 0.5, 3.0, ((0, 8), (1, 16)))
    c_proj = noise(key_list[3], (SEQS, LEN, G * N), 0.5, 3.0, ((0, 8), (1, 16)))
    dt_raw = draw_dt_raw(jax.random.fold_in(key_list[11], 71), 0)
    a_log = draw_a_log(jax.random.fold_in(key_list[11], 71), 0)
    dt_bias = jnp.clip(jax.random.uniform(key_list[6], (H,), jnp.float32, -0.5, 0.5), -0.5, 0.5)
    d_skip = jnp.clip(jax.random.uniform(key_list[7], (H,), jnp.float32, 0.5, 1.5), 0.5, 1.5)
    norm_gain = jnp.clip(1.0 + 0.15 * jax.random.normal(key_list[8], (E,), jnp.float32), 0.25, 1.75)
    w_out = noise(key_list[9], (E, D), E ** -0.5, 0.09375, ((0, 8),))
    cotangent = noise(key_list[10], (SEQS, LEN, D), 1.0, 6.0, ((0, 8), (1, 16)))
    return {"xs": xs, "z_gate": z_gate, "b_proj": b_proj, "c_proj": c_proj, "dt_raw": dt_raw, "a_log": a_log, "dt_bias": dt_bias, "d_skip": d_skip, "norm_gain": norm_gain, "w_out": w_out, "cotangent": cotangent}


PRECISE = lax.Precision.HIGHEST
EPSILON = 1e-05

def block_math(state, x_blk, rate_blk, b_blk, c_blk, a_neg):
    block_len = x_blk.shape[0]
    running = jnp.cumsum(rate_blk * a_neg, axis=0)
    log_gap = running[:, None] - running[None, :]
    positions = jnp.arange(block_len)
    causal = (positions[:, None] >= positions[None, :])[:, :, None, None]
    decays = jnp.where(causal, jnp.exp(jnp.where(causal, log_gap, 0.0)), 0.0)
    intersection = jnp.einsum('tgn,sgn->tsg', c_blk, b_blk, precision=PRECISE)
    scores = intersection[..., None] * decays
    scaled = x_blk * rate_blk[..., None]
    within = jnp.einsum('tsgk,sgkp->tgkp', scores, scaled, precision=PRECISE)
    carried = jnp.einsum('tgn,gkpn->tgkp', c_blk, state, precision=PRECISE) * jnp.exp(running)[..., None]
    to_end = jnp.exp(running[-1][None] - running)
    fresh = jnp.einsum('sgkp,sgn->gkpn', scaled * to_end[..., None], b_blk, precision=PRECISE)
    return (state * jnp.exp(running[-1])[..., None, None] + fresh, within + carried)

def ssd_all(values, raw_rates, input_matrix_values, c_vals, a_log, dt_bias, d_skip):
    heads_group = H // G
    a_neg = -jnp.exp(a_log).reshape(G, heads_group)
    block_len = math.gcd(256, LEN)
    block_count = LEN // block_len

    def advance(current, pieces):
        return block_math(current, pieces[0], pieces[1], pieces[2], pieces[3], a_neg)
    advance_saved = jax.checkpoint(advance)

    def per_sequence(inputs_one):
        x_seq, raw_seq, b_seq, c_seq = inputs_one
        rates = jax.nn.softplus(raw_seq.reshape(LEN, G, heads_group) + dt_bias.reshape(G, heads_group))
        x_grid = x_seq.reshape(LEN, G, heads_group, P_SIZE)
        blocks = (x_grid.reshape(block_count, block_len, G, heads_group, P_SIZE), rates.reshape(block_count, block_len, G, heads_group), b_seq.reshape(block_count, block_len, G, N), c_seq.reshape(block_count, block_len, G, N))
        start_state = jnp.zeros((G, heads_group, P_SIZE, N), jnp.float32)
        _, outputs = lax.scan(advance_saved, start_state, blocks)
        outputs = outputs.reshape(LEN, G, heads_group, P_SIZE) + d_skip.reshape(G, heads_group)[:, :, None] * x_grid
        return outputs.reshape(LEN, H * P_SIZE)
    return lax.map(per_sequence, (values, raw_rates, input_matrix_values, c_vals))

def reference(xs, z_gate, b_proj, c_proj, dt_raw, a_log, dt_bias, d_skip, norm_gain, w_out, cotangent):
    values = xs.astype(jnp.float32)
    raw_rates = dt_raw.astype(jnp.float32)
    input_matrix_values = b_proj.astype(jnp.float32)
    c_vals = c_proj.astype(jnp.float32)

    def forward_ssd(values_in, raw_in, b_in, c_in):
        return ssd_all(values_in, raw_in, b_in, c_in, a_log, dt_bias, d_skip)
    ssd_out, ssd_back = jax.vjp(forward_ssd, values, raw_rates, input_matrix_values, c_vals)
    z_float = z_gate.astype(jnp.float32)
    z_silu = jax.nn.silu(z_float)
    gated = ssd_out * z_silu
    rscale = lax.rsqrt(lax.optimization_barrier(jnp.mean(gated * gated, axis=-1, keepdims=True)) + EPSILON)
    normed = (gated * rscale * norm_gain).astype(jnp.bfloat16)
    flat_normed = normed.reshape(SEQS * LEN, E)
    flat_cot = cotangent.reshape(SEQS * LEN, D)
    layer_out = jnp.dot(flat_normed, w_out, preferred_element_type=jnp.float32).astype(jnp.bfloat16)
    d_normed = lax.dot_general(flat_cot, w_out, (((1,), (1,)), ((), ())), preferred_element_type=jnp.float32).astype(jnp.bfloat16)
    grad_w_out = lax.dot_general(flat_normed, flat_cot, (((0,), (0,)), ((), ())), preferred_element_type=jnp.float32)
    d_gain_in = d_normed.reshape(SEQS, LEN, E).astype(jnp.float32) * norm_gain
    inner_mean = lax.optimization_barrier(jnp.mean(d_gain_in * gated, axis=-1, keepdims=True))
    d_gated = rscale * (d_gain_in - gated * rscale * rscale * inner_mean)
    sigma = jax.nn.sigmoid(z_float)
    grad_gate = (d_gated * ssd_out * sigma * (1.0 + z_float * (1.0 - sigma))).astype(jnp.bfloat16)
    d_ssd = d_gated * z_silu
    d_values, d_raw, d_b, d_c = ssd_back(d_ssd)
    return (layer_out.reshape(SEQS, LEN, D), d_values.astype(jnp.bfloat16), grad_gate, d_b.astype(jnp.bfloat16), d_c.astype(jnp.bfloat16), d_raw.astype(jnp.bfloat16), grad_w_out)
```

```python
import math

import jax
import jax.numpy as jnp
from jax import lax
from jax.experimental import pallas as pl
from jax.experimental.pallas import tpu as pltpu
from jax.sharding import PartitionSpec as P

H = 64
P_SIZE = 64
N = 64
G = 4
E = 4096
HG = H // G
EG = E // G
EPSILON = 1e-05
LOG2E = math.log2(math.e)
EXT = 80
bf16 = jnp.bfloat16
f32 = jnp.float32
VMEM_LIMIT = 60 * 1024 * 1024


def dot(a, b):
    return lax.dot_general(a, b, (((1,), (0,)), ((), ())), preferred_element_type=f32)


def dot_nt(a, b):
    return lax.dot_general(a, b, (((1,), (1,)), ((), ())), preferred_element_type=f32)


def dot_tn(a, b):
    return lax.dot_general(a, b, (((0,), (0,)), ((), ())), preferred_element_type=f32)


def split3(v):
    a = v.astype(bf16)
    rest = v - a.astype(f32)
    b = rest.astype(bf16)
    c = (rest - b.astype(f32)).astype(bf16)
    return a, b, c


def mask_dot(mask, v):
    a, b, c = split3(v)
    return dot(mask, a) + dot(mask, b) + dot(mask, c)


def low_half(rows):
    return lax.broadcasted_iota(jnp.int32, (rows, 128), 1) < P_SIZE


def pair(values, p, low):
    return jnp.where(low, values[:, 2 * p : 2 * p + 1], values[:, 2 * p + 1 : 2 * p + 2])


def state_kernel(x_ref, b_ref, c_ref, dt_ref, al_ref, bias_ref,
                 s_ref, ext_ref, xr_ref, xw_ref, lg_ref, rg_ref, lt_ref, bg_ref, cg_ref):
    rows = x_ref.shape[0]
    rate = jax.nn.softplus(dt_ref[...].astype(f32) + bias_ref[...])
    steps = rate * (-LOG2E * jnp.exp(al_ref[...]))
    t_pos = lax.broadcasted_iota(jnp.int32, (rows, rows), 0)
    s_pos = lax.broadcasted_iota(jnp.int32, (rows, rows), 1)
    log = mask_dot((t_pos >= s_pos).astype(bf16), steps)
    lt_ref[...] = log.T
    last = log[rows - 1 : rows, :]
    to_end = jnp.exp2(last - log)
    low = low_half(rows)
    low1 = low_half(1)
    for g in range(G):
        lg_ref[g] = log[:, g * HG : (g + 1) * HG]
        rg_ref[g] = rate[:, g * HG : (g + 1) * HG]
        bg_ref[g] = b_ref[:, g * N : (g + 1) * N]
        cg_ref[g] = c_ref[:, g * N : (g + 1) * N]
    for p in range(H // 2):
        lanes = slice(p * 128, (p + 1) * 128)
        xr = x_ref[:, lanes].astype(f32) * pair(rate, p, low)
        xr_ref[:, lanes] = xr.astype(bf16)
        xw_ref[:, lanes] = (xr * pair(to_end, p, low)).astype(bf16)
        total = pair(last, p, low1)
        hi, mid, lo = split3(total)
        ext_ref[N : N + 1, lanes] = hi
        ext_ref[N + 1 : N + 2, lanes] = mid
        ext_ref[N + 2 : N + 3, lanes] = lo
        ext_ref[N + 3 : EXT, lanes] = jnp.zeros((EXT - N - 3, 128), bf16)
    for g in range(G):
        lanes = slice(g * EG, (g + 1) * EG)
        state = dot_tn(bg_ref[g], xw_ref[:, lanes])
        s_ref[:, lanes] = state
        ext_ref[0:N, lanes] = state.astype(bf16)


def link_kernel(reverse, ext_ref, out_ref):
    count = ext_ref.shape[0]
    acc = jnp.zeros((N, ext_ref.shape[2]), f32)
    for step in range(count):
        j = count - 1 - step if reverse else step
        out_ref[j] = acc.astype(bf16)
        rows = ext_ref[j].astype(f32)
        total = rows[N : N + 1] + rows[N + 1 : N + 2] + rows[N + 2 : N + 3]
        acc = jnp.exp2(total) * acc + rows[0:N]


def forward_kernel(x_ref, xr_ref, z_ref, lg_ref, lt_ref, bg_ref, cg_ref, sin_ref, skip_ref, gain_ref,
                   y_ref, normed_ref, r_ref, gated_ref, ss_ref):
    rows = x_ref.shape[0]
    low = low_half(rows)
    low1 = low_half(1)
    t_pos = lax.broadcasted_iota(jnp.int32, (rows, rows), 0)
    s_pos = lax.broadcasted_iota(jnp.int32, (rows, rows), 1)
    causal = t_pos >= s_pos
    ss_ref[...] = jnp.zeros_like(ss_ref)

    def group(g, _):
        base = pl.multiple_of(g * EG, EG)
        log = lg_ref[g]
        log_t = lt_ref[pl.ds(pl.multiple_of(g * HG, HG), HG), :]
        grown = jnp.exp2(log)
        cb = dot_nt(cg_ref[g], bg_ref[g])
        c_blk = cg_ref[g]
        total = ss_ref[...]
        for p in range(HG // 2):
            lanes = pl.ds(pl.multiple_of(base + p * 128, 128), 128)
            parts = []
            for h in (2 * p, 2 * p + 1):
                gap = jnp.where(causal, log[:, h : h + 1] - log_t[h : h + 1, :], -1e30)
                parts.append((cb * jnp.exp2(gap)).astype(bf16))
            both = dot(jnp.concatenate(parts, axis=0), xr_ref[:, lanes])
            y = jnp.where(low, both[:rows], both[rows:])
            y = y + pair(grown, p, low) * dot(c_blk, sin_ref[:, lanes])
            y_ref[:, lanes] = y
            out = y + pair(skip_ref[g], p, low1) * x_ref[:, lanes].astype(f32)
            z = z_ref[:, lanes].astype(f32)
            gated = out * (z * jax.nn.sigmoid(z))
            gated_ref[:, lanes] = gated
            total = total + gated * gated
        ss_ref[...] = total
        return 0

    lax.fori_loop(0, G, group, 0)
    r = lax.rsqrt(jnp.sum(ss_ref[...], axis=1, keepdims=True) * (1.0 / E) + EPSILON)
    r_ref[...] = jnp.broadcast_to(r, r_ref.shape)

    def finish(i, _):
        lanes = pl.ds(pl.multiple_of(i * 512, 512), 512)
        normed_ref[:, lanes] = (gated_ref[:, lanes] * r * gain_ref[:, lanes]).astype(bf16)
        return 0

    lax.fori_loop(0, E // 512, finish, 0)


def gate_kernel(dn_ref, y_ref, x_ref, z_ref, r_ref, lg_ref, cg_ref, skip_ref, gain_ref, ext_ref,
                dz_ref, dy_ref, dyel_ref, gext_ref, acc_ref):
    rows = x_ref.shape[0]
    low = low_half(rows)
    low1 = low_half(1)
    r = r_ref[...]
    acc_ref[...] = jnp.zeros_like(acc_ref)

    def first(g, _):
        base = pl.multiple_of(g * EG, EG)
        acc = acc_ref[...]
        for p in range(HG // 2):
            lanes = pl.ds(pl.multiple_of(base + p * 128, 128), 128)
            z = z_ref[:, lanes].astype(f32)
            out = y_ref[:, lanes] + pair(skip_ref[g], p, low1) * x_ref[:, lanes].astype(f32)
            gated = out * (z * jax.nn.sigmoid(z))
            acc = acc + dn_ref[:, lanes].astype(f32) * gain_ref[:, lanes] * gated
        acc_ref[...] = acc
        return 0

    lax.fori_loop(0, G, first, 0)
    inner = jnp.sum(acc_ref[...], axis=1, keepdims=True) * (1.0 / E)
    scaled = r * r * inner

    def second(g, _):
        base = pl.multiple_of(g * EG, EG)
        grown = jnp.exp2(lg_ref[g])
        for p in range(HG // 2):
            lanes = pl.ds(pl.multiple_of(base + p * 128, 128), 128)
            z = z_ref[:, lanes].astype(f32)
            sig = jax.nn.sigmoid(z)
            silu = z * sig
            out = y_ref[:, lanes] + pair(skip_ref[g], p, low1) * x_ref[:, lanes].astype(f32)
            dg = dn_ref[:, lanes].astype(f32) * gain_ref[:, lanes]
            d_gated = r * (dg - out * silu * scaled)
            dz_ref[:, lanes] = (d_gated * out * (sig * (1.0 + z * (1.0 - sig)))).astype(bf16)
            dy = d_gated * silu
            dy_ref[:, lanes] = dy.astype(bf16)
            dyel_ref[:, lanes] = (dy * pair(grown, p, low)).astype(bf16)
        lanes = pl.ds(base, EG)
        gext_ref[0:N, lanes] = dot_tn(cg_ref[g], dyel_ref[:, lanes]).astype(bf16)
        return 0

    lax.fori_loop(0, G, second, 0)
    gext_ref[N:EXT, :] = ext_ref[N:EXT, :]


def backward_kernel(x_ref, xr_ref, xw_ref, dy_ref, dyel_ref, y_ref, lg_ref, rg_ref, lt_ref, bg_ref, cg_ref,
                    sin_ref, s_ref, reach_ref, skip_ref, dt_ref, al_ref, bias_ref,
                    dx_ref, db_ref, dc_ref, ddt_ref,
                    fresh_ref, q1h_ref, q1l_ref, q2_ref, dcb_ref, qs_ref, dbg_ref, dcg_ref):
    rows = x_ref.shape[0]
    low = low_half(rows)
    low1 = low_half(1)
    s_pos = lax.broadcasted_iota(jnp.int32, (rows, rows), 0)
    t_pos = lax.broadcasted_iota(jnp.int32, (rows, rows), 1)
    causal = t_pos >= s_pos
    e_pos = lax.broadcasted_iota(jnp.int32, (EG, HG), 0)
    h_pos = lax.broadcasted_iota(jnp.int32, (EG, HG), 1)
    heads = ((e_pos // P_SIZE) == h_pos).astype(bf16)

    def group(g, _):
        base = pl.multiple_of(g * EG, EG)
        wide = pl.ds(base, EG)
        log = lg_ref[g]
        rate = rg_ref[g]
        log_t = lt_ref[pl.ds(pl.multiple_of(g * HG, HG), HG), :]
        b_blk = bg_ref[g]
        c_blk = cg_ref[g]
        last = log[rows - 1 : rows, :]
        to_end = jnp.exp2(last - log)
        cbt = dot_nt(b_blk, c_blk)
        reach = reach_ref[:, wide]
        fresh_ref[...] = dot(b_blk, reach)
        dcb_ref[...] = jnp.zeros_like(dcb_ref)
        for p in range(HG // 2):
            here = slice(p * 128, (p + 1) * 128)
            lanes = pl.ds(pl.multiple_of(base + p * 128, 128), 128)
            dy = dy_ref[:, lanes]
            xr = xr_ref[:, lanes]
            decays = []
            parts = []
            for h in (2 * p, 2 * p + 1):
                gap = jnp.where(causal, log_t[h : h + 1, :] - log[:, h : h + 1], -1e30)
                decay = jnp.exp2(gap)
                decays.append(decay)
                parts.append((cbt * decay).astype(bf16))
            both = dot(jnp.concatenate(parts, axis=0), dy)
            dxr = jnp.where(low, both[:rows], both[rows:])
            dxr = dxr + pair(to_end, p, low) * fresh_ref[:, here]
            zero = jnp.zeros_like(xr)
            halves = jnp.concatenate([jnp.where(low, xr, zero), jnp.where(low, zero, xr)], axis=0)
            dm = dot_nt(halves, dy)
            dcb_ref[...] += dm[:rows] * decays[0] + dm[rows:] * decays[1]
            x = x_ref[:, lanes].astype(f32)
            dyf = dy.astype(f32)
            dx_ref[:, lanes] = (dxr * pair(rate, p, low) + pair(skip_ref[g], p, low1) * dyf).astype(bf16)
            q1 = dyf * y_ref[:, lanes] - xr.astype(f32) * dxr
            hi = q1.astype(bf16)
            q1h_ref[:, here] = hi
            q1l_ref[:, here] = (q1 - hi.astype(f32)).astype(bf16)
            q2_ref[:, here] = (x * dxr).astype(bf16)
        dcb = dcb_ref[...].astype(bf16)
        dbg_ref[g] = dot(dcb, c_blk) + dot_nt(xw_ref[:, wide], reach)
        dcg_ref[g] = dot_tn(dcb, b_blk) + dot_nt(dyel_ref[:, wide], sin_ref[:, wide])
        through = (jnp.sum(sin_ref[:, wide].astype(f32) * reach.astype(f32), axis=0, keepdims=True),
                   jnp.sum(s_ref[:, wide] * reach.astype(f32), axis=0, keepdims=True))
        sums = []
        for v in through:
            a, b, _ = split3(jnp.broadcast_to(v, (16, EG)))
            sums.append((dot(a, heads) + dot(b, heads))[0:1])
        at_end = jnp.exp2(last) * sums[0] + sums[1]
        q1 = dot(q1h_ref[...], heads) + dot(q1l_ref[...], heads)
        d_log = mask_dot(causal.astype(bf16), q1) + at_end
        qs_ref[g] = d_log
        rg2 = dot(q2_ref[...], heads)
        qs_ref[G + g] = rg2
        return 0

    lax.fori_loop(0, G, group, 0)
    a_neg = -jnp.exp(al_ref[...])
    slope = jax.nn.sigmoid(dt_ref[...].astype(f32) + bias_ref[...])
    for g in range(G):
        heads_here = slice(g * HG, (g + 1) * HG)
        d_rate = a_neg[:, heads_here] * qs_ref[g] + qs_ref[G + g]
        ddt_ref[:, heads_here] = (d_rate * slope[:, heads_here]).astype(bf16)
        db_ref[:, g * N : (g + 1) * N] = dbg_ref[g].astype(bf16)
        dc_ref[:, g * N : (g + 1) * N] = dcg_ref[g].astype(bf16)


def call(kernel, outs, scratch, *args):
    return pl.pallas_call(
        kernel,
        out_shape=[jax.ShapeDtypeStruct(s, d) for s, d in outs],
        in_specs=[pl.BlockSpec(memory_space=pltpu.VMEM)] * len(args),
        out_specs=[pl.BlockSpec(memory_space=pltpu.VMEM)] * len(outs),
        scratch_shapes=[pltpu.VMEM(s, d) for s, d in scratch],
        compiler_params=pltpu.CompilerParams(vmem_limit_bytes=VMEM_LIMIT),
    )(*args)


def link(ext, reverse):
    count = lax.axis_size("ctx")
    share = E // count
    mine = lax.all_to_all(ext, "ctx", split_axis=1, concat_axis=0, tiled=True).reshape(count, EXT, share)
    (out,) = call(lambda e, o: link_kernel(reverse, e, o), [((count, N, share), bf16)], [], mine)
    return lax.all_to_all(out.reshape(count * N, share), "ctx", split_axis=0, concat_axis=1, tiled=True)


def shards(xs, z_gate, b_proj, c_proj, dt_raw, a_log, dt_bias, d_skip, norm_gain, w_out, cotangent):
    rows = xs.shape[1]
    x, z, b, c, dt, cot = xs[0], z_gate[0], b_proj[0], c_proj[0], dt_raw[0], cotangent[0]
    al, bias, gain = a_log[None], dt_bias[None], norm_gain[None]
    skip = d_skip.reshape(G, 1, HG)
    width = w_out.shape[1]
    full_weight = lax.all_gather(w_out, "dp", axis=0, tiled=True)
    d_normed = lax.dot_general(
        cot, full_weight, (((1,), (1,)), ((), ())), preferred_element_type=f32
    ).astype(bf16)
    wide16 = ((rows, E), bf16)
    s_loc, ext, xr, xw, lg, rg, lt, bg, cg = call(
        state_kernel,
        [((N, E), f32), ((EXT, E), bf16), wide16, wide16, ((G, rows, HG), f32), ((G, rows, HG), f32),
         ((H, rows), f32), ((G, rows, N), bf16), ((G, rows, N), bf16)],
        [], x, b, c, dt, al, bias)
    s_in = link(ext, False)
    y, normed, r = call(
        forward_kernel,
        [((rows, E), f32), wide16, ((rows, 128), f32)],
        [((rows, E), f32), ((rows, 128), f32)],
        x, xr, z, lg, lt, bg, cg, s_in, skip, gain)
    dz, dy, dyel, gext = call(
        gate_kernel,
        [wide16, wide16, wide16, ((EXT, E), bf16)],
        [((rows, 128), f32)],
        d_normed, y, x, z, r, lg, cg, skip, gain, ext)
    reach = link(gext, True)
    dx, db, dc, ddt = call(
        backward_kernel,
        [wide16, ((rows, G * N), bf16), ((rows, G * N), bf16), ((rows, H), bf16)],
        [((rows, EG), f32), ((rows, EG), bf16), ((rows, EG), bf16), ((rows, EG), bf16), ((rows, rows), f32),
         ((2 * G, rows, HG), f32), ((G, rows, N), f32), ((G, rows, N), f32)],
        x, xr, xw, dy, dyel, y, lg, rg, lt, bg, cg, s_in, s_loc, reach, skip, dt, al, bias)

    layer_out = jnp.dot(normed, full_weight, preferred_element_type=f32).astype(bf16)
    columns = lax.all_to_all(normed, "dp", split_axis=1, concat_axis=0, tiled=True)
    cot_all = lax.all_gather(cot, "dp", axis=0, tiled=True)
    grad_local = lax.dot_general(
        columns, cot_all, (((0,), (0,)), ((), ())), preferred_element_type=f32
    ).astype(bf16)
    count = lax.axis_size("ctx")
    pieces = lax.all_to_all(grad_local, "ctx", split_axis=0, concat_axis=0, tiled=True)
    piece = jnp.sum(pieces.reshape(count, -1, width).astype(f32), axis=0).astype(bf16)
    grad_w = lax.all_gather(piece, "ctx", axis=0, tiled=True).astype(f32)
    return layer_out[None], dx[None], dz[None], db[None], dc[None], ddt[None], grad_w


def solution(mesh):
    rows = P("dp", "ctx", None)
    in_specs = (rows,) * 5 + (P(),) * 4 + (P("dp", None), rows)
    out_specs = (rows,) * 6 + (P("dp", None),)
    return jax.shard_map(shards, mesh=mesh, in_specs=in_specs, out_specs=out_specs, check_vma=False)
```

```python
import math

import jax
import jax.numpy as jnp
from jax import lax
from jax.experimental import pallas as pl
from jax.experimental.pallas import tpu as pltpu
from jax.sharding import PartitionSpec as P

H = 64
P_SIZE = 64
N = 64
G = 4
E = 4096
HG = H // G
EG = E // G
EPSILON = 1e-05
LOG2E = math.log2(math.e)
EXT = 80
bf16 = jnp.bfloat16
f32 = jnp.float32
VMEM_LIMIT = 63 * 1024 * 1024
MESH = pl.DeviceIdType.MESH


def dot(a, b):
    return lax.dot_general(a, b, (((1,), (0,)), ((), ())), preferred_element_type=f32)


def dot_nt(a, b):
    return lax.dot_general(a, b, (((1,), (1,)), ((), ())), preferred_element_type=f32)


def dot_tn(a, b):
    return lax.dot_general(a, b, (((0,), (0,)), ((), ())), preferred_element_type=f32)


def split3(v):
    a = v.astype(bf16)
    rest = v - a.astype(f32)
    b = rest.astype(bf16)
    c = (rest - b.astype(f32)).astype(bf16)
    return a, b, c


def mask_dot(mask, v):
    a, b, c = split3(v)
    return dot(mask, a) + dot(mask, b) + dot(mask, c)


def low_half(rows):
    return lax.broadcasted_iota(jnp.int32, (rows, 128), 1) < P_SIZE


def pair(values, p, low):
    return jnp.where(low, values[:, 2 * p : 2 * p + 1], values[:, 2 * p + 1 : 2 * p + 2])


NZ = 4
NX = 4
NDP = 2 * NZ
NCTX = 4 * NX
SHARE = E // NCTX


def layer_kernel(x_ref, z_ref, b_ref, c_ref, dt_ref, al_ref, bias_ref, skip_ref, gain_ref, w_ref, cot_ref,
                 out_ref, dx_ref, dz_ref, db_ref, dc_ref, ddt_ref, gw_ref,
                 w_all, cot_all, nb, nrecv, xr_ref, xw_ref, y_ref, wide_ref, dn_ref, dy_ref, dyel_ref,
                 lay_ref, dcb_ref, qs_ref, dbg_ref, dcg_ref,
                 lg_ref, rg_ref, lt_ref, bg_ref, cg_ref, acc_ref,
                 ext_ref, mine_ref, link_ref, sin_ref, gext_ref, gmine_ref, reach_ref,
                 own_ref, other_ref, sib_ref, rs_ref, piece_ref,
                 local_sem, w_send, w_recv, c_send, c_recv, n_send, n_recv,
                 a_send, a_recv, o_send, o_recv, ga_send, ga_recv, go_send, go_recv,
                 b_send, b_recv, r_send, r_recv, p_send, p_recv, f_send, f_recv):
    rows = x_ref.shape[0]
    width = cot_ref.shape[1]
    half_width = width // 2
    shard = w_ref.shape[0]
    half = shard // 2
    quarter = shard // 4
    dp = lax.axis_index("dp")
    ctx = lax.axis_index("ctx")
    yh, z = dp // NZ, dp % NZ
    x, yl, core = ctx // 4, (ctx // 2) % 2, ctx % 2
    z_up, z_down = (z + 1) % NZ, (z + NZ - 1) % NZ
    z_far = (z + 2) % NZ

    def dev(yh_=yh, z_=z, x_=x, yl_=yl, core_=core):
        return {"dp": yh_ * NZ + z_, "ctx": x_ * 4 + yl_ * 2 + core_}

    up, down = dev(z_=z_up), dev(z_=z_down)
    cross = dev(yh_=1 - yh, yl_=1 - yl)
    sibling = dev(core_=1 - core)

    def remote(src, dst, send, recv, target):
        return pltpu.make_async_remote_copy(
            src_ref=src, dst_ref=dst, send_sem=send, recv_sem=recv, device_id=target, device_id_type=MESH)

    barrier = pltpu.get_barrier_semaphore()

    def greet_ctx(k, _):
        pl.semaphore_signal(barrier, inc=1, device_id={"dp": dp, "ctx": (ctx + k) % NCTX}, device_id_type=MESH)
        return 0

    def greet_plane(k, _):
        pl.semaphore_signal(
            barrier, inc=1, device_id=dev(yh_=(dp + k // 2) % NDP // NZ, z_=(dp + k // 2) % NDP % NZ, yl_=(yl + k) % 2),
            device_id_type=MESH)
        return 0

    lax.fori_loop(1, NCTX, greet_ctx, 0)
    lax.fori_loop(1, 2 * NDP, greet_plane, 0)
    own_w = pltpu.make_async_copy(w_ref, w_all.at[dp], local_sem.at[0])
    own_w.start()
    own_cot = pltpu.make_async_copy(cot_ref, cot_all.at[x], local_sem.at[1])
    own_cot.start()
    pl.semaphore_wait(barrier, NCTX - 1 + 2 * NDP - 1)

    def slot(yh_, z_, start=0, count=half, core_=core):
        return w_all.at[yh_ * NZ + z_, pl.ds(pl.multiple_of(core_ * half + start, quarter), count)]

    def send_w(i, src, dst, target):
        cp = remote(src, dst, w_send.at[i], w_recv.at[i], target)
        cp.start()
        return cp

    mine = w_ref.at[pl.ds(pl.multiple_of(core * half, half), half)]
    w_up = send_w(0, mine, slot(yh, z), up)
    w_down = send_w(1, mine, slot(yh, z), down)
    w_cross = send_w(2, mine, slot(yh, z), cross)
    sent = [w_up, w_down, w_cross]
    shared = {}

    def share(i, yh_, z_):
        cp = send_w(i, slot(yh_, z_), slot(yh_, z_), sibling)
        sent.append(cp)
        return cp

    def send_cot(k):
        return remote(cot_ref, cot_all.at[x], c_send.at[k - 1], c_recv.at[k - 1], dev(x_=(x + k) % NX))

    def send_normed(k):
        return remote(nb.at[(x + k) % NX], nrecv.at[x], n_send.at[k - 1], n_recv.at[k - 1], dev(x_=(x + k) % NX))

    for k in (1, 3, 2):
        send_cot(k).start()

    rate = jax.nn.softplus(dt_ref[...].astype(f32) + bias_ref[...])
    steps = rate * (-LOG2E * jnp.exp(al_ref[...]))
    row_pos = lax.broadcasted_iota(jnp.int32, (rows, rows), 0)
    col_pos = lax.broadcasted_iota(jnp.int32, (rows, rows), 1)
    causal = row_pos >= col_pos
    anticausal = col_pos >= row_pos
    log = mask_dot(causal.astype(bf16), steps)
    lt_ref[...] = log.T
    last = log[rows - 1 : rows, :]
    to_end = jnp.exp2(last - log)
    low = low_half(rows)
    low1 = low_half(1)
    for g in range(G):
        lg_ref[g] = log[:, g * HG : (g + 1) * HG]
        rg_ref[g] = rate[:, g * HG : (g + 1) * HG]
        bg_ref[g] = b_ref[:, g * N : (g + 1) * N]
        cg_ref[g] = c_ref[:, g * N : (g + 1) * N]
    for p in range(H // 2):
        lanes = slice(p * 128, (p + 1) * 128)
        xr = x_ref[:, lanes].astype(f32) * pair(rate, p, low)
        xr_ref[:, lanes] = xr.astype(bf16)
        xw_ref[:, lanes] = (xr * pair(to_end, p, low)).astype(bf16)
        hi, mid, lo = split3(pair(last, p, low1))
        tail = jnp.concatenate([hi, mid, lo, jnp.zeros((EXT - N - 3, 128), bf16)], axis=0)
        ext_ref[N:EXT, lanes] = tail
        gext_ref[N:EXT, lanes] = tail
    for g in range(G):
        lanes = slice(g * EG, (g + 1) * EG)
        state = dot_tn(bg_ref[g], xw_ref[:, lanes])
        ext_ref[0:N, lanes] = state.astype(bf16)

    def lanes_of(j):
        return pl.ds(pl.multiple_of(j * SHARE, SHARE), SHARE)

    def along(k):
        return (ctx + k) % NCTX

    def spread(ext, into, sends, recvs, k):
        return remote(ext.at[:, lanes_of(along(k))], into.at[ctx], sends.at[k - 1], recvs.at[k - 1],
                      {"dp": dp, "ctx": along(k)})

    def back(linked, into, sends, recvs, k):
        return remote(linked.at[along(k)], into.at[:, lanes_of(ctx)], sends.at[k - 1], recvs.at[k - 1],
                      {"dp": dp, "ctx": along(k)})

    def start_all(make):
        lax.fori_loop(1, NCTX, lambda k, _: (make(k).start(), 0)[1], 0)

    def wait_recv_all(make):
        lax.fori_loop(1, NCTX, lambda k, _: (make(k).wait_recv(), 0)[1], 0)

    def wait_send_all(make):
        lax.fori_loop(1, NCTX, lambda k, _: (make(k).wait_send(), 0)[1], 0)

    def link(reverse, gathered, linked, into):
        acc = jnp.zeros((N, SHARE), f32)
        for step in range(NCTX):
            j = NCTX - 1 - step if reverse else step
            linked[j] = acc.astype(bf16)
            part = gathered[j].astype(f32)
            total = part[N : N + 1] + part[N + 1 : N + 2] + part[N + 2 : N + 3]
            acc = jnp.exp2(total) * acc + part[0:N]
        into[:, lanes_of(ctx)] = linked[ctx]

    fwd_out = lambda k: spread(ext_ref, mine_ref, a_send, a_recv, k)
    fwd_back = lambda k: back(link_ref, sin_ref, o_send, o_recv, k)
    rev_out = lambda k: spread(gext_ref, gmine_ref, ga_send, ga_recv, k)
    rev_back = lambda k: back(link_ref, reach_ref, go_send, go_recv, k)
    start_all(fwd_out)
    mine_ref[ctx] = ext_ref[:, lanes_of(ctx)]

    def within(g, _):
        base = pl.multiple_of(g * EG, EG)
        log = lg_ref[g]
        log_t = lt_ref[pl.ds(pl.multiple_of(g * HG, HG), HG), :]
        cb = dot_nt(cg_ref[g], bg_ref[g])
        for p in range(HG // 2):
            lanes = pl.ds(pl.multiple_of(base + p * 128, 128), 128)
            parts = []
            for h in (2 * p, 2 * p + 1):
                gap = jnp.where(causal, log[:, h : h + 1] - log_t[h : h + 1, :], -1e30)
                parts.append((cb * jnp.exp2(gap)).astype(bf16))
            both = dot(jnp.concatenate(parts, axis=0), xr_ref[:, lanes])
            y_ref[:, lanes] = jnp.where(low, both[:rows], both[rows:])
        return 0

    lax.fori_loop(0, G, within, 0)
    wait_recv_all(fwd_out)
    link(False, mine_ref, link_ref, sin_ref)
    start_all(fwd_back)

    w_up.wait_recv()
    sent.append(send_w(3, slot(yh, z_down, 0, quarter), slot(yh, z_down, 0, quarter), up))
    w_down.wait_recv()
    sent.append(send_w(4, slot(yh, z_up, quarter, quarter), slot(yh, z_up, quarter, quarter), down))
    w_cross.wait_recv()
    sent.append(send_w(5, slot(1 - yh, z), slot(1 - yh, z), up))
    sent.append(send_w(6, slot(1 - yh, z), slot(1 - yh, z), down))
    w_far1, w_far2, w_cup, w_cdown = sent[3:7]
    shared[0] = share(8, yh, z_down)
    shared[1] = share(9, yh, z_up)
    shared[2] = share(10, 1 - yh, z)

    wait_recv_all(fwd_back)

    acc_ref[...] = jnp.zeros_like(acc_ref)

    def gate(g, _):
        base = pl.multiple_of(g * EG, EG)
        grown = jnp.exp2(lg_ref[g])
        c_blk = cg_ref[g]
        total = acc_ref[...]
        for p in range(HG // 2):
            lanes = pl.ds(pl.multiple_of(base + p * 128, 128), 128)
            y = y_ref[:, lanes] + pair(grown, p, low) * dot(c_blk, sin_ref[:, lanes])
            y_ref[:, lanes] = y
            out = y + pair(skip_ref[g], p, low1) * x_ref[:, lanes].astype(f32)
            zf = z_ref[:, lanes].astype(f32)
            gated = out * (zf * jax.nn.sigmoid(zf))
            wide_ref[:, lanes] = gated
            total = total + gated * gated
        acc_ref[...] = total
        return 0

    lax.fori_loop(0, G, gate, 0)
    r = lax.rsqrt(jnp.sum(acc_ref[...], axis=1, keepdims=True) * (1.0 / E) + EPSILON)

    def norm(i, _):
        for q in range(NX):
            lanes = pl.ds(pl.multiple_of(i * 512 + q * 128, 128), 128)
            nb[q, :, pl.ds(pl.multiple_of(i * 128, 128), 128)] = (
                wide_ref[:, lanes] * r * gain_ref[:, lanes]).astype(bf16)
        return 0

    lax.fori_loop(0, NDP, norm, 0)
    for k in (1, 3, 2):
        send_normed(k).start()
    nrecv[x] = nb[x]

    own_w.wait()
    own_cot.wait()
    lay_ref[...] = jnp.zeros_like(lay_ref)

    def project(yh_, z_):
        k = yh_ * NZ + z_
        dn_ref[:, pl.ds(pl.multiple_of(k * shard, shard), shard)] = dot_nt(cot_all[x], w_all[k]).astype(bf16)
        block = jnp.concatenate([nb[q, :, pl.ds(pl.multiple_of(k * 128, 128), 128)] for q in range(NX)], axis=1)

        def tile(n, _):
            cols = pl.ds(pl.multiple_of(n * (width // 4), width // 4), width // 4)
            lay_ref[:, cols] += dot(block, w_all[k, :, cols])
            return 0

        lax.fori_loop(0, 4, tile, 0)

    project(yh, z)
    shared[0].wait_recv()
    project(yh, z_down)
    shared[1].wait_recv()
    project(yh, z_up)
    shared[2].wait_recv()
    project(1 - yh, z)
    w_far1.wait_recv()
    w_far2.wait_recv()
    w_last = send_w(7, slot(yh, z_far), slot(yh, z_far), cross)
    sent.append(w_last)
    shared[3] = share(11, yh, z_far)
    w_cup.wait_recv()
    shared[4] = share(12, 1 - yh, z_down)
    w_cdown.wait_recv()
    shared[5] = share(13, 1 - yh, z_up)
    shared[3].wait_recv()
    project(yh, z_far)
    shared[4].wait_recv()
    project(1 - yh, z_down)
    shared[5].wait_recv()
    project(1 - yh, z_up)

    for k in (1, 3, 2):
        send_cot(k).wait_recv()
        send_normed(k).wait_recv()

    def block_of(k):
        return (dp + k) % NDP

    def send_half(k):
        i = block_of(k)
        return remote(other_ref.at[i], sib_ref.at[i], b_send.at[k], b_recv.at[k], sibling)

    def weigh(k, _):
        i = block_of(k)
        lanes = pl.ds(pl.multiple_of(i * 128, 128), 128)

        def product(side):
            cols = pl.ds(pl.multiple_of(side * half_width, half_width), half_width)
            total = dot_tn(nrecv[0, :, lanes], cot_all[0, :, cols])
            for s in range(1, NX):
                total = total + dot_tn(nrecv[s, :, lanes], cot_all[s, :, cols])
            return total.astype(bf16)

        other_ref[i] = product(1 - core)
        send_half(k).start()
        own_ref[i] = product(core)
        return 0

    lax.fori_loop(0, NDP, weigh, 0)

    def send_piece(k, j):
        i = block_of(k)
        other = (yl + j) % 2
        return remote(own_ref.at[i, pl.ds(pl.multiple_of(other * 64, 64), 64)], rs_ref.at[dp * 2 + yl],
                      r_send.at[2 * k + j], r_recv.at[2 * k + j], dev(yh_=i // NZ, z_=i % NZ, yl_=other))

    def combine(k, _):
        i = block_of(k)
        send_half(k).wait_recv()
        own_ref[i] = (own_ref[i].astype(f32) + sib_ref[i].astype(f32)).astype(bf16)
        return 0

    def send_both(k, _):
        combine(k, 0)
        send_piece(k, 0).start()
        send_piece(k, 1).start()
        return 0

    combine(0, 0)
    send_piece(0, 1).start()
    lax.fori_loop(1, NDP, send_both, 0)
    rs_ref[dp * 2 + yl] = own_ref[dp, pl.ds(pl.multiple_of(yl * 64, 64), 64)]

    w_last.wait_recv()
    shared[6] = share(14, 1 - yh, z_far)
    shared[6].wait_recv()
    project(1 - yh, z_far)
    out_ref[...] = lay_ref[...].astype(bf16)

    acc_ref[...] = jnp.zeros_like(acc_ref)

    def mean(g, _):
        base = pl.multiple_of(g * EG, EG)
        acc = acc_ref[...]
        for p in range(HG // 2):
            lanes = pl.ds(pl.multiple_of(base + p * 128, 128), 128)
            acc = acc + dn_ref[:, lanes].astype(f32) * gain_ref[:, lanes] * wide_ref[:, lanes]
        acc_ref[...] = acc
        return 0

    lax.fori_loop(0, G, mean, 0)
    inner = jnp.sum(acc_ref[...], axis=1, keepdims=True) * (1.0 / E)
    scaled = r * r * inner

    def gate_back(g, _):
        base = pl.multiple_of(g * EG, EG)
        grown = jnp.exp2(lg_ref[g])
        for p in range(HG // 2):
            lanes = pl.ds(pl.multiple_of(base + p * 128, 128), 128)
            zf = z_ref[:, lanes].astype(f32)
            sig = jax.nn.sigmoid(zf)
            silu = zf * sig
            out = y_ref[:, lanes] + pair(skip_ref[g], p, low1) * x_ref[:, lanes].astype(f32)
            dg = dn_ref[:, lanes].astype(f32) * gain_ref[:, lanes]
            d_gated = r * (dg - wide_ref[:, lanes] * scaled)
            dz_ref[:, lanes] = (d_gated * out * (sig * (1.0 + zf * (1.0 - sig)))).astype(bf16)
            dy = d_gated * silu
            dy_ref[:, lanes] = dy.astype(bf16)
            dyel_ref[:, lanes] = (dy * pair(grown, p, low)).astype(bf16)
        lanes = pl.ds(base, EG)
        gext_ref[0:N, lanes] = dot_tn(cg_ref[g], dyel_ref[:, lanes]).astype(bf16)
        return 0

    lax.fori_loop(0, G, gate_back, 0)
    start_all(rev_out)
    gmine_ref[ctx] = gext_ref[:, lanes_of(ctx)]

    def within_back(g, _):
        base = pl.multiple_of(g * EG, EG)
        log = lg_ref[g]
        log_t = lt_ref[pl.ds(pl.multiple_of(g * HG, HG), HG), :]
        cbt = dot_nt(bg_ref[g], cg_ref[g])
        for p in range(HG // 2):
            lanes = pl.ds(pl.multiple_of(base + p * 128, 128), 128)
            dy = dy_ref[:, lanes]
            xr = xr_ref[:, lanes]
            decays = []
            parts = []
            for h in (2 * p, 2 * p + 1):
                gap = jnp.where(anticausal, log_t[h : h + 1, :] - log[:, h : h + 1], -1e30)
                decay = jnp.exp2(gap)
                decays.append(decay)
                parts.append((cbt * decay).astype(bf16))
            both = dot(jnp.concatenate(parts, axis=0), dy)
            wide_ref[:, lanes] = jnp.where(low, both[:rows], both[rows:])
            zero = jnp.zeros_like(xr)
            halves = jnp.concatenate([jnp.where(low, xr, zero), jnp.where(low, zero, xr)], axis=0)
            dm = dot_nt(halves, dy)
            add = dm[:rows] * decays[0] + dm[rows:] * decays[1]
            if p == 0:
                dcb_ref[g] = add
            else:
                dcb_ref[g] += add
        return 0

    lax.fori_loop(0, G // 2, within_back, 0)
    wait_recv_all(rev_out)
    wait_send_all(fwd_back)
    link(True, gmine_ref, link_ref, reach_ref)
    start_all(rev_back)
    lax.fori_loop(G // 2, G, within_back, 0)

    for k in range(NDP):
        for j in range(2):
            if k + j > 0:
                send_piece(k, j).wait_recv()

    total = rs_ref[0].astype(f32)
    for q in range(1, 2 * NDP):
        total = total + rs_ref[q].astype(f32)
    piece_ref[...] = total.astype(bf16)

    def ring(k):
        return (x + k // 2) % NX, (yl + k) % 2

    def ring_from(k):
        return (x + NX - k // 2) % NX * 4 + (yl + k) % 2 * 2 + core

    def send_sum(k):
        x_, yl_ = ring(k)
        return remote(piece_ref, gw_ref.at[ctx], p_send.at[k], p_recv.at[k], dev(x_=x_, yl_=yl_))

    def hand_on(k):
        src = gw_ref.at[ring_from(k)]
        return remote(src, src, f_send.at[k], f_recv.at[k], sibling)

    for k in range(1, 2 * NX):
        send_sum(k).start()
    to_sibling = remote(piece_ref, gw_ref.at[ctx], p_send.at[0], p_recv.at[0], sibling)
    to_sibling.start()
    own_piece = pltpu.make_async_copy(piece_ref, gw_ref.at[ctx], local_sem.at[2])
    own_piece.start()

    wait_recv_all(rev_back)

    e_pos = lax.broadcasted_iota(jnp.int32, (EG, HG), 0)
    h_pos = lax.broadcasted_iota(jnp.int32, (EG, HG), 1)
    heads = ((e_pos // P_SIZE) == h_pos).astype(bf16)

    def finish(g, _):
        base = pl.multiple_of(g * EG, EG)
        wide = pl.ds(base, EG)
        log = lg_ref[g]
        rate = rg_ref[g]
        b_blk = bg_ref[g]
        c_blk = cg_ref[g]
        last = log[rows - 1 : rows, :]
        to_end = jnp.exp2(last - log)
        for p in range(HG // 2):
            here = slice(p * 128, (p + 1) * 128)
            lanes = pl.ds(pl.multiple_of(base + p * 128, 128), 128)
            dyf = dy_ref[:, lanes].astype(f32)
            dxr = wide_ref[:, lanes] + pair(to_end, p, low) * dot(b_blk, reach_ref[:, lanes])
            dy_ref[:, lanes] = (dxr * pair(rate, p, low) + pair(skip_ref[g], p, low1) * dyf).astype(bf16)
            q1 = dyf * y_ref[:, lanes] - xr_ref[:, lanes].astype(f32) * dxr
            hi = q1.astype(bf16)
            dn_ref[:, here] = hi
            dn_ref[:, slice(EG + p * 128, EG + (p + 1) * 128)] = (q1 - hi.astype(f32)).astype(bf16)
            dn_ref[:, slice(2 * EG + p * 128, 2 * EG + (p + 1) * 128)] = (x_ref[:, lanes].astype(f32) * dxr).astype(bf16)
        reach = reach_ref[:, wide]
        dcb = dcb_ref[g].astype(bf16)
        dbg_ref[g] = (dot(dcb, c_blk) + dot_nt(xw_ref[:, wide], reach)).astype(bf16)
        dcg_ref[g] = (dot_tn(dcb, b_blk) + dot_nt(dyel_ref[:, wide], sin_ref[:, wide])).astype(bf16)
        sums = []
        for v in (sin_ref[:, wide].astype(f32), ext_ref[0:N, wide].astype(f32)):
            v = jnp.sum(v * reach.astype(f32), axis=0, keepdims=True)
            a, b, _ = split3(jnp.broadcast_to(v, (16, EG)))
            sums.append((dot(a, heads) + dot(b, heads))[0:1])
        at_end = jnp.exp2(last) * sums[0] + sums[1]
        q1 = dot(dn_ref[:, 0:EG], heads) + dot(dn_ref[:, EG : 2 * EG], heads)
        qs_ref[g] = mask_dot(anticausal.astype(bf16), q1) + at_end
        qs_ref[G + g] = dot(dn_ref[:, 2 * EG : 3 * EG], heads)
        return 0

    lax.fori_loop(0, G, finish, 0)
    dx_out = pltpu.make_async_copy(dy_ref, dx_ref, local_sem.at[3])
    dx_out.start()
    a_neg = -jnp.exp(al_ref[...])
    slope = jax.nn.sigmoid(dt_ref[...].astype(f32) + bias_ref[...])
    for g in range(G):
        here = slice(g * HG, (g + 1) * HG)
        d_rate = a_neg[:, here] * qs_ref[g] + qs_ref[G + g]
        ddt_ref[:, here] = (d_rate * slope[:, here]).astype(bf16)
        db_ref[:, g * N : (g + 1) * N] = dbg_ref[g]
        dc_ref[:, g * N : (g + 1) * N] = dcg_ref[g]

    for k in range(1, 2 * NX):
        send_sum(k).wait_recv()
        hand_on(k).start()

    dx_out.wait()
    own_piece.wait()
    to_sibling.wait()
    for k in range(1, 2 * NX):
        send_sum(k).wait_send()
        hand_on(k).wait()
    for cp in sent:
        cp.wait_send()
    for k in (1, 3, 2):
        send_cot(k).wait_send()
        send_normed(k).wait_send()
    for make in (fwd_out, rev_out, rev_back):
        wait_send_all(make)
    for k in range(NDP):
        send_half(k).wait_send()
        for j in range(2):
            if k + j > 0:
                send_piece(k, j).wait_send()


def shards(xs, z_gate, b_proj, c_proj, dt_raw, a_log, dt_bias, d_skip, norm_gain, w_out, cotangent):
    rows = xs.shape[1]
    width = cotangent.shape[2]
    shard = w_out.shape[0]
    wide = ((rows, E), bf16)
    outs = [((rows, width), bf16), wide, wide, ((rows, G * N), bf16), ((rows, G * N), bf16), ((rows, H), bf16),
            ((NCTX, shard // 8, width // 2), bf16)]
    state = ((N, E), bf16)
    ext = ((EXT, E), bf16)
    share = ((NCTX, EXT, SHARE), bf16)
    linked = ((NCTX, N, SHARE), bf16)
    per_group = ((G, rows, HG), f32)
    group_cols = ((G, rows, N), bf16)
    quad = ((NX, rows, E // NX), bf16)
    block = ((NDP, 128, width // 2), bf16)
    scratch = [
        ((NDP, shard, width), bf16), ((NX, rows, width), bf16), quad, quad, wide, wide, ((rows, E), f32),
        ((rows, E), f32), wide, wide, wide,
        ((rows, width), f32), ((G, rows, rows), f32),
        ((2 * G, rows, HG), f32), group_cols, group_cols,
        per_group, per_group, ((H, rows), f32), group_cols, group_cols, ((rows, 128), f32),
        ext, share, linked, state, ext, share, state,
        block, block, block, ((2 * NDP, 64, width // 2), bf16), ((64, width // 2), bf16),
    ]
    sems = [4, 15, 15, 3, 3, 3, 3] + [NCTX - 1] * 8 + [NDP, NDP, 2 * NDP, 2 * NDP] + [2 * NX] * 4
    vmem = pl.BlockSpec(memory_space=pltpu.VMEM)
    hbm = pl.BlockSpec(memory_space=pl.ANY)
    layer_out, dx, dz, db, dc, ddt, gw = pl.pallas_call(
        layer_kernel,
        out_shape=[jax.ShapeDtypeStruct(s, d) for s, d in outs],
        in_specs=[vmem] * 9 + [hbm, hbm],
        out_specs=[vmem, hbm] + [vmem] * 4 + [hbm],
        scratch_shapes=[pltpu.VMEM(s, d) for s, d in scratch] + [pltpu.SemaphoreType.DMA((n,)) for n in sems],
        compiler_params=pltpu.CompilerParams(
            collective_id=0, has_side_effects=True, vmem_limit_bytes=VMEM_LIMIT),
    )(xs[0], z_gate[0], b_proj[0], c_proj[0], dt_raw[0], a_log[None], dt_bias[None],
      d_skip.reshape(G, 1, HG), norm_gain[None], w_out, cotangent[0])
    gw = gw.reshape(NX, 2, 2, 64, width // 2).transpose(0, 1, 3, 2, 4).reshape(shard, width).astype(f32)
    return layer_out[None], dx[None], dz[None], db[None], dc[None], ddt[None], gw


def solution(mesh):
    rows = P("dp", "ctx", None)
    in_specs = (rows,) * 5 + (P(),) * 4 + (P("dp", None), rows)
    out_specs = (rows,) * 6 + (P("dp", None),)
    return jax.shard_map(shards, mesh=mesh, in_specs=in_specs, out_specs=out_specs, check_vma=False)
```

```python
import math

import jax
import jax.numpy as jnp
from jax import lax
from jax.experimental import pallas as pl
from jax.experimental.pallas import tpu as pltpu
from jax.sharding import PartitionSpec as P

H = 64
P_SIZE = 64
N = 64
G = 4
E = 4096
HG = H // G
EG = E // G
EPSILON = 1e-05
LOG2E = math.log2(math.e)
EXT = 80
bf16 = jnp.bfloat16
f32 = jnp.float32
VMEM_LIMIT = 63 * 1024 * 1024
MESH = pl.DeviceIdType.MESH


def dot(a, b):
    return lax.dot_general(a, b, (((1,), (0,)), ((), ())), preferred_element_type=f32)


def dot_nt(a, b):
    return lax.dot_general(a, b, (((1,), (1,)), ((), ())), preferred_element_type=f32)


def dot_tn(a, b):
    return lax.dot_general(a, b, (((0,), (0,)), ((), ())), preferred_element_type=f32)


def split3(v):
    a = v.astype(bf16)
    rest = v - a.astype(f32)
    b = rest.astype(bf16)
    c = (rest - b.astype(f32)).astype(bf16)
    return a, b, c


def mask_dot(mask, v):
    a, b, c = split3(v)
    return dot(mask, a) + dot(mask, b) + dot(mask, c)


def low_half(rows):
    return lax.broadcasted_iota(jnp.int32, (rows, 128), 1) < P_SIZE


def pair(values, p, low):
    return jnp.where(low, values[:, 2 * p : 2 * p + 1], values[:, 2 * p + 1 : 2 * p + 2])


NZ = 4
NX = 4
NDP = 2 * NZ
NCTX = 4 * NX
SHARE = E // NCTX


def layer_kernel(x_in, z_in, b_ref, c_ref, dt_ref, al_ref, bias_ref, skips_ref, gain_ref, w_ref, cot_ref,
                 layer_ref, dx_ref, dz_out, db_ref, dc_ref, ddt_ref, gw_ref,
                 x_ref, z_ref, out_ref, dz_ref, w_all, cot_all, nb, nrecv, xr_ref, xw_ref, y_ref, wide_ref, dn_ref, dy_ref, dyel_ref,
                 lay_ref, dcb_ref, qs_ref, dbg_ref, dcg_ref,
                 lg_ref, rg_ref, lt_ref, bg_ref, cg_ref, acc_ref, skip_ref,
                 ext_ref, mine_ref, link_ref, sin_ref, gext_ref, gmine_ref, reach_ref,
                 own_ref, other_ref, sib_ref, ra1_ref, rb1_ref, ra2_ref, rb2_ref, piece_ref,
                 local_sem, w_send, w_recv, c_send, c_recv, n_send, n_recv,
                 a_send, a_recv, o_send, o_recv, ga_send, ga_recv, go_send, go_recv,
                 b_send, b_recv, r_send, r_recv, p_send, p_recv, f_send, f_recv):
    rows = x_ref.shape[0]
    width = cot_ref.shape[1]
    half_width = width // 2
    shard = w_ref.shape[0]
    half = shard // 2
    quarter = shard // 4
    dp = lax.axis_index("dp")
    ctx = lax.axis_index("ctx")
    yh, z = dp // NZ, dp % NZ
    x, yl, core = ctx // 4, (ctx // 2) % 2, ctx % 2
    z_up, z_down = (z + 1) % NZ, (z + NZ - 1) % NZ
    z_far = (z + 2) % NZ

    def dev(yh_=yh, z_=z, x_=x, yl_=yl, core_=core):
        return {"dp": yh_ * NZ + z_, "ctx": x_ * 4 + yl_ * 2 + core_}

    up, down = dev(z_=z_up), dev(z_=z_down)
    cross = dev(yh_=1 - yh, yl_=1 - yl)
    sibling = dev(core_=1 - core)

    def remote(src, dst, send, recv, target):
        return pltpu.make_async_remote_copy(
            src_ref=src, dst_ref=dst, send_sem=send, recv_sem=recv, device_id=target, device_id_type=MESH)

    x_copy = pltpu.make_async_copy(x_in, x_ref, local_sem.at[4])
    x_copy.start()
    z_copy = pltpu.make_async_copy(z_in, z_ref, local_sem.at[5])
    z_copy.start()

    barrier = pltpu.get_barrier_semaphore()

    def greet_ctx(k, _):
        pl.semaphore_signal(barrier, inc=1, device_id={"dp": dp, "ctx": (ctx + k) % NCTX}, device_id_type=MESH)
        return 0

    for other in [dev(z_=(z + k) % NZ) for k in (1, 2, 3)] + [dev(yh_=1 - yh, yl_=k) for k in (0, 1)]:
        pl.semaphore_signal(barrier, inc=1, device_id=other, device_id_type=MESH)
    lax.fori_loop(1, NCTX, greet_ctx, 0)
    rate = jax.nn.softplus(dt_ref[...].astype(f32).T + bias_ref[...])
    steps = rate * (-LOG2E * jnp.exp(al_ref[...]))
    row_pos = lax.broadcasted_iota(jnp.int32, (rows, rows), 0)
    col_pos = lax.broadcasted_iota(jnp.int32, (rows, rows), 1)
    causal = row_pos >= col_pos
    anticausal = col_pos >= row_pos
    log = mask_dot(causal.astype(bf16), steps)
    lt_ref[...] = log.T
    last = log[rows - 1 : rows, :]
    to_end = jnp.exp2(last - log)
    low = low_half(rows)
    low1 = low_half(1)
    for g in range(G):
        lg_ref[g] = log[:, g * HG : (g + 1) * HG]
        rg_ref[g] = rate[:, g * HG : (g + 1) * HG]
        skip_ref[g] = skips_ref[:, g * HG : (g + 1) * HG]
        bg_ref[g] = b_ref[:, g * N : (g + 1) * N]
        cg_ref[g] = c_ref[:, g * N : (g + 1) * N]
    x_copy.wait()
    for p in range(H // 2):
        lanes = slice(p * 128, (p + 1) * 128)
        xr = x_ref[:, lanes].astype(f32) * pair(rate, p, low)
        xr_ref[:, lanes] = xr.astype(bf16)
        xw_ref[:, lanes] = (xr * pair(to_end, p, low)).astype(bf16)
        hi, mid, lo = split3(pair(last, p, low1))
        tail = jnp.concatenate([hi, mid, lo, jnp.zeros((EXT - N - 3, 128), bf16)], axis=0)
        ext_ref[N:EXT, lanes] = tail
        gext_ref[N:EXT, lanes] = tail
    for g in range(G):
        lanes = slice(g * EG, (g + 1) * EG)
        state = dot_tn(bg_ref[g], xw_ref[:, lanes])
        ext_ref[0:N, lanes] = state.astype(bf16)

    own_w = pltpu.make_async_copy(w_ref, w_all.at[dp], local_sem.at[0])
    own_w.start()
    own_cot = pltpu.make_async_copy(cot_ref, cot_all.at[x], local_sem.at[1])
    own_cot.start()
    pl.semaphore_wait(barrier, NCTX - 1 + 5)

    up_y = dev(yl_=1 - yl)
    mine, theirs = yl, 1 - yl

    def unit(yh_, z_, q, part=None):
        start = core * half + q * quarter + (0 if part is None else part * (quarter // 2))
        count = quarter if part is None else quarter // 2
        return w_all.at[yh_ * NZ + z_, pl.ds(pl.multiple_of(start, quarter // 2), count)]

    waits = {}
    sent = []

    def send_w(name, src, target, dst=None):
        i = len(waits)
        cp = remote(src, src if dst is None else dst, w_send.at[i], w_recv.at[i], target)
        cp.start()
        waits[name] = cp
        sent.append(cp)

    def arrived(*names):
        for name in names:
            waits[name].wait_recv()

    def own_unit(q):
        return w_ref.at[pl.ds(pl.multiple_of(core * half + q * quarter, quarter), quarter)]

    def share(name, yh_, z_, q):
        send_w(name, unit(yh_, z_, q), sibling)

    def send_cot(k, part):
        here = pl.ds(part * (rows // 2), rows // 2)
        i = k - 1 + part
        return remote(cot_ref.at[here], cot_all.at[x, here], c_send.at[i], c_recv.at[i], dev(x_=(x + k) % NX))

    def hand_cot(part, side):
        k = 1 + 2 * side
        here = pl.ds(part * (rows // 2) + side * (rows // 4), rows // 4)
        there = cot_all.at[(x + NX - k) % NX, here]
        i = 4 + 2 * part + side
        return remote(there, there, c_send.at[i], c_recv.at[i], dev(x_=(x + k) % NX))

    def pass_cot(part):
        for k in (1, 3):
            send_cot(k, part).wait_recv()
        for side in range(2):
            hand_cot(part, side).start()

    def send_normed(k):
        return remote(nb.at[(x + k) % NX], nrecv.at[x], n_send.at[k - 1], n_recv.at[k - 1], dev(x_=(x + k) % NX))

    def lanes_of(j):
        return pl.ds(pl.multiple_of(j * SHARE, SHARE), SHARE)

    def along(k):
        return (ctx + k) % NCTX

    def spread(ext, into, sends, recvs, k):
        return remote(ext.at[:, lanes_of(along(k))], into.at[ctx], sends.at[k - 1], recvs.at[k - 1],
                      {"dp": dp, "ctx": along(k)})

    def back(linked, into, sends, recvs, k):
        return remote(linked.at[along(k)], into.at[:, lanes_of(ctx)], sends.at[k - 1], recvs.at[k - 1],
                      {"dp": dp, "ctx": along(k)})

    def start_all(make):
        lax.fori_loop(1, NCTX, lambda k, _: (make(k).start(), 0)[1], 0)

    def wait_recv_all(make):
        lax.fori_loop(1, NCTX, lambda k, _: (make(k).wait_recv(), 0)[1], 0)

    def wait_send_all(make):
        lax.fori_loop(1, NCTX, lambda k, _: (make(k).wait_send(), 0)[1], 0)

    def link(reverse, gathered, linked, into):
        acc = jnp.zeros((N, SHARE), f32)
        for step in range(NCTX):
            j = NCTX - 1 - step if reverse else step
            linked[j] = acc.astype(bf16)
            part = gathered[j].astype(f32)
            total = part[N : N + 1] + part[N + 1 : N + 2] + part[N + 2 : N + 3]
            acc = jnp.exp2(total) * acc + part[0:N]
        into[:, lanes_of(ctx)] = linked[ctx]

    fwd_out = lambda k: spread(ext_ref, mine_ref, a_send, a_recv, k)
    fwd_back = lambda k: back(link_ref, sin_ref, o_send, o_recv, k)
    rev_out = lambda k: spread(gext_ref, gmine_ref, ga_send, ga_recv, k)
    rev_back = lambda k: back(link_ref, reach_ref, go_send, go_recv, k)
    start_all(fwd_out)
    send_w("a1", own_unit(mine), up, unit(yh, z, mine))
    send_w("a2", own_unit(mine), down, unit(yh, z, mine))
    send_w("b1", own_unit(theirs), cross, unit(yh, z, theirs))
    send_w("b2", own_unit(mine), cross, unit(yh, z, mine))
    for k in (1, 3):
        send_cot(k, 0).start()
    mine_ref[ctx] = ext_ref[:, lanes_of(ctx)]

    def within(g, _):
        base = pl.multiple_of(g * EG, EG)
        log = lg_ref[g]
        log_t = lt_ref[pl.ds(pl.multiple_of(g * HG, HG), HG), :]
        cb = dot_nt(cg_ref[g], bg_ref[g])
        for p in range(HG // 2):
            lanes = pl.ds(pl.multiple_of(base + p * 128, 128), 128)
            parts = []
            for h in (2 * p, 2 * p + 1):
                gap = jnp.where(causal, log[:, h : h + 1] - log_t[h : h + 1, :], -1e30)
                parts.append((cb * jnp.exp2(gap)).astype(bf16))
            both = dot(jnp.concatenate(parts, axis=0), xr_ref[:, lanes])
            y_ref[:, lanes] = jnp.where(low, both[:rows], both[rows:])
        return 0

    lax.fori_loop(0, G, within, 0)
    wait_recv_all(fwd_out)
    link(False, mine_ref, link_ref, sin_ref)
    start_all(fwd_back)

    arrived("a1", "a2")
    for name, z_ in (("n1", z_down), ("n2", z_up)):
        send_w(name, unit(yh, z_, mine), up_y)
    send_w("f1", unit(yh, z_down, mine, 0), up)
    send_w("f2", unit(yh, z_up, mine, 1), down)
    arrived("b1")
    send_w("c1", unit(1 - yh, z, mine), up)
    send_w("c2", unit(1 - yh, z, mine), down)
    for name, z_ in (("m1", z_down), ("m2", z_up)):
        send_w(name, unit(yh, z_, mine), cross)
    share("s1", yh, z_down, mine)
    share("s2", yh, z_up, mine)
    share("s3", 1 - yh, z, mine)
    pass_cot(0)
    for k in (1, 3):
        send_cot(k, 1).start()

    wait_recv_all(fwd_back)

    z_copy.wait()
    acc_ref[...] = jnp.zeros_like(acc_ref)

    def gate(g, _):
        base = pl.multiple_of(g * EG, EG)
        grown = jnp.exp2(lg_ref[g])
        c_blk = cg_ref[g]
        total = acc_ref[...]
        for p in range(HG // 2):
            lanes = pl.ds(pl.multiple_of(base + p * 128, 128), 128)
            y = y_ref[:, lanes] + pair(grown, p, low) * dot(c_blk, sin_ref[:, lanes])
            y_ref[:, lanes] = y
            out = y + pair(skip_ref[g], p, low1) * x_ref[:, lanes].astype(f32)
            zf = z_ref[:, lanes].astype(f32)
            gated = out * (zf * jax.nn.sigmoid(zf))
            wide_ref[:, lanes] = gated
            total = total + gated * gated
        acc_ref[...] = total
        return 0

    lax.fori_loop(0, G, gate, 0)
    r = lax.rsqrt(jnp.sum(acc_ref[...], axis=1, keepdims=True) * (1.0 / E) + EPSILON)

    def norm(i, _):
        for q in range(NX):
            lanes = pl.ds(pl.multiple_of(i * 512 + q * 128, 128), 128)
            nb[q, :, pl.ds(pl.multiple_of(i * 128, 128), 128)] = (
                wide_ref[:, lanes] * r * gain_ref[:, lanes]).astype(bf16)
        return 0

    lax.fori_loop(0, NDP, norm, 0)
    for k in (1, 3, 2):
        send_normed(k).start()
    nrecv[x] = nb[x]

    own_w.wait()
    own_cot.wait()
    lay_ref[...] = jnp.zeros_like(lay_ref)

    def project(yh_, z_):
        k = yh_ * NZ + z_
        dn_ref[:, pl.ds(pl.multiple_of(k * shard, shard), shard)] = dot_nt(cot_all[x], w_all[k]).astype(bf16)
        block = jnp.concatenate([nb[q, :, pl.ds(pl.multiple_of(k * 128, 128), 128)] for q in range(NX)], axis=1)

        def tile(n, _):
            cols = pl.ds(pl.multiple_of(n * (width // 4), width // 4), width // 4)
            lay_ref[:, cols] += dot(block, w_all[k, :, cols])
            return 0

        lax.fori_loop(0, 4, tile, 0)

    project(yh, z)
    pass_cot(1)

    arrived("f1", "f2")
    share("s4", yh, z_far, mine)
    arrived("b2")
    share("s5", 1 - yh, z, theirs)
    arrived("c1", "c2")
    send_w("g1", unit(1 - yh, z_down, mine, 0), up)
    send_w("g2", unit(1 - yh, z_up, mine, 1), down)
    share("s6", 1 - yh, z_down, mine)
    share("s7", 1 - yh, z_up, mine)
    arrived("n1", "n2")
    send_w("f3", unit(yh, z_down, theirs, 0), up)
    send_w("f4", unit(yh, z_up, theirs, 1), down)
    share("s8", yh, z_down, theirs)
    share("s9", yh, z_up, theirs)
    arrived("g1", "g2")
    send_w("n4", unit(1 - yh, z_far, mine), up_y)
    share("s10", 1 - yh, z_far, mine)
    arrived("s3", "s5")
    project(1 - yh, z)
    arrived("s1", "s8")
    project(yh, z_down)
    arrived("s2", "s9")
    project(yh, z_up)

    arrived("m1", "m2")
    share("s11", 1 - yh, z_down, theirs)
    share("s12", 1 - yh, z_up, theirs)
    arrived("f3", "f4")
    share("s13", yh, z_far, theirs)
    arrived("s6", "s11")
    project(1 - yh, z_down)
    arrived("s7", "s12")
    project(1 - yh, z_up)
    arrived("s4", "s13")
    project(yh, z_far)
    arrived("n4")
    share("s14", 1 - yh, z_far, theirs)

    for part in range(2):
        for side in range(2):
            hand_cot(part, side).wait_recv()
    for k in (1, 3, 2):
        send_normed(k).wait_recv()

    def block_of(k):
        return (dp + k) % NDP

    def send_half(k):
        i = block_of(k)
        return remote(other_ref.at[i], sib_ref.at[i], b_send.at[k], b_recv.at[k], sibling)

    def weigh(k, _):
        i = block_of(k)
        lanes = pl.ds(pl.multiple_of(i * 128, 128), 128)

        def product(side):
            cols = pl.ds(pl.multiple_of(side * half_width, half_width), half_width)
            total = dot_tn(nrecv[0, :, lanes], cot_all[0, :, cols])
            for s in range(1, NX):
                total = total + dot_tn(nrecv[s, :, lanes], cot_all[s, :, cols])
            return total.astype(bf16)

        other_ref[i] = product(1 - core)
        send_half(k).start()
        own_ref[i // NZ, i % NZ] = product(core)
        return 0

    lax.fori_loop(0, NDP, weigh, 0)

    def combine(k, _):
        i = block_of(k)
        send_half(k).wait_recv()
        own_ref[i // NZ, i % NZ] = (own_ref[i // NZ, i % NZ].astype(f32) + sib_ref[i].astype(f32)).astype(bf16)
        return 0

    lax.fori_loop(0, NDP, combine, 0)

    first, second = pl.ds(0, half_width // 2), pl.ds(half_width // 2, half_width // 2)
    y = 2 * yh + yl

    def rows_of(yl_):
        return pl.ds(pl.multiple_of(yl_ * 64, 64), 64)

    def reduce_copy(i, src, dst, target):
        return remote(src, dst, r_send.at[i], r_recv.at[i], target)

    def along_y(k):
        there = (y + k) % 4
        return there // 2, there % 2

    def first_step():
        copies = []
        for k in (1, 3, 2):
            yh_, yl_ = along_y(k)
            copies.append(reduce_copy(k - 1, own_ref.at[yh_, :, rows_of(yl_), first], ra1_ref.at[y],
                                      dev(yh_=yh_, yl_=yl_)))
            z_ = (z + k) % NZ
            copies.append(reduce_copy(k + 2, own_ref.at[:, z_, :, second], rb1_ref.at[z], dev(z_=z_)))
        return copies

    def second_step():
        copies = []
        for k in (1, 3, 2):
            yh_, yl_ = along_y(k)
            z_ = (z + k) % NZ
            copies.append(reduce_copy(k + 5, ra1_ref.at[y, z_], ra2_ref.at[z], dev(z_=z_)))
            copies.append(reduce_copy(k + 8, rb1_ref.at[z, yh_, rows_of(yl_)], rb2_ref.at[y],
                                      dev(yh_=yh_, yl_=yl_)))
        return copies

    def total_of(ref):
        total = ref[0].astype(f32)
        for q in range(1, 4):
            total = total + ref[q].astype(f32)
        return total.astype(bf16)

    step1 = first_step()
    for cp in step1:
        cp.start()
    ra1_ref[y] = own_ref[yh, :, rows_of(yl), first]
    rb1_ref[z] = own_ref[:, z, :, second]

    arrived("s10", "s14")
    project(1 - yh, z_far)
    out_ref[...] = lay_ref[...].astype(bf16)
    layer_copy = pltpu.make_async_copy(out_ref, layer_ref, local_sem.at[6])
    layer_copy.start()

    acc_ref[...] = jnp.zeros_like(acc_ref)

    def mean(g, _):
        base = pl.multiple_of(g * EG, EG)
        acc = acc_ref[...]
        for p in range(HG // 2):
            lanes = pl.ds(pl.multiple_of(base + p * 128, 128), 128)
            acc = acc + dn_ref[:, lanes].astype(f32) * gain_ref[:, lanes] * wide_ref[:, lanes]
        acc_ref[...] = acc
        return 0

    lax.fori_loop(0, G, mean, 0)
    inner = jnp.sum(acc_ref[...], axis=1, keepdims=True) * (1.0 / E)
    scaled = r * r * inner

    def gate_back(g, _):
        base = pl.multiple_of(g * EG, EG)
        grown = jnp.exp2(lg_ref[g])
        for p in range(HG // 2):
            lanes = pl.ds(pl.multiple_of(base + p * 128, 128), 128)
            zf = z_ref[:, lanes].astype(f32)
            sig = jax.nn.sigmoid(zf)
            silu = zf * sig
            out = y_ref[:, lanes] + pair(skip_ref[g], p, low1) * x_ref[:, lanes].astype(f32)
            dg = dn_ref[:, lanes].astype(f32) * gain_ref[:, lanes]
            d_gated = r * (dg - wide_ref[:, lanes] * scaled)
            dz_ref[:, lanes] = (d_gated * out * (sig * (1.0 + zf * (1.0 - sig)))).astype(bf16)
            dy = d_gated * silu
            dy_ref[:, lanes] = dy.astype(bf16)
            dyel_ref[:, lanes] = (dy * pair(grown, p, low)).astype(bf16)
        lanes = pl.ds(base, EG)
        gext_ref[0:N, lanes] = dot_tn(cg_ref[g], dyel_ref[:, lanes]).astype(bf16)
        return 0

    lax.fori_loop(0, G, gate_back, 0)
    dz_copy = pltpu.make_async_copy(dz_ref, dz_out, local_sem.at[7])
    dz_copy.start()
    start_all(rev_out)
    gmine_ref[ctx] = gext_ref[:, lanes_of(ctx)]

    e_pos = lax.broadcasted_iota(jnp.int32, (EG, HG), 0)
    h_pos = lax.broadcasted_iota(jnp.int32, (EG, HG), 1)
    heads = ((e_pos // P_SIZE) == h_pos).astype(bf16)

    def within_back(g, _):
        base = pl.multiple_of(g * EG, EG)
        log = lg_ref[g]
        log_t = lt_ref[pl.ds(pl.multiple_of(g * HG, HG), HG), :]
        cbt = dot_nt(bg_ref[g], cg_ref[g])
        for p in range(HG // 2):
            lanes = pl.ds(pl.multiple_of(base + p * 128, 128), 128)
            dy = dy_ref[:, lanes]
            xr = xr_ref[:, lanes]
            decays = []
            parts = []
            for h in (2 * p, 2 * p + 1):
                gap = jnp.where(anticausal, log_t[h : h + 1, :] - log[:, h : h + 1], -1e30)
                decay = jnp.exp2(gap)
                decays.append(decay)
                parts.append((cbt * decay).astype(bf16))
            both = dot(jnp.concatenate(parts, axis=0), dy)
            dxr = jnp.where(low, both[:rows], both[rows:])
            wide_ref[:, lanes] = dxr
            q1 = dy.astype(f32) * y_ref[:, lanes] - xr.astype(f32) * dxr
            hi = q1.astype(bf16)
            dn_ref[:, slice(p * 128, (p + 1) * 128)] = hi
            dn_ref[:, slice(EG + p * 128, EG + (p + 1) * 128)] = (q1 - hi.astype(f32)).astype(bf16)
            dn_ref[:, slice(2 * EG + p * 128, 2 * EG + (p + 1) * 128)] = (
                x_ref[:, lanes].astype(f32) * dxr).astype(bf16)
            zero = jnp.zeros_like(xr)
            halves = jnp.concatenate([jnp.where(low, xr, zero), jnp.where(low, zero, xr)], axis=0)
            dm = dot_nt(halves, dy)
            add = dm[:rows] * decays[0] + dm[rows:] * decays[1]
            if p == 0:
                dcb_ref[...] = add
            else:
                dcb_ref[...] += add
        wide = pl.ds(base, EG)
        dcb = dcb_ref[...].astype(bf16)
        dbg_ref[g] = dot(dcb, cg_ref[g])
        qs_ref[g] = dot(dn_ref[:, 0:EG], heads) + dot(dn_ref[:, EG : 2 * EG], heads)
        qs_ref[G + g] = dot(dn_ref[:, 2 * EG : 3 * EG], heads)
        dcg_ref[g] = (dot_tn(dcb, bg_ref[g]) + dot_nt(dyel_ref[:, wide], sin_ref[:, wide])).astype(bf16)
        return 0

    lax.fori_loop(0, G // 2, within_back, 0)
    for cp in step1:
        cp.wait_recv()
    ra1_ref[y] = total_of(ra1_ref)
    rb1_ref[z] = total_of(rb1_ref)
    step2 = second_step()
    for cp in step2:
        cp.start()
    ra2_ref[z] = ra1_ref[y, z]
    rb2_ref[y] = rb1_ref[z, yh, rows_of(yl)]
    wait_recv_all(rev_out)
    wait_send_all(fwd_back)
    link(True, gmine_ref, link_ref, reach_ref)
    start_all(rev_back)
    lax.fori_loop(G // 2, G, within_back, 0)

    for cp in step2:
        cp.wait_recv()
    piece_ref[:, first] = total_of(ra2_ref)
    piece_ref[:, second] = total_of(rb2_ref)

    def ring(k):
        return (x + k // 2) % NX, (yl + k) % 2

    def place(x_, yl_):
        rows_here = pl.ds(pl.multiple_of(x_ * 128 + yl_ * 64, 64), 64)
        return gw_ref.at[rows_here, pl.ds(pl.multiple_of(core * half_width, half_width), half_width)]

    def send_sum(k):
        x_, yl_ = ring(k)
        return remote(piece_ref, place(x, yl), p_send.at[k], p_recv.at[k], dev(x_=x_, yl_=yl_))

    def hand_on(k):
        src = place((x + NX - k // 2) % NX, (yl + k) % 2)
        return remote(src, src, f_send.at[k], f_recv.at[k], sibling)

    for k in range(1, 2 * NX):
        send_sum(k).start()
    to_sibling = remote(piece_ref, place(x, yl), p_send.at[0], p_recv.at[0], sibling)
    to_sibling.start()
    own_piece = pltpu.make_async_copy(piece_ref, place(x, yl), local_sem.at[2])
    own_piece.start()
    wait_recv_all(rev_back)

    def finish(g, _):
        base = pl.multiple_of(g * EG, EG)
        wide = pl.ds(base, EG)
        log = lg_ref[g]
        rate = rg_ref[g]
        b_blk = bg_ref[g]
        last = log[rows - 1 : rows, :]
        to_end = jnp.exp2(last - log)
        for p in range(HG // 2):
            here = slice(p * 128, (p + 1) * 128)
            lanes = pl.ds(pl.multiple_of(base + p * 128, 128), 128)
            dyf = dy_ref[:, lanes].astype(f32)
            late = pair(to_end, p, low) * dot(b_blk, reach_ref[:, lanes])
            dxr = wide_ref[:, lanes] + late
            dy_ref[:, lanes] = (dxr * pair(rate, p, low) + pair(skip_ref[g], p, low1) * dyf).astype(bf16)
            q2 = x_ref[:, lanes].astype(f32) * late
            hi = q2.astype(bf16)
            dn_ref[:, here] = hi
            dn_ref[:, slice(EG + p * 128, EG + (p + 1) * 128)] = (q2 - hi.astype(f32)).astype(bf16)
        reach = reach_ref[:, wide]
        dbg_ref[g] += dot_nt(xw_ref[:, wide], reach)
        sums = []
        for v in (sin_ref[:, wide].astype(f32), ext_ref[0:N, wide].astype(f32)):
            v = jnp.sum(v * reach.astype(f32), axis=0, keepdims=True)
            a, b, _ = split3(jnp.broadcast_to(v, (16, EG)))
            sums.append((dot(a, heads) + dot(b, heads))[0:1])
        at_end = jnp.exp2(last) * sums[0] + sums[1]
        q2 = dot(dn_ref[:, 0:EG], heads) + dot(dn_ref[:, EG : 2 * EG], heads)
        qs_ref[g] = mask_dot(anticausal.astype(bf16), qs_ref[g] - rate * q2) + at_end
        qs_ref[G + g] += q2
        return 0

    lax.fori_loop(0, G, finish, 0)
    dx_out = pltpu.make_async_copy(dy_ref, dx_ref, local_sem.at[3])
    dx_out.start()
    a_neg = -jnp.exp(al_ref[...])
    slope = jax.nn.sigmoid(dt_ref[...].astype(f32).T + bias_ref[...])
    for g in range(G):
        here = slice(g * HG, (g + 1) * HG)
        d_rate = a_neg[:, here] * qs_ref[g] + qs_ref[G + g]
        ddt_ref[here, :] = (d_rate * slope[:, here]).T.astype(bf16)
        db_ref[:, g * N : (g + 1) * N] = dbg_ref[g].astype(bf16)
        dc_ref[:, g * N : (g + 1) * N] = dcg_ref[g]

    for k in range(1, 2 * NX):
        send_sum(k).wait_recv()
        hand_on(k).start()

    dx_out.wait()
    layer_copy.wait()
    dz_copy.wait()
    own_piece.wait()
    to_sibling.wait()
    for k in range(1, 2 * NX):
        send_sum(k).wait_send()
        hand_on(k).wait()
    for cp in sent:
        cp.wait_send()
    for part in range(2):
        for k in (1, 3):
            send_cot(k, part).wait_send()
        for side in range(2):
            hand_cot(part, side).wait_send()
    for k in (1, 3, 2):
        send_normed(k).wait_send()
    for make in (fwd_out, rev_out, rev_back):
        wait_send_all(make)
    for k in range(NDP):
        send_half(k).wait_send()
    for cp in step1 + step2:
        cp.wait_send()


def result_kernel(*refs):
    ins, outs = refs[:7], refs[7:14]
    held = refs[14:20]
    narrow, wide, sems, in_sems, out_sems = refs[20:]
    rows = narrow.shape[0] // 4
    loads = [pltpu.make_async_copy(ins[6].at[pl.ds(i * rows, rows)], narrow.at[pl.ds(i * rows, rows)], in_sems.at[i])
             for i in range(4)]
    for cp in loads:
        cp.start()
    arrays = [pltpu.make_async_copy(ins[i], held[i], sems.at[i]) for i in range(6)]
    for cp in arrays:
        cp.start()
    copies = []
    for i in range(4):
        here = pl.ds(i * rows, rows)
        loads[i].wait()
        wide[here] = narrow[here].astype(f32)
        cp = pltpu.make_async_copy(wide.at[here], outs[6].at[here], out_sems.at[i])
        cp.start()
        copies.append(cp)
    for i in range(6):
        arrays[i].wait()
        cp = pltpu.make_async_copy(held[i], outs[i], sems.at[6 + i])
        cp.start()
        copies.append(cp)
    for cp in copies:
        cp.wait()


def shards(xs, z_gate, b_proj, c_proj, dt_raw, a_log, dt_bias, d_skip, norm_gain, w_out, cotangent):
    rows = xs.shape[1]
    width = cotangent.shape[2]
    shard = w_out.shape[0]
    wide = ((rows, E), bf16)
    outs = [((rows, width), bf16), wide, wide, ((rows, G * N), bf16), ((rows, G * N), bf16), ((H, rows), bf16),
            ((shard, width), bf16)]
    state = ((N, E), bf16)
    ext = ((EXT, E), bf16)
    share = ((NCTX, EXT, SHARE), bf16)
    linked = ((NCTX, N, SHARE), bf16)
    per_group = ((G, rows, HG), f32)
    group_cols = ((G, rows, N), bf16)
    quad = ((NX, rows, E // NX), bf16)
    block = ((NDP, 128, width // 2), bf16)
    scratch = [
        wide, wide, ((rows, width), bf16), wide,
        ((NDP, shard, width), bf16), ((NX, rows, width), bf16), quad, quad, wide, wide, ((rows, E), f32),
        ((rows, E), f32), wide, wide, wide,
        ((rows, width), f32), ((rows, rows), f32),
        ((2 * G, rows, HG), f32), ((G, rows, N), f32), group_cols,
        per_group, per_group, ((H, rows), f32), group_cols, group_cols, ((rows, 128), f32), ((G, 1, HG), f32),
        ext, share, linked, state, ext, share, state,
        ((2, NZ, 128, width // 2), bf16), block, block, ((4, NZ, 64, width // 4), bf16), ((NZ, 2, 128, width // 4), bf16),
        ((NZ, 64, width // 4), bf16), ((4, 64, width // 4), bf16), ((64, width // 2), bf16),
    ]
    sems = [8, 32, 32, 8, 8, 3, 3] + [NCTX - 1] * 8 + [NDP, NDP, 12, 12] + [2 * NX] * 4
    vmem = pl.BlockSpec(memory_space=pltpu.VMEM)
    hbm = pl.BlockSpec(memory_space=pl.ANY)
    layer_out, dx, dz, db, dc, ddt, gw = pl.pallas_call(
        layer_kernel,
        out_shape=[jax.ShapeDtypeStruct(s, d) for s, d in outs],
        in_specs=[hbm] * 2 + [vmem] * 7 + [hbm] * 2,
        out_specs=[hbm] * 3 + [vmem] * 3 + [hbm],
        scratch_shapes=[pltpu.VMEM(s, d) for s, d in scratch] + [pltpu.SemaphoreType.DMA((n,)) for n in sems],
        compiler_params=pltpu.CompilerParams(
            collective_id=0, has_side_effects=True, vmem_limit_bytes=VMEM_LIMIT),
    )(xs[0], z_gate[0], b_proj[0], c_proj[0], dt_raw[0].T, a_log[None], dt_bias[None],
      d_skip[None], norm_gain[None], w_out, cotangent[0])
    layer_out, dx, dz, db, dc, ddt, gw = pl.pallas_call(
        result_kernel,
        out_shape=[jax.ShapeDtypeStruct(s, d) for s, d in outs[:6]] + [jax.ShapeDtypeStruct((shard, width), f32)],
        in_specs=[hbm] * 7,
        out_specs=[hbm] * 7,
        scratch_shapes=[pltpu.VMEM(s, d) for s, d in outs[:6]]
        + [pltpu.VMEM((shard, width), bf16), pltpu.VMEM((shard, width), f32), pltpu.SemaphoreType.DMA((12,)), pltpu.SemaphoreType.DMA((4,)),
           pltpu.SemaphoreType.DMA((4,))],
        compiler_params=pltpu.CompilerParams(vmem_limit_bytes=VMEM_LIMIT),
    )(layer_out, dx, dz, db, dc, ddt, gw)
    return layer_out[None], dx[None], dz[None], db[None], dc[None], ddt.T[None], gw


def solution(mesh):
    rows = P("dp", "ctx", None)
    in_specs = (rows,) * 5 + (P(),) * 4 + (P("dp", None), rows)
    out_specs = (rows,) * 6 + (P("dp", None),)
    return jax.shard_map(shards, mesh=mesh, in_specs=in_specs, out_specs=out_specs, check_vma=False)
```

```python
import math

import jax
import jax.numpy as jnp
from jax import lax
from jax.experimental import pallas as pl
from jax.experimental.pallas import tpu as pltpu
from jax.sharding import PartitionSpec as P

H = 64
P_SIZE = 64
N = 64
G = 4
E = 4096
HG = H // G
EG = E // G
EPSILON = 1e-05
LOG2E = math.log2(math.e)
EXT = 80
bf16 = jnp.bfloat16
f32 = jnp.float32
VMEM_LIMIT = 63 * 1024 * 1024
MESH = pl.DeviceIdType.MESH


def dot(a, b):
    return lax.dot_general(a, b, (((1,), (0,)), ((), ())), preferred_element_type=f32)


def dot_nt(a, b):
    return lax.dot_general(a, b, (((1,), (1,)), ((), ())), preferred_element_type=f32)


def dot_tn(a, b):
    return lax.dot_general(a, b, (((0,), (0,)), ((), ())), preferred_element_type=f32)


def split3(v):
    a = v.astype(bf16)
    rest = v - a.astype(f32)
    b = rest.astype(bf16)
    c = (rest - b.astype(f32)).astype(bf16)
    return a, b, c


def mask_dot(mask, v):
    a, b, c = split3(v)
    return dot(mask, a) + dot(mask, b) + dot(mask, c)


def low_half(rows):
    return lax.broadcasted_iota(jnp.int32, (rows, 128), 1) < P_SIZE


def pair(values, p, low):
    return jnp.where(low, values[:, 2 * p : 2 * p + 1], values[:, 2 * p + 1 : 2 * p + 2])


NZ = 4
NX = 4
NDP = 2 * NZ
NCTX = 4 * NX
SHARE = E // NCTX


def layer_kernel(x_in, z_in, b_ref, c_ref, dt_ref, al_ref, bias_ref, skips_ref, gain_ref, w_ref, cot_ref,
                 layer_ref, dx_ref, dz_out, db_ref, dc_ref, ddt_ref, gw_ref,
                 x_ref, z_ref, out_ref, dz_ref, w_all, cot_all, nb, nrecv, xr_ref, xw_ref, y_ref, wide_ref, dn_ref, dy_ref, dyel_ref,
                 lay_ref, dcb_ref, qs_ref, dbg_ref, dcg_ref,
                 lg_ref, rg_ref, lt_ref, bg_ref, cg_ref, acc_ref, skip_ref,
                 ext_ref, mine_ref, link_ref, sin_ref, gext_ref, gmine_ref, reach_ref,
                 own_ref, other_ref, sib_ref, ra1_ref, rb1_ref, ra2_ref, rb2_ref, piece_ref,
                 local_sem, w_send, w_recv, c_send, c_recv, n_send, n_recv,
                 a_send, a_recv, o_send, o_recv, ga_send, ga_recv, go_send, go_recv,
                 b_send, b_recv, r_send, r_recv, p_send, p_recv, f_send, f_recv):
    rows = x_ref.shape[0]
    width = cot_ref.shape[1]
    half_width = width // 2
    shard = w_ref.shape[0]
    half = shard // 2
    quarter = shard // 4
    dp = lax.axis_index("dp")
    ctx = lax.axis_index("ctx")
    yh, z = dp // NZ, dp % NZ
    x, yl, core = ctx // 4, (ctx // 2) % 2, ctx % 2
    z_up, z_down = (z + 1) % NZ, (z + NZ - 1) % NZ
    z_far = (z + 2) % NZ

    def dev(yh_=yh, z_=z, x_=x, yl_=yl, core_=core):
        return {"dp": yh_ * NZ + z_, "ctx": x_ * 4 + yl_ * 2 + core_}

    up, down = dev(z_=z_up), dev(z_=z_down)
    cross = dev(yh_=1 - yh, yl_=1 - yl)
    sibling = dev(core_=1 - core)

    def remote(src, dst, send, recv, target):
        return pltpu.make_async_remote_copy(
            src_ref=src, dst_ref=dst, send_sem=send, recv_sem=recv, device_id=target, device_id_type=MESH)

    x_copy = pltpu.make_async_copy(x_in, x_ref, local_sem.at[4])
    x_copy.start()
    z_copy = pltpu.make_async_copy(z_in, z_ref, local_sem.at[5])
    z_copy.start()

    def tokens(x_, start=0, count=rows):
        return pl.ds(pl.multiple_of(x_ * rows + start, 16), count)

    barrier = pltpu.get_barrier_semaphore()

    def greet_ctx(k, _):
        pl.semaphore_signal(barrier, inc=1, device_id={"dp": dp, "ctx": (ctx + k) % NCTX}, device_id_type=MESH)
        return 0

    for other in [dev(z_=(z + k) % NZ) for k in (1, 2, 3)] + [dev(yh_=1 - yh, yl_=k) for k in (0, 1)]:
        pl.semaphore_signal(barrier, inc=1, device_id=other, device_id_type=MESH)
    lax.fori_loop(1, NCTX, greet_ctx, 0)
    rate = jax.nn.softplus(dt_ref[...].astype(f32).T + bias_ref[...])
    steps = rate * (-LOG2E * jnp.exp(al_ref[...]))
    row_pos = lax.broadcasted_iota(jnp.int32, (rows, rows), 0)
    col_pos = lax.broadcasted_iota(jnp.int32, (rows, rows), 1)
    causal = row_pos >= col_pos
    anticausal = col_pos >= row_pos
    log = mask_dot(causal.astype(bf16), steps)
    lt_ref[...] = log.T
    last = log[rows - 1 : rows, :]
    to_end = jnp.exp2(last - log)
    low = low_half(rows)
    low1 = low_half(1)
    for g in range(G):
        lg_ref[g] = log[:, g * HG : (g + 1) * HG]
        rg_ref[g] = rate[:, g * HG : (g + 1) * HG]
        skip_ref[g] = skips_ref[:, g * HG : (g + 1) * HG]
        bg_ref[g] = b_ref[:, g * N : (g + 1) * N]
        cg_ref[g] = c_ref[:, g * N : (g + 1) * N]
    own_w = pltpu.make_async_copy(w_ref, w_all.at[dp], local_sem.at[0])
    own_w.start()
    own_cot = pltpu.make_async_copy(cot_ref, cot_all.at[tokens(x)], local_sem.at[1])
    own_cot.start()
    pl.semaphore_wait(barrier, NCTX - 1 + 5)

    up_y = dev(yl_=1 - yl)
    mine, theirs = yl, 1 - yl

    def unit(yh_, z_, q, part=None):
        start = core * half + q * quarter + (0 if part is None else part * (quarter // 2))
        count = quarter if part is None else quarter // 2
        return w_all.at[yh_ * NZ + z_, pl.ds(pl.multiple_of(start, quarter // 2), count)]

    waits = {}
    sent = []

    def send_w(name, src, target, dst=None):
        i = len(waits)
        cp = remote(src, src if dst is None else dst, w_send.at[i], w_recv.at[i], target)
        cp.start()
        waits[name] = cp
        sent.append(cp)

    def arrived(*names):
        for name in names:
            waits[name].wait_recv()

    def own_unit(q, part=None):
        start = core * half + q * quarter + (0 if part is None else part * (quarter // 2))
        count = quarter if part is None else quarter // 2
        return w_ref.at[pl.ds(pl.multiple_of(start, quarter // 2), count)]

    def share(name, yh_, z_, q):
        send_w(name, unit(yh_, z_, q), sibling)

    def send_cot(k, part):
        here = pl.ds(part * (rows // 2), rows // 2)
        i = k - 1 + part
        return remote(cot_ref.at[here], cot_all.at[tokens(x, part * (rows // 2), rows // 2)], c_send.at[i], c_recv.at[i], dev(x_=(x + k) % NX))

    def hand_cot(part, side):
        k = 1 + 2 * side
        there = cot_all.at[tokens((x + NX - k) % NX, part * (rows // 2) + side * (rows // 4), rows // 4)]
        i = 4 + 2 * part + side
        return remote(there, there, c_send.at[i], c_recv.at[i], dev(x_=(x + k) % NX))

    def pass_cot(part):
        for k in (1, 3):
            send_cot(k, part).wait_recv()
        for side in range(2):
            hand_cot(part, side).start()

    def send_normed(k):
        return remote(nb.at[(x + k) % NX], nrecv.at[tokens(x)], n_send.at[k - 1], n_recv.at[k - 1], dev(x_=(x + k) % NX))

    send_w("a1", own_unit(mine), up, unit(yh, z, mine))
    send_w("a2", own_unit(mine), down, unit(yh, z, mine))
    send_w("b1", own_unit(theirs), cross, unit(yh, z, theirs))
    send_w("e1", own_unit(theirs, 1), up, unit(yh, z, theirs, 1))
    send_w("e2", own_unit(theirs, 1), down, unit(yh, z, theirs, 1))
    send_w("b2", own_unit(mine), cross, unit(yh, z, mine))
    for k in (1, 3):
        send_cot(k, 0).start()
    x_copy.wait()
    for p in range(H // 2):
        lanes = slice(p * 128, (p + 1) * 128)
        xr = x_ref[:, lanes].astype(f32) * pair(rate, p, low)
        xr_ref[:, lanes] = xr.astype(bf16)
        xw_ref[:, lanes] = (xr * pair(to_end, p, low)).astype(bf16)
        hi, mid, lo = split3(pair(last, p, low1))
        tail = jnp.concatenate([hi, mid, lo, jnp.zeros((EXT - N - 3, 128), bf16)], axis=0)
        ext_ref[N:EXT, lanes] = tail
    for g in range(G):
        lanes = slice(g * EG, (g + 1) * EG)
        state = dot_tn(bg_ref[g], xw_ref[:, lanes])
        ext_ref[0:N, lanes] = state.astype(bf16)

    def lanes_of(j):
        return pl.ds(pl.multiple_of(j * SHARE, SHARE), SHARE)

    def along(k):
        return (ctx + k) % NCTX

    def spread(ext, into, sends, recvs, k):
        return remote(ext.at[:, lanes_of(along(k))], into.at[ctx], sends.at[k - 1], recvs.at[k - 1],
                      {"dp": dp, "ctx": along(k)})

    def back(linked, into, sends, recvs, k):
        return remote(linked.at[along(k)], into.at[:, lanes_of(ctx)], sends.at[k - 1], recvs.at[k - 1],
                      {"dp": dp, "ctx": along(k)})

    def start_all(make):
        lax.fori_loop(1, NCTX, lambda k, _: (make(k).start(), 0)[1], 0)

    def wait_recv_all(make):
        lax.fori_loop(1, NCTX, lambda k, _: (make(k).wait_recv(), 0)[1], 0)

    def wait_send_all(make):
        lax.fori_loop(1, NCTX, lambda k, _: (make(k).wait_send(), 0)[1], 0)

    def link(reverse, gathered, linked, into):
        acc = jnp.zeros((N, SHARE), f32)
        for step in range(NCTX):
            j = NCTX - 1 - step if reverse else step
            linked[j] = acc.astype(bf16)
            tail = mine_ref[j, N:EXT, :].astype(f32)
            total = tail[0:1] + tail[1:2] + tail[2:3]
            acc = jnp.exp2(total) * acc + gathered[j, 0:N, :].astype(f32)
        into[:, lanes_of(ctx)] = linked[ctx]

    fwd_out = lambda k: spread(ext_ref, mine_ref, a_send, a_recv, k)
    fwd_back = lambda k: back(link_ref, sin_ref, o_send, o_recv, k)
    rev_out = lambda k: spread(gext_ref, gmine_ref, ga_send, ga_recv, k)
    rev_back = lambda k: back(link_ref, reach_ref, go_send, go_recv, k)
    start_all(fwd_out)
    mine_ref[ctx] = ext_ref[:, lanes_of(ctx)]

    def within(g, _):
        base = pl.multiple_of(g * EG, EG)
        log = lg_ref[g]
        log_t = lt_ref[pl.ds(pl.multiple_of(g * HG, HG), HG), :]
        cb = dot_nt(cg_ref[g], bg_ref[g])
        for p in range(HG // 2):
            lanes = pl.ds(pl.multiple_of(base + p * 128, 128), 128)
            parts = []
            for h in (2 * p, 2 * p + 1):
                gap = jnp.where(causal, log[:, h : h + 1] - log_t[h : h + 1, :], -1e30)
                parts.append((cb * jnp.exp2(gap)).astype(bf16))
            both = dot(jnp.concatenate(parts, axis=0), xr_ref[:, lanes])
            y_ref[:, lanes] = jnp.where(low, both[:rows], both[rows:])
        return 0

    lax.fori_loop(0, G, within, 0)
    wait_recv_all(fwd_out)
    link(False, mine_ref, link_ref, sin_ref)
    start_all(fwd_back)

    arrived("b1")
    send_w("c1", unit(1 - yh, z, mine), up)
    send_w("c2", unit(1 - yh, z, mine), down)
    arrived("a1", "a2")
    for name, z_ in (("n1", z_down), ("n2", z_up)):
        send_w(name, unit(yh, z_, mine, 0), up_y)
    for name, z_ in (("m1", z_down), ("m2", z_up)):
        send_w(name, unit(yh, z_, mine), cross)
    share("s1", yh, z_down, mine)
    share("s2", yh, z_up, mine)
    share("s3", 1 - yh, z, mine)
    pass_cot(0)
    for k in (1, 3):
        send_cot(k, 1).start()

    wait_recv_all(fwd_back)

    z_copy.wait()
    acc_ref[...] = jnp.zeros_like(acc_ref)

    def gate(g, _):
        base = pl.multiple_of(g * EG, EG)
        grown = jnp.exp2(lg_ref[g])
        c_blk = cg_ref[g]
        total = acc_ref[...]
        for p in range(HG // 2):
            lanes = pl.ds(pl.multiple_of(base + p * 128, 128), 128)
            y = y_ref[:, lanes] + pair(grown, p, low) * dot(c_blk, sin_ref[:, lanes])
            y_ref[:, lanes] = y
            out = y + pair(skip_ref[g], p, low1) * x_ref[:, lanes].astype(f32)
            zf = z_ref[:, lanes].astype(f32)
            gated = out * (zf * jax.nn.sigmoid(zf))
            wide_ref[:, lanes] = gated
            total = total + gated * gated
        acc_ref[...] = total
        return 0

    lax.fori_loop(0, G, gate, 0)
    r = lax.rsqrt(jnp.sum(acc_ref[...], axis=1, keepdims=True) * (1.0 / E) + EPSILON)

    def norm(i, _):
        for q in range(NX):
            lanes = pl.ds(pl.multiple_of(i * 512 + q * 128, 128), 128)
            nb[q, :, pl.ds(pl.multiple_of(i * 128, 128), 128)] = (
                wide_ref[:, lanes] * r * gain_ref[:, lanes]).astype(bf16)
        return 0

    lax.fori_loop(0, NDP, norm, 0)
    for k in (1, 3, 2):
        send_normed(k).start()
    nrecv[tokens(x)] = nb[x]

    own_w.wait()
    own_cot.wait()
    lay_ref[...] = jnp.zeros_like(lay_ref)

    acc_ref[...] = jnp.zeros_like(acc_ref)

    def project_back(yh_, z_):
        k = yh_ * NZ + z_
        acc = acc_ref[...]
        for q in range(NX):
            lanes = pl.ds(pl.multiple_of(k * shard + q * 128, 128), 128)
            dn = dot_nt(cot_all[tokens(x)], w_all[k, q * 128 : (q + 1) * 128, :]).astype(bf16)
            dn_ref[:, lanes] = dn
            acc = acc + dn.astype(f32) * gain_ref[:, lanes] * wide_ref[:, lanes]
        acc_ref[...] = acc

    def project_out(yh_, z_):
        k = yh_ * NZ + z_
        block = jnp.concatenate([nb[q, :, pl.ds(pl.multiple_of(k * 128, 128), 128)] for q in range(NX)], axis=1)

        def tile(n, _):
            cols = pl.ds(pl.multiple_of(n * (width // 4), width // 4), width // 4)
            lay_ref[:, cols] += dot(block, w_all[k, :, cols])
            return 0

        lax.fori_loop(0, 4, tile, 0)

    def project(yh_, z_):
        project_back(yh_, z_)
        project_out(yh_, z_)

    project(yh, z)

    arrived("c1", "c2")
    send_w("g1", unit(1 - yh, z_down, mine, 0), up)
    send_w("g2", unit(1 - yh, z_up, mine, 1), down)
    send_w("f1", unit(yh, z_down, mine, 0), up)
    send_w("f2", unit(yh, z_up, mine, 1), down)
    arrived("e2")
    send_w("f4", unit(yh, z_up, theirs, 1), down)
    share("s6", 1 - yh, z_down, mine)
    share("s7", 1 - yh, z_up, mine)
    arrived("b2")
    share("s5", 1 - yh, z, theirs)
    pass_cot(1)
    arrived("n1")
    send_w("f3", unit(yh, z_down, theirs, 0), up)
    arrived("n2", "e1")
    share("s8", yh, z_down, theirs)
    share("s9", yh, z_up, theirs)
    arrived("s3", "s5")
    project(1 - yh, z)
    arrived("g1", "g2")
    send_w("n4", unit(1 - yh, z_far, mine), up_y)
    share("s10", 1 - yh, z_far, mine)
    arrived("s1", "s8")
    project(yh, z_down)
    arrived("s2", "s9")
    project(yh, z_up)

    arrived("m1", "m2")
    share("s11", 1 - yh, z_down, theirs)
    share("s12", 1 - yh, z_up, theirs)
    arrived("f1", "f2")
    share("s4", yh, z_far, mine)
    arrived("s6", "s11")
    project(1 - yh, z_down)
    arrived("f3", "f4")
    share("s13", yh, z_far, theirs)
    arrived("s7", "s12")
    project(1 - yh, z_up)
    arrived("s4", "s13")
    project(yh, z_far)
    arrived("n4")
    share("s14", 1 - yh, z_far, theirs)

    for part in range(2):
        for side in range(2):
            hand_cot(part, side).wait_recv()
    for k in (1, 3, 2):
        send_normed(k).wait_recv()

    def send_half(j):
        return remote(other_ref.at[j], sib_ref.at[j], b_send.at[j], b_recv.at[j], sibling)

    def product(j, side):
        cols = pl.ds(pl.multiple_of(side * half_width, half_width), half_width)
        return dot_tn(nrecv[:, pl.ds(pl.multiple_of(j * 256, 256), 256)], cot_all[:, cols]).astype(bf16)

    def weigh_other(j, _):
        other_ref[j] = product(j, 1 - core)
        send_half(j).start()
        return 0

    def weigh_own(j, _):
        part = product(j, core)
        own_ref[j // 2, 2 * (j % 2)] = part[0:128]
        own_ref[j // 2, 2 * (j % 2) + 1] = part[128:256]
        return 0

    def combine(j, _):
        send_half(j).wait_recv()
        for i in range(2):
            here = (j // 2, 2 * (j % 2) + i)
            got = sib_ref[j, i * 128 : (i + 1) * 128, :]
            own_ref[here] = (own_ref[here].astype(f32) + got.astype(f32)).astype(bf16)
        return 0

    lax.fori_loop(0, NDP // 2, weigh_other, 0)
    lax.fori_loop(0, NDP // 2, weigh_own, 0)
    lax.fori_loop(0, NDP // 2, combine, 0)

    y = 2 * yh + yl
    part_width = half_width // 2
    y_span = part_width // 4
    z_span = part_width - y_span

    def y_first(part, start=0):
        return pl.ds(part * start + part * (0 if start else y_span), y_span)

    def z_first(part, start=0):
        return pl.ds(part * start + (y_span if start else part * z_span), z_span)

    def rows_of(yl_):
        return pl.ds(pl.multiple_of(yl_ * 64, 64), 64)

    def reduce_copy(i, src, dst, target):
        return remote(src, dst, r_send.at[i], r_recv.at[i], target)

    def along_y(k):
        there = (y + k) % 4
        return there // 2, there % 2

    def first_step(part):
        copies = []
        for k in (1, 3, 2):
            yh_, yl_ = along_y(k)
            copies.append(reduce_copy(12 * part + k - 1, own_ref.at[yh_, :, rows_of(yl_), y_first(part, part_width)],
                                      ra1_ref.at[y, :, :, y_first(part)], dev(yh_=yh_, yl_=yl_)))
            z_ = (z + k) % NZ
            copies.append(reduce_copy(12 * part + k + 2, own_ref.at[:, z_, :, z_first(part, part_width)],
                                      rb1_ref.at[z, :, :, z_first(part)], dev(z_=z_)))
        for cp in copies:
            cp.start()
        return copies

    def total_of(ref, here):
        total = ref[(0, Ellipsis, here)].astype(f32)
        for q in range(1, 4):
            total = total + ref[(q, Ellipsis, here)].astype(f32)
        return total.astype(bf16)

    def second_step(part):
        for cp in step1[part]:
            cp.wait_recv()
        ya, za = y_first(part), z_first(part)
        ra1_ref[y, :, :, ya] = total_of(ra1_ref, ya)
        rb1_ref[z, :, :, za] = total_of(rb1_ref, za)
        copies = []
        for k in (1, 3, 2):
            yh_, yl_ = along_y(k)
            z_ = (z + k) % NZ
            copies.append(reduce_copy(12 * part + k + 5, ra1_ref.at[y, z_, :, ya], ra2_ref.at[z, :, ya],
                                      dev(z_=z_)))
            copies.append(reduce_copy(12 * part + k + 8, rb1_ref.at[z, yh_, rows_of(yl_), za],
                                      rb2_ref.at[y, :, za], dev(yh_=yh_, yl_=yl_)))
        for cp in copies:
            cp.start()
        ra2_ref[z, :, ya] = ra1_ref[y, z, :, ya]
        rb2_ref[y, :, za] = rb1_ref[z, yh, rows_of(yl), za]
        return copies

    def place(x_, yl_, part):
        rows_here = pl.ds(pl.multiple_of(x_ * 128 + yl_ * 64, 64), 64)
        start = core * half_width + part * (half_width // 2)
        return gw_ref.at[rows_here, pl.ds(pl.multiple_of(start, half_width // 2), half_width // 2)]

    def own_cols(part):
        return piece_ref.at[:, pl.ds(part * (half_width // 2), half_width // 2)]

    def send_sum(k, part):
        i = 8 * part + k
        target = sibling if k == 0 else dev(x_=(x + k // 2) % NX, yl_=(yl + k) % 2)
        return remote(own_cols(part), place(x, yl, part), p_send.at[i], p_recv.at[i], target)

    def hand_on(k, part):
        src = place((x + NX - k // 2) % NX, (yl + k) % 2, part)
        i = 8 * part + k
        return remote(src, src, f_send.at[i], f_recv.at[i], sibling)

    def own_piece(part):
        return pltpu.make_async_copy(own_cols(part), place(x, yl, part), local_sem.at[2 + 6 * part])

    def spread_sum(part):
        for cp in step2[part]:
            cp.wait_recv()
        piece_ref[:, y_first(part, part_width)] = total_of(ra2_ref, y_first(part))
        piece_ref[:, z_first(part, part_width)] = total_of(rb2_ref, z_first(part))
        for k in (2, 6, 4, 1, 3, 7, 5, 0):
            send_sum(k, part).start()
        own_piece(part).start()

    def hand_all(part):
        for k in (2, 6, 1, 3, 7, 4, 5):
            send_sum(k, part).wait_recv()
            hand_on(k, part).start()

    step1 = [first_step(0), first_step(1)]
    for part in range(2):
        ra1_ref[y, :, :, y_first(part)] = own_ref[yh, :, rows_of(yl), y_first(part, part_width)]
        rb1_ref[z, :, :, z_first(part)] = own_ref[:, z, :, z_first(part, part_width)]

    arrived("s10", "s14")
    project_back(1 - yh, z_far)

    inner = jnp.sum(acc_ref[...], axis=1, keepdims=True) * (1.0 / E)
    scaled = r * r * inner

    def gate_back(g, _):
        base = pl.multiple_of(g * EG, EG)
        grown = jnp.exp2(lg_ref[g])
        for p in range(HG // 2):
            lanes = pl.ds(pl.multiple_of(base + p * 128, 128), 128)
            zf = z_ref[:, lanes].astype(f32)
            sig = jax.nn.sigmoid(zf)
            silu = zf * sig
            out = y_ref[:, lanes] + pair(skip_ref[g], p, low1) * x_ref[:, lanes].astype(f32)
            dg = dn_ref[:, lanes].astype(f32) * gain_ref[:, lanes]
            d_gated = r * (dg - wide_ref[:, lanes] * scaled)
            dz_ref[:, lanes] = (d_gated * out * (sig * (1.0 + zf * (1.0 - sig)))).astype(bf16)
            dy = d_gated * silu
            dy_ref[:, lanes] = dy.astype(bf16)
            dyel_ref[:, lanes] = (dy * pair(grown, p, low)).astype(bf16)
        lanes = pl.ds(base, EG)
        gext_ref[:, lanes] = dot_tn(cg_ref[g], dyel_ref[:, lanes]).astype(bf16)
        return 0

    lax.fori_loop(0, G, gate_back, 0)
    dz_copy = pltpu.make_async_copy(dz_ref, dz_out, local_sem.at[7])
    dz_copy.start()
    start_all(rev_out)
    gmine_ref[ctx] = gext_ref[:, lanes_of(ctx)]
    project_out(1 - yh, z_far)
    out_ref[...] = lay_ref[...].astype(bf16)
    layer_copy = pltpu.make_async_copy(out_ref, layer_ref, local_sem.at[6])
    layer_copy.start()

    e_pos = lax.broadcasted_iota(jnp.int32, (EG, HG), 0)
    h_pos = lax.broadcasted_iota(jnp.int32, (EG, HG), 1)
    heads = ((e_pos // P_SIZE) == h_pos).astype(bf16)

    def within_back(g, _):
        base = pl.multiple_of(g * EG, EG)
        log = lg_ref[g]
        log_t = lt_ref[pl.ds(pl.multiple_of(g * HG, HG), HG), :]
        cbt = dot_nt(bg_ref[g], cg_ref[g])
        for p in range(HG // 2):
            lanes = pl.ds(pl.multiple_of(base + p * 128, 128), 128)
            dy = dy_ref[:, lanes]
            xr = xr_ref[:, lanes]
            decays = []
            parts = []
            for h in (2 * p, 2 * p + 1):
                gap = jnp.where(anticausal, log_t[h : h + 1, :] - log[:, h : h + 1], -1e30)
                decay = jnp.exp2(gap)
                decays.append(decay)
                parts.append((cbt * decay).astype(bf16))
            both = dot(jnp.concatenate(parts, axis=0), dy)
            dxr = jnp.where(low, both[:rows], both[rows:])
            wide_ref[:, lanes] = dxr
            q1 = dy.astype(f32) * y_ref[:, lanes] - xr.astype(f32) * dxr
            hi = q1.astype(bf16)
            dn_ref[:, slice(p * 128, (p + 1) * 128)] = hi
            dn_ref[:, slice(EG + p * 128, EG + (p + 1) * 128)] = (q1 - hi.astype(f32)).astype(bf16)
            dn_ref[:, slice(2 * EG + p * 128, 2 * EG + (p + 1) * 128)] = (
                x_ref[:, lanes].astype(f32) * dxr).astype(bf16)
            zero = jnp.zeros_like(xr)
            halves = jnp.concatenate([jnp.where(low, xr, zero), jnp.where(low, zero, xr)], axis=0)
            dm = dot_nt(halves, dy)
            add = dm[:rows] * decays[0] + dm[rows:] * decays[1]
            if p == 0:
                dcb_ref[...] = add
            else:
                dcb_ref[...] += add
        wide = pl.ds(base, EG)
        dcb = dcb_ref[...].astype(bf16)
        dbg_ref[g] = dot(dcb, cg_ref[g])
        qs_ref[g] = dot(dn_ref[:, 0:EG], heads) + dot(dn_ref[:, EG : 2 * EG], heads)
        qs_ref[G + g] = dot(dn_ref[:, 2 * EG : 3 * EG], heads)
        dcg_ref[g] = (dot_tn(dcb, bg_ref[g]) + dot_nt(dyel_ref[:, wide], sin_ref[:, wide])).astype(bf16)
        return 0

    lax.fori_loop(0, G // 2, within_back, 0)
    step2 = [second_step(0)]
    lax.fori_loop(G // 2, G, within_back, 0)
    wait_recv_all(rev_out)
    wait_send_all(fwd_back)
    link(True, gmine_ref, link_ref, reach_ref)
    start_all(rev_back)

    step2.append(second_step(1))
    spread_sum(0)
    wait_recv_all(rev_back)

    def finish(g, _):
        base = pl.multiple_of(g * EG, EG)
        wide = pl.ds(base, EG)
        log = lg_ref[g]
        rate = rg_ref[g]
        b_blk = bg_ref[g]
        last = log[rows - 1 : rows, :]
        to_end = jnp.exp2(last - log)
        for p in range(HG // 2):
            here = slice(p * 128, (p + 1) * 128)
            lanes = pl.ds(pl.multiple_of(base + p * 128, 128), 128)
            dyf = dy_ref[:, lanes].astype(f32)
            late = pair(to_end, p, low) * dot(b_blk, reach_ref[:, lanes])
            dxr = wide_ref[:, lanes] + late
            dy_ref[:, lanes] = (dxr * pair(rate, p, low) + pair(skip_ref[g], p, low1) * dyf).astype(bf16)
            q2 = x_ref[:, lanes].astype(f32) * late
            hi = q2.astype(bf16)
            dn_ref[:, here] = hi
            dn_ref[:, slice(EG + p * 128, EG + (p + 1) * 128)] = (q2 - hi.astype(f32)).astype(bf16)
        reach = reach_ref[:, wide]
        dbg_ref[g] += dot_nt(xw_ref[:, wide], reach)
        sums = []
        for v in (sin_ref[:, wide].astype(f32), ext_ref[0:N, wide].astype(f32)):
            v = jnp.sum(v * reach.astype(f32), axis=0, keepdims=True)
            a, b, _ = split3(jnp.broadcast_to(v, (16, EG)))
            sums.append((dot(a, heads) + dot(b, heads))[0:1])
        at_end = jnp.exp2(last) * sums[0] + sums[1]
        q2 = dot(dn_ref[:, 0:EG], heads) + dot(dn_ref[:, EG : 2 * EG], heads)
        qs_ref[g] = mask_dot(anticausal.astype(bf16), qs_ref[g] - rate * q2) + at_end
        qs_ref[G + g] += q2
        return 0

    lax.fori_loop(0, G // 2, finish, 0)
    spread_sum(1)
    lax.fori_loop(G // 2, G, finish, 0)
    hand_all(0)
    dx_out = pltpu.make_async_copy(dy_ref, dx_ref, local_sem.at[3])
    dx_out.start()
    a_neg = -jnp.exp(al_ref[...])
    slope = jax.nn.sigmoid(dt_ref[...].astype(f32).T + bias_ref[...])
    for g in range(G):
        here = slice(g * HG, (g + 1) * HG)
        d_rate = a_neg[:, here] * qs_ref[g] + qs_ref[G + g]
        ddt_ref[here, :] = (d_rate * slope[:, here]).T.astype(bf16)
        db_ref[:, g * N : (g + 1) * N] = dbg_ref[g].astype(bf16)
        dc_ref[:, g * N : (g + 1) * N] = dcg_ref[g]

    hand_all(1)

    dx_out.wait()
    layer_copy.wait()
    dz_copy.wait()
    for part in range(2):
        own_piece(part).wait()
        send_sum(0, part).wait()
        for k in range(1, 2 * NX):
            send_sum(k, part).wait_send()
            hand_on(k, part).wait()
    for cp in sent:
        cp.wait_send()
    for part in range(2):
        for k in (1, 3):
            send_cot(k, part).wait_send()
        for side in range(2):
            hand_cot(part, side).wait_send()
    for k in (1, 3, 2):
        send_normed(k).wait_send()
    for make in (fwd_out, rev_out, rev_back):
        wait_send_all(make)
    for k in range(NDP // 2):
        send_half(k).wait_send()
    for copies in step1 + step2:
        for cp in copies:
            cp.wait_send()


def result_kernel(*refs):
    ins, outs = refs[:7], refs[7:14]
    held = refs[14:20]
    narrow, wide, sems, in_sems, out_sems = refs[20:]
    rows = narrow.shape[0] // 4
    loads = [pltpu.make_async_copy(ins[6].at[pl.ds(i * rows, rows)], narrow.at[pl.ds(i * rows, rows)], in_sems.at[i])
             for i in range(4)]
    for cp in loads:
        cp.start()
    arrays = [pltpu.make_async_copy(ins[i], held[i], sems.at[i]) for i in range(6)]
    for cp in arrays:
        cp.start()
    copies = []
    for i in range(4):
        here = pl.ds(i * rows, rows)
        loads[i].wait()
        wide[here] = narrow[here].astype(f32)
        cp = pltpu.make_async_copy(wide.at[here], outs[6].at[here], out_sems.at[i])
        cp.start()
        copies.append(cp)
    for i in range(6):
        arrays[i].wait()
        cp = pltpu.make_async_copy(held[i], outs[i], sems.at[6 + i])
        cp.start()
        copies.append(cp)
    for cp in copies:
        cp.wait()


def shards(xs, z_gate, b_proj, c_proj, dt_raw, a_log, dt_bias, d_skip, norm_gain, w_out, cotangent):
    rows = xs.shape[1]
    width = cotangent.shape[2]
    shard = w_out.shape[0]
    wide = ((rows, E), bf16)
    outs = [((rows, width), bf16), wide, wide, ((rows, G * N), bf16), ((rows, G * N), bf16), ((H, rows), bf16),
            ((shard, width), bf16)]
    state = ((N, E), bf16)
    ext = ((EXT, E), bf16)
    share = ((NCTX, EXT, SHARE), bf16)
    linked = ((NCTX, N, SHARE), bf16)
    per_group = ((G, rows, HG), f32)
    group_cols = ((G, rows, N), bf16)
    quad = ((NX, rows, E // NX), bf16)
    block = ((NDP // 2, 256, width // 2), bf16)
    scratch = [
        wide, wide, ((rows, width), bf16), wide,
        ((NDP, shard, width), bf16), ((NX * rows, width), bf16), quad, ((NX * rows, E // NX), bf16), wide, wide, ((rows, E), f32),
        ((rows, E), f32), wide, wide, wide,
        ((rows, width), f32), ((rows, rows), f32),
        ((2 * G, rows, HG), f32), ((G, rows, N), f32), group_cols,
        per_group, per_group, ((H, rows), f32), group_cols, group_cols, ((rows, 128), f32), ((G, 1, HG), f32),
        ext, share, linked, state, state, linked, state,
        ((2, NZ, 128, width // 2), bf16), block, block, ((4, NZ, 64, width // 8), bf16), ((NZ, 2, 128, 3 * width // 8), bf16),
        ((NZ, 64, width // 8), bf16), ((4, 64, 3 * width // 8), bf16), ((64, width // 2), bf16),
    ]
    sems = [9, 36, 36, 8, 8, 3, 3] + [NCTX - 1] * 8 + [NDP // 2, NDP // 2, 24, 24] + [4 * NX] * 4
    vmem = pl.BlockSpec(memory_space=pltpu.VMEM)
    hbm = pl.BlockSpec(memory_space=pl.ANY)
    layer_out, dx, dz, db, dc, ddt, gw = pl.pallas_call(
        layer_kernel,
        out_shape=[jax.ShapeDtypeStruct(s, d) for s, d in outs],
        in_specs=[hbm] * 2 + [vmem] * 7 + [hbm] * 2,
        out_specs=[hbm] * 3 + [vmem] * 3 + [hbm],
        scratch_shapes=[pltpu.VMEM(s, d) for s, d in scratch] + [pltpu.SemaphoreType.DMA((n,)) for n in sems],
        compiler_params=pltpu.CompilerParams(
            collective_id=0, has_side_effects=True, vmem_limit_bytes=VMEM_LIMIT),
    )(xs[0], z_gate[0], b_proj[0], c_proj[0], dt_raw[0].T, a_log[None], dt_bias[None],
      d_skip[None], norm_gain[None], w_out, cotangent[0])
    layer_out, dx, dz, db, dc, ddt, gw = pl.pallas_call(
        result_kernel,
        out_shape=[jax.ShapeDtypeStruct(s, d) for s, d in outs[:6]] + [jax.ShapeDtypeStruct((shard, width), f32)],
        in_specs=[hbm] * 7,
        out_specs=[hbm] * 7,
        scratch_shapes=[pltpu.VMEM(s, d) for s, d in outs[:6]]
        + [pltpu.VMEM((shard, width), bf16), pltpu.VMEM((shard, width), f32), pltpu.SemaphoreType.DMA((12,)), pltpu.SemaphoreType.DMA((4,)),
           pltpu.SemaphoreType.DMA((4,))],
        compiler_params=pltpu.CompilerParams(vmem_limit_bytes=VMEM_LIMIT),
    )(layer_out, dx, dz, db, dc, ddt, gw)
    return layer_out[None], dx[None], dz[None], db[None], dc[None], ddt.T[None], gw


def solution(mesh):
    rows = P("dp", "ctx", None)
    in_specs = (rows,) * 5 + (P(),) * 4 + (P("dp", None), rows)
    out_specs = (rows,) * 6 + (P("dp", None),)
    return jax.shard_map(shards, mesh=mesh, in_specs=in_specs, out_specs=out_specs, check_vma=False)
```

```python
import math

import jax
import jax.numpy as jnp
from jax import lax
from jax.experimental import pallas as pl
from jax.experimental.pallas import tpu as pltpu
from jax.sharding import PartitionSpec as P

H = 64
P_SIZE = 64
N = 64
G = 4
E = 4096
HG = H // G
EG = E // G
EPSILON = 1e-05
LOG2E = math.log2(math.e)
EXT = 80
bf16 = jnp.bfloat16
f32 = jnp.float32
VMEM_LIMIT = 63 * 1024 * 1024
MESH = pl.DeviceIdType.MESH


def dot(a, b):
    return lax.dot_general(a, b, (((1,), (0,)), ((), ())), preferred_element_type=f32)


def dot_nt(a, b):
    return lax.dot_general(a, b, (((1,), (1,)), ((), ())), preferred_element_type=f32)


def dot_tn(a, b):
    return lax.dot_general(a, b, (((0,), (0,)), ((), ())), preferred_element_type=f32)


def split3(v):
    a = v.astype(bf16)
    rest = v - a.astype(f32)
    b = rest.astype(bf16)
    c = (rest - b.astype(f32)).astype(bf16)
    return a, b, c


def mask_dot(mask, v):
    a, b, c = split3(v)
    return dot(mask, a) + dot(mask, b) + dot(mask, c)


def low_half(rows):
    return lax.broadcasted_iota(jnp.int32, (rows, 128), 1) < P_SIZE


def pair(values, p, low):
    return jnp.where(low, values[:, 2 * p : 2 * p + 1], values[:, 2 * p + 1 : 2 * p + 2])


NZ = 4
NX = 4
NDP = 2 * NZ
NCTX = 4 * NX
SHARE = E // NCTX


def layer_kernel(x_in, z_in, b_ref, c_ref, dt_ref, al_ref, bias_ref, skips_ref, gain_ref, w_ref, cot_ref,
                 layer_ref, dx_ref, dz_out, db_ref, dc_ref, ddt_ref, gw_ref,
                 x_ref, z_ref, out_ref, dz_ref, w_all, cot_all, nb, nrecv, xr_ref, xw_ref, y_ref, wide_ref, dn_ref, dy_ref, dyel_ref,
                 lay_ref, dcb_ref, qs_ref, dbg_ref, dcg_ref,
                 lg_ref, rg_ref, lt_ref, bg_ref, cg_ref, acc_ref, skip_ref,
                 ext_ref, mine_ref, link_ref, sin_ref, gext_ref, gmine_ref, reach_ref,
                 own_ref, other_ref, sib_ref, ra1_ref, rb1_ref, ra2_ref, rb2_ref, piece_ref,
                 local_sem, w_send, w_recv, c_send, c_recv, n_send, n_recv,
                 a_send, a_recv, o_send, o_recv, ga_send, ga_recv, go_send, go_recv,
                 b_send, b_recv, r_send, r_recv, p_send, p_recv, f_send, f_recv):
    rows = x_ref.shape[0]
    width = cot_ref.shape[1]
    half_width = width // 2
    shard = w_ref.shape[0]
    half = shard // 2
    quarter = shard // 4
    dp = lax.axis_index("dp")
    ctx = lax.axis_index("ctx")
    yh, z = dp // NZ, dp % NZ
    x, yl, core = ctx // 4, (ctx // 2) % 2, ctx % 2
    z_up, z_down = (z + 1) % NZ, (z + NZ - 1) % NZ
    z_far = (z + 2) % NZ

    def dev(yh_=yh, z_=z, x_=x, yl_=yl, core_=core):
        return {"dp": yh_ * NZ + z_, "ctx": x_ * 4 + yl_ * 2 + core_}

    up, down = dev(z_=z_up), dev(z_=z_down)
    cross = dev(yh_=1 - yh, yl_=1 - yl)
    sibling = dev(core_=1 - core)

    def remote(src, dst, send, recv, target):
        return pltpu.make_async_remote_copy(
            src_ref=src, dst_ref=dst, send_sem=send, recv_sem=recv, device_id=target, device_id_type=MESH)

    x_copy = pltpu.make_async_copy(x_in, x_ref, local_sem.at[4])
    x_copy.start()
    z_copy = pltpu.make_async_copy(z_in, z_ref, local_sem.at[5])
    z_copy.start()

    def tokens(x_, start=0, count=rows):
        return pl.ds(pl.multiple_of(x_ * rows + start, 16), count)

    barrier = pltpu.get_barrier_semaphore()

    def greet_ctx(k, _):
        pl.semaphore_signal(barrier, inc=1, device_id={"dp": dp, "ctx": (ctx + k) % NCTX}, device_id_type=MESH)
        return 0

    for other in [dev(z_=(z + k) % NZ) for k in (1, 2, 3)] + [dev(yh_=1 - yh, yl_=k) for k in (0, 1)]:
        pl.semaphore_signal(barrier, inc=1, device_id=other, device_id_type=MESH)
    lax.fori_loop(1, NCTX, greet_ctx, 0)
    rate = jax.nn.softplus(dt_ref[...].astype(f32).T + bias_ref[...])
    steps = rate * (-LOG2E * jnp.exp(al_ref[...]))
    row_pos = lax.broadcasted_iota(jnp.int32, (rows, rows), 0)
    col_pos = lax.broadcasted_iota(jnp.int32, (rows, rows), 1)
    causal = row_pos >= col_pos
    anticausal = col_pos >= row_pos
    log = mask_dot(causal.astype(bf16), steps)
    lt_ref[...] = log.T
    last = log[rows - 1 : rows, :]
    to_end = jnp.exp2(last - log)
    low = low_half(rows)
    low1 = low_half(1)
    for g in range(G):
        lg_ref[g] = log[:, g * HG : (g + 1) * HG]
        rg_ref[g] = rate[:, g * HG : (g + 1) * HG]
        skip_ref[g] = skips_ref[:, g * HG : (g + 1) * HG]
        bg_ref[g] = b_ref[:, g * N : (g + 1) * N]
        cg_ref[g] = c_ref[:, g * N : (g + 1) * N]
    own_w = pltpu.make_async_copy(w_ref, w_all.at[dp], local_sem.at[0])
    own_w.start()
    own_cot = pltpu.make_async_copy(cot_ref, cot_all.at[tokens(x)], local_sem.at[1])
    own_cot.start()
    pl.semaphore_wait(barrier, NCTX - 1 + 5)

    up_y = dev(yl_=1 - yl)
    mine, theirs = yl, 1 - yl

    def unit(yh_, z_, q, part=None):
        start = core * half + q * quarter + (0 if part is None else part * (quarter // 2))
        count = quarter if part is None else quarter // 2
        return w_all.at[yh_ * NZ + z_, pl.ds(pl.multiple_of(start, quarter // 2), count)]

    waits = {}
    sent = []

    def send_w(name, src, target, dst=None):
        i = len(waits)
        cp = remote(src, src if dst is None else dst, w_send.at[i], w_recv.at[i], target)
        cp.start()
        waits[name] = cp
        sent.append(cp)

    def arrived(*names):
        for name in names:
            waits[name].wait_recv()

    def own_unit(q, part=None):
        start = core * half + q * quarter + (0 if part is None else part * (quarter // 2))
        count = quarter if part is None else quarter // 2
        return w_ref.at[pl.ds(pl.multiple_of(start, quarter // 2), count)]

    def share(name, yh_, z_, q):
        send_w(name, unit(yh_, z_, q), sibling)

    def send_cot(k, part):
        here = pl.ds(part * (rows // 2), rows // 2)
        i = k - 1 + part
        return remote(cot_ref.at[here], cot_all.at[tokens(x, part * (rows // 2), rows // 2)], c_send.at[i], c_recv.at[i], dev(x_=(x + k) % NX))

    def hand_cot(part, side):
        k = 1 + 2 * side
        there = cot_all.at[tokens((x + NX - k) % NX, part * (rows // 2) + side * (rows // 4), rows // 4)]
        i = 4 + 2 * part + side
        return remote(there, there, c_send.at[i], c_recv.at[i], dev(x_=(x + k) % NX))

    def pass_cot(part):
        for k in (1, 3):
            send_cot(k, part).wait_recv()
        for side in range(2):
            hand_cot(part, side).start()

    def send_normed(k):
        return remote(nb.at[(x + k) % NX], nrecv.at[tokens(x)], n_send.at[k - 1], n_recv.at[k - 1], dev(x_=(x + k) % NX))

    send_w("a1", own_unit(mine), up, unit(yh, z, mine))
    send_w("a2", own_unit(mine), down, unit(yh, z, mine))
    send_w("b1", own_unit(theirs), cross, unit(yh, z, theirs))
    send_w("e1", own_unit(theirs, 1), up, unit(yh, z, theirs, 1))
    send_w("e2", own_unit(theirs, 1), down, unit(yh, z, theirs, 1))
    send_w("b2", own_unit(mine), cross, unit(yh, z, mine))
    for k in (1, 3):
        send_cot(k, 0).start()
    x_copy.wait()
    for p in range(H // 2):
        lanes = slice(p * 128, (p + 1) * 128)
        xr = x_ref[:, lanes].astype(f32) * pair(rate, p, low)
        xr_ref[:, lanes] = xr.astype(bf16)
        xw_ref[:, lanes] = (xr * pair(to_end, p, low)).astype(bf16)
        hi, mid, lo = split3(pair(last, p, low1))
        tail = jnp.concatenate([hi, mid, lo, jnp.zeros((EXT - N - 3, 128), bf16)], axis=0)
        ext_ref[N:EXT, lanes] = tail
    for g in range(G):
        lanes = slice(g * EG, (g + 1) * EG)
        state = dot_tn(bg_ref[g], xw_ref[:, lanes])
        ext_ref[0:N, lanes] = state.astype(bf16)

    def lanes_of(j):
        return pl.ds(pl.multiple_of(j * SHARE, SHARE), SHARE)

    def along(k):
        return (ctx + k) % NCTX

    def spread(ext, into, sends, recvs, k):
        return remote(ext.at[:, lanes_of(along(k))], into.at[ctx], sends.at[k - 1], recvs.at[k - 1],
                      {"dp": dp, "ctx": along(k)})

    def back(linked, into, sends, recvs, k):
        return remote(linked.at[along(k)], into.at[:, lanes_of(ctx)], sends.at[k - 1], recvs.at[k - 1],
                      {"dp": dp, "ctx": along(k)})

    def start_all(make):
        lax.fori_loop(1, NCTX, lambda k, _: (make(k).start(), 0)[1], 0)

    def wait_recv_all(make):
        lax.fori_loop(1, NCTX, lambda k, _: (make(k).wait_recv(), 0)[1], 0)

    def wait_send_all(make):
        lax.fori_loop(1, NCTX, lambda k, _: (make(k).wait_send(), 0)[1], 0)

    def link(reverse, gathered, linked, into):
        acc = jnp.zeros((N, SHARE), f32)
        for step in range(NCTX):
            j = NCTX - 1 - step if reverse else step
            linked[j] = acc.astype(bf16)
            tail = mine_ref[j, N:EXT, :].astype(f32)
            total = tail[0:1] + tail[1:2] + tail[2:3]
            acc = jnp.exp2(total) * acc + gathered[j, 0:N, :].astype(f32)
        into[:, lanes_of(ctx)] = linked[ctx]

    fwd_out = lambda k: spread(ext_ref, mine_ref, a_send, a_recv, k)
    fwd_back = lambda k: back(link_ref, sin_ref, o_send, o_recv, k)
    rev_out = lambda k: spread(gext_ref, gmine_ref, ga_send, ga_recv, k)
    rev_back = lambda k: back(link_ref, reach_ref, go_send, go_recv, k)
    start_all(fwd_out)
    mine_ref[ctx] = ext_ref[:, lanes_of(ctx)]

    def within(g, _):
        base = pl.multiple_of(g * EG, EG)
        log = lg_ref[g]
        log_t = lt_ref[pl.ds(pl.multiple_of(g * HG, HG), HG), :]
        cb = dot_nt(cg_ref[g], bg_ref[g])
        for p in range(HG // 2):
            lanes = pl.ds(pl.multiple_of(base + p * 128, 128), 128)
            parts = []
            for h in (2 * p, 2 * p + 1):
                gap = jnp.where(causal, log[:, h : h + 1] - log_t[h : h + 1, :], -1e30)
                parts.append((cb * jnp.exp2(gap)).astype(bf16))
            both = dot(jnp.concatenate(parts, axis=0), xr_ref[:, lanes])
            y_ref[:, lanes] = jnp.where(low, both[:rows], both[rows:])
        return 0

    lax.fori_loop(0, G, within, 0)
    wait_recv_all(fwd_out)
    link(False, mine_ref, link_ref, sin_ref)
    start_all(fwd_back)

    arrived("b1")
    send_w("c1", unit(1 - yh, z, mine), up)
    send_w("c2", unit(1 - yh, z, mine), down)
    arrived("a1", "a2")
    for name, z_ in (("n1", z_down), ("n2", z_up)):
        send_w(name, unit(yh, z_, mine, 0), up_y)
    for name, z_ in (("m1", z_down), ("m2", z_up)):
        send_w(name, unit(yh, z_, mine), cross)
    share("s1", yh, z_down, mine)
    share("s2", yh, z_up, mine)
    share("s3", 1 - yh, z, mine)
    pass_cot(0)
    for k in (1, 3):
        send_cot(k, 1).start()

    wait_recv_all(fwd_back)

    z_copy.wait()
    acc_ref[...] = jnp.zeros_like(acc_ref)

    def gate(g, _):
        base = pl.multiple_of(g * EG, EG)
        grown = jnp.exp2(lg_ref[g])
        c_blk = cg_ref[g]
        total = acc_ref[...]
        for p in range(HG // 2):
            lanes = pl.ds(pl.multiple_of(base + p * 128, 128), 128)
            y = y_ref[:, lanes] + pair(grown, p, low) * dot(c_blk, sin_ref[:, lanes])
            y_ref[:, lanes] = y
            out = y + pair(skip_ref[g], p, low1) * x_ref[:, lanes].astype(f32)
            zf = z_ref[:, lanes].astype(f32)
            gated = out * (zf * jax.nn.sigmoid(zf))
            wide_ref[:, lanes] = gated
            total = total + gated * gated
        acc_ref[...] = total
        return 0

    lax.fori_loop(0, G, gate, 0)
    r = lax.rsqrt(jnp.sum(acc_ref[...], axis=1, keepdims=True) * (1.0 / E) + EPSILON)

    def norm(i, _):
        for q in range(NX):
            lanes = pl.ds(pl.multiple_of(i * 512 + q * 128, 128), 128)
            nb[q, :, pl.ds(pl.multiple_of(i * 128, 128), 128)] = (
                wide_ref[:, lanes] * r * gain_ref[:, lanes]).astype(bf16)
        return 0

    lax.fori_loop(0, NDP, norm, 0)
    for k in (1, 3, 2):
        send_normed(k).start()
    nrecv[tokens(x)] = nb[x]

    own_w.wait()
    own_cot.wait()
    lay_ref[...] = jnp.zeros_like(lay_ref)

    acc_ref[...] = jnp.zeros_like(acc_ref)

    def project_back(yh_, z_):
        k = yh_ * NZ + z_
        acc = acc_ref[...]
        for q in range(NX):
            lanes = pl.ds(pl.multiple_of(k * shard + q * 128, 128), 128)
            dn = dot_nt(cot_all[tokens(x)], w_all[k, q * 128 : (q + 1) * 128, :]).astype(bf16)
            dn_ref[:, lanes] = dn
            acc = acc + dn.astype(f32) * gain_ref[:, lanes] * wide_ref[:, lanes]
        acc_ref[...] = acc

    def project_out(yh_, z_):
        k = yh_ * NZ + z_
        block = jnp.concatenate([nb[q, :, pl.ds(pl.multiple_of(k * 128, 128), 128)] for q in range(NX)], axis=1)

        def tile(n, _):
            cols = pl.ds(pl.multiple_of(n * (width // 4), width // 4), width // 4)
            lay_ref[:, cols] += dot(block, w_all[k, :, cols])
            return 0

        lax.fori_loop(0, 4, tile, 0)

    def project(yh_, z_):
        project_back(yh_, z_)
        project_out(yh_, z_)

    project(yh, z)

    arrived("c1", "c2")
    send_w("g1", unit(1 - yh, z_down, mine, 0), up)
    send_w("g2", unit(1 - yh, z_up, mine, 1), down)
    send_w("f1", unit(yh, z_down, mine, 0), up)
    send_w("f2", unit(yh, z_up, mine, 1), down)
    arrived("e2")
    send_w("f4", unit(yh, z_up, theirs, 1), down)
    share("s6", 1 - yh, z_down, mine)
    share("s7", 1 - yh, z_up, mine)
    arrived("b2")
    share("s5", 1 - yh, z, theirs)
    pass_cot(1)
    arrived("n1")
    send_w("f3", unit(yh, z_down, theirs, 0), up)
    arrived("n2", "e1")
    share("s8", yh, z_down, theirs)
    share("s9", yh, z_up, theirs)
    arrived("s3", "s5")
    project(1 - yh, z)
    arrived("g1", "g2")
    send_w("n4", unit(1 - yh, z_far, mine), up_y)
    share("s10", 1 - yh, z_far, mine)
    arrived("s1", "s8")
    project(yh, z_down)
    arrived("s2", "s9")
    project(yh, z_up)

    arrived("m1", "m2")
    share("s11", 1 - yh, z_down, theirs)
    share("s12", 1 - yh, z_up, theirs)
    arrived("f1", "f2")
    share("s4", yh, z_far, mine)
    arrived("s6", "s11")
    project(1 - yh, z_down)
    arrived("f3", "f4")
    share("s13", yh, z_far, theirs)
    arrived("s7", "s12")
    project(1 - yh, z_up)
    arrived("s4", "s13")
    project(yh, z_far)
    arrived("n4")
    share("s14", 1 - yh, z_far, theirs)

    arrived("s10", "s14")
    project_back(1 - yh, z_far)

    inner = jnp.sum(acc_ref[...], axis=1, keepdims=True) * (1.0 / E)
    scaled = r * r * inner

    def gate_back(g, _):
        base = pl.multiple_of(g * EG, EG)
        grown = jnp.exp2(lg_ref[g])
        for p in range(HG // 2):
            lanes = pl.ds(pl.multiple_of(base + p * 128, 128), 128)
            zf = z_ref[:, lanes].astype(f32)
            sig = jax.nn.sigmoid(zf)
            silu = zf * sig
            out = y_ref[:, lanes] + pair(skip_ref[g], p, low1) * x_ref[:, lanes].astype(f32)
            dg = dn_ref[:, lanes].astype(f32) * gain_ref[:, lanes]
            d_gated = r * (dg - wide_ref[:, lanes] * scaled)
            dz_ref[:, lanes] = (d_gated * out * (sig * (1.0 + zf * (1.0 - sig)))).astype(bf16)
            dy = d_gated * silu
            dy_ref[:, lanes] = dy.astype(bf16)
            dyel_ref[:, lanes] = (dy * pair(grown, p, low)).astype(bf16)
        lanes = pl.ds(base, EG)
        gext_ref[:, lanes] = dot_tn(cg_ref[g], dyel_ref[:, lanes]).astype(bf16)
        return 0

    lax.fori_loop(0, G, gate_back, 0)
    dz_copy = pltpu.make_async_copy(dz_ref, dz_out, local_sem.at[7])
    dz_copy.start()
    start_all(rev_out)
    gmine_ref[ctx] = gext_ref[:, lanes_of(ctx)]

    for part in range(2):
        for side in range(2):
            hand_cot(part, side).wait_recv()
    for k in (1, 3, 2):
        send_normed(k).wait_recv()

    def send_half(j):
        return remote(other_ref.at[j], sib_ref.at[j], b_send.at[j], b_recv.at[j], sibling)

    def product(j, side):
        cols = pl.ds(pl.multiple_of(side * half_width, half_width), half_width)
        return dot_tn(nrecv[:, pl.ds(pl.multiple_of(j * 256, 256), 256)], cot_all[:, cols]).astype(bf16)

    def weigh_other(j, _):
        other_ref[j] = product(j, 1 - core)
        send_half(j).start()
        return 0

    def weigh_own(j, _):
        part = product(j, core)
        own_ref[j // 2, 2 * (j % 2)] = part[0:128]
        own_ref[j // 2, 2 * (j % 2) + 1] = part[128:256]
        return 0

    def combine(j, _):
        send_half(j).wait_recv()
        for i in range(2):
            here = (j // 2, 2 * (j % 2) + i)
            got = sib_ref[j, i * 128 : (i + 1) * 128, :]
            own_ref[here] = (own_ref[here].astype(f32) + got.astype(f32)).astype(bf16)
        return 0

    lax.fori_loop(0, NDP // 2, weigh_other, 0)
    lax.fori_loop(0, NDP // 2, weigh_own, 0)
    lax.fori_loop(0, NDP // 2, combine, 0)

    y = 2 * yh + yl
    part_width = half_width // 2
    y_spans = (part_width // 4, part_width // 2)
    z_spans = tuple(part_width - n for n in y_spans)

    def y_first(part, whole=False):
        return pl.ds(part * part_width if whole else part * y_spans[0], y_spans[part])

    def z_first(part, whole=False):
        return pl.ds(part * part_width + y_spans[part] if whole else part * z_spans[0], z_spans[part])

    def rows_of(yl_):
        return pl.ds(pl.multiple_of(yl_ * 64, 64), 64)

    def reduce_copy(i, src, dst, target):
        return remote(src, dst, r_send.at[i], r_recv.at[i], target)

    def along_y(k):
        there = (y + k) % 4
        return there // 2, there % 2

    def first_step(part):
        copies = []
        for k in (1, 3, 2):
            yh_, yl_ = along_y(k)
            copies.append(reduce_copy(12 * part + k - 1, own_ref.at[yh_, :, rows_of(yl_), y_first(part, True)],
                                      ra1_ref.at[y, :, :, y_first(part)], dev(yh_=yh_, yl_=yl_)))
            z_ = (z + k) % NZ
            copies.append(reduce_copy(12 * part + k + 2, own_ref.at[:, z_, :, z_first(part, True)],
                                      rb1_ref.at[z, :, :, z_first(part)], dev(z_=z_)))
        for cp in copies:
            cp.start()
        return copies

    def total_of(ref, here):
        total = ref[(0, Ellipsis, here)].astype(f32)
        for q in range(1, 4):
            total = total + ref[(q, Ellipsis, here)].astype(f32)
        return total.astype(bf16)

    def second_step(part):
        for cp in step1[part]:
            cp.wait_recv()
        ya, za = y_first(part), z_first(part)
        ra1_ref[y, :, :, ya] = total_of(ra1_ref, ya)
        rb1_ref[z, :, :, za] = total_of(rb1_ref, za)
        copies = []
        for k in (1, 3, 2):
            yh_, yl_ = along_y(k)
            z_ = (z + k) % NZ
            copies.append(reduce_copy(12 * part + k + 5, ra1_ref.at[y, z_, :, ya], ra2_ref.at[z, :, ya],
                                      dev(z_=z_)))
            copies.append(reduce_copy(12 * part + k + 8, rb1_ref.at[z, yh_, rows_of(yl_), za],
                                      rb2_ref.at[y, :, za], dev(yh_=yh_, yl_=yl_)))
        for cp in copies:
            cp.start()
        ra2_ref[z, :, ya] = ra1_ref[y, z, :, ya]
        rb2_ref[y, :, za] = rb1_ref[z, yh, rows_of(yl), za]
        return copies

    def place(x_, yl_, part):
        rows_here = pl.ds(pl.multiple_of(x_ * 128 + yl_ * 64, 64), 64)
        start = core * half_width + part * (half_width // 2)
        return gw_ref.at[rows_here, pl.ds(pl.multiple_of(start, half_width // 2), half_width // 2)]

    def own_cols(part):
        return piece_ref.at[:, pl.ds(part * (half_width // 2), half_width // 2)]

    def send_sum(k, part):
        i = 8 * part + k
        target = sibling if k == 0 else dev(x_=(x + k // 2) % NX, yl_=(yl + k) % 2)
        return remote(own_cols(part), place(x, yl, part), p_send.at[i], p_recv.at[i], target)

    def hand_on(k, part):
        src = place((x + NX - k // 2) % NX, (yl + k) % 2, part)
        i = 8 * part + k
        return remote(src, src, f_send.at[i], f_recv.at[i], sibling)

    def own_piece(part):
        return pltpu.make_async_copy(own_cols(part), place(x, yl, part), local_sem.at[2 + 6 * part])

    def spread_sum(part):
        for cp in step2[part]:
            cp.wait_recv()
        piece_ref[:, y_first(part, True)] = total_of(ra2_ref, y_first(part))
        piece_ref[:, z_first(part, True)] = total_of(rb2_ref, z_first(part))
        for k in (2, 6, 4, 1, 3, 7, 5, 0):
            send_sum(k, part).start()
        own_piece(part).start()

    def hand_all(part):
        for k in (2, 6, 1, 3, 7, 4, 5):
            send_sum(k, part).wait_recv()
            hand_on(k, part).start()

    step1 = [first_step(0), first_step(1)]
    for part in range(2):
        ra1_ref[y, :, :, y_first(part)] = own_ref[yh, :, rows_of(yl), y_first(part, True)]
        rb1_ref[z, :, :, z_first(part)] = own_ref[:, z, :, z_first(part, True)]

    project_out(1 - yh, z_far)
    out_ref[...] = lay_ref[...].astype(bf16)
    layer_copy = pltpu.make_async_copy(out_ref, layer_ref, local_sem.at[6])
    layer_copy.start()

    e_pos = lax.broadcasted_iota(jnp.int32, (EG, HG), 0)
    h_pos = lax.broadcasted_iota(jnp.int32, (EG, HG), 1)
    heads = ((e_pos // P_SIZE) == h_pos).astype(bf16)

    def within_back(g, _):
        base = pl.multiple_of(g * EG, EG)
        log = lg_ref[g]
        log_t = lt_ref[pl.ds(pl.multiple_of(g * HG, HG), HG), :]
        cbt = dot_nt(bg_ref[g], cg_ref[g])
        for p in range(HG // 2):
            lanes = pl.ds(pl.multiple_of(base + p * 128, 128), 128)
            dy = dy_ref[:, lanes]
            xr = xr_ref[:, lanes]
            decays = []
            parts = []
            for h in (2 * p, 2 * p + 1):
                gap = jnp.where(anticausal, log_t[h : h + 1, :] - log[:, h : h + 1], -1e30)
                decay = jnp.exp2(gap)
                decays.append(decay)
                parts.append((cbt * decay).astype(bf16))
            both = dot(jnp.concatenate(parts, axis=0), dy)
            dxr = jnp.where(low, both[:rows], both[rows:])
            wide_ref[:, lanes] = dxr
            q1 = dy.astype(f32) * y_ref[:, lanes] - xr.astype(f32) * dxr
            hi = q1.astype(bf16)
            dn_ref[:, slice(p * 128, (p + 1) * 128)] = hi
            dn_ref[:, slice(EG + p * 128, EG + (p + 1) * 128)] = (q1 - hi.astype(f32)).astype(bf16)
            dn_ref[:, slice(2 * EG + p * 128, 2 * EG + (p + 1) * 128)] = (
                x_ref[:, lanes].astype(f32) * dxr).astype(bf16)
            zero = jnp.zeros_like(xr)
            halves = jnp.concatenate([jnp.where(low, xr, zero), jnp.where(low, zero, xr)], axis=0)
            dm = dot_nt(halves, dy)
            add = dm[:rows] * decays[0] + dm[rows:] * decays[1]
            if p == 0:
                dcb_ref[...] = add
            else:
                dcb_ref[...] += add
        wide = pl.ds(base, EG)
        dcb = dcb_ref[...].astype(bf16)
        dbg_ref[g] = dot(dcb, cg_ref[g])
        qs_ref[g] = dot(dn_ref[:, 0:EG], heads) + dot(dn_ref[:, EG : 2 * EG], heads)
        qs_ref[G + g] = dot(dn_ref[:, 2 * EG : 3 * EG], heads)
        dcg_ref[g] = (dot_tn(dcb, bg_ref[g]) + dot_nt(dyel_ref[:, wide], sin_ref[:, wide])).astype(bf16)
        return 0

    lax.fori_loop(0, G // 2, within_back, 0)
    wait_recv_all(rev_out)
    wait_send_all(fwd_back)
    link(True, gmine_ref, link_ref, reach_ref)
    start_all(rev_back)
    step2 = [second_step(0)]
    lax.fori_loop(G // 2, G, within_back, 0)
    spread_sum(0)

    wait_recv_all(rev_back)

    def finish(g, _):
        base = pl.multiple_of(g * EG, EG)
        wide = pl.ds(base, EG)
        log = lg_ref[g]
        rate = rg_ref[g]
        b_blk = bg_ref[g]
        last = log[rows - 1 : rows, :]
        to_end = jnp.exp2(last - log)
        for p in range(HG // 2):
            here = slice(p * 128, (p + 1) * 128)
            lanes = pl.ds(pl.multiple_of(base + p * 128, 128), 128)
            dyf = dy_ref[:, lanes].astype(f32)
            late = pair(to_end, p, low) * dot(b_blk, reach_ref[:, lanes])
            dxr = wide_ref[:, lanes] + late
            dy_ref[:, lanes] = (dxr * pair(rate, p, low) + pair(skip_ref[g], p, low1) * dyf).astype(bf16)
            q2 = x_ref[:, lanes].astype(f32) * late
            hi = q2.astype(bf16)
            dn_ref[:, here] = hi
            dn_ref[:, slice(EG + p * 128, EG + (p + 1) * 128)] = (q2 - hi.astype(f32)).astype(bf16)
        reach = reach_ref[:, wide]
        dbg_ref[g] += dot_nt(xw_ref[:, wide], reach)
        sums = []
        for v in (sin_ref[:, wide].astype(f32), ext_ref[0:N, wide].astype(f32)):
            v = jnp.sum(v * reach.astype(f32), axis=0, keepdims=True)
            a, b, _ = split3(jnp.broadcast_to(v, (16, EG)))
            sums.append((dot(a, heads) + dot(b, heads))[0:1])
        at_end = jnp.exp2(last) * sums[0] + sums[1]
        q2 = dot(dn_ref[:, 0:EG], heads) + dot(dn_ref[:, EG : 2 * EG], heads)
        qs_ref[g] = mask_dot(anticausal.astype(bf16), qs_ref[g] - rate * q2) + at_end
        qs_ref[G + g] += q2
        return 0

    step2.append(second_step(1))
    lax.fori_loop(0, G // 2, finish, 0)
    spread_sum(1)
    hand_all(0)
    lax.fori_loop(G // 2, G, finish, 0)
    dx_out = pltpu.make_async_copy(dy_ref, dx_ref, local_sem.at[3])
    dx_out.start()
    a_neg = -jnp.exp(al_ref[...])
    slope = jax.nn.sigmoid(dt_ref[...].astype(f32).T + bias_ref[...])
    for g in range(G):
        here = slice(g * HG, (g + 1) * HG)
        d_rate = a_neg[:, here] * qs_ref[g] + qs_ref[G + g]
        ddt_ref[here, :] = (d_rate * slope[:, here]).T.astype(bf16)
        db_ref[:, g * N : (g + 1) * N] = dbg_ref[g].astype(bf16)
        dc_ref[:, g * N : (g + 1) * N] = dcg_ref[g]

    hand_all(1)

    dx_out.wait()
    layer_copy.wait()
    dz_copy.wait()
    for part in range(2):
        own_piece(part).wait()
        send_sum(0, part).wait()
        for k in range(1, 2 * NX):
            send_sum(k, part).wait_send()
            hand_on(k, part).wait()
    for cp in sent:
        cp.wait_send()
    for part in range(2):
        for k in (1, 3):
            send_cot(k, part).wait_send()
        for side in range(2):
            hand_cot(part, side).wait_send()
    for k in (1, 3, 2):
        send_normed(k).wait_send()
    for make in (fwd_out, rev_out, rev_back):
        wait_send_all(make)
    for k in range(NDP // 2):
        send_half(k).wait_send()
    for copies in step1 + step2:
        for cp in copies:
            cp.wait_send()


def result_kernel(*refs):
    ins, outs = refs[:7], refs[7:14]
    held = refs[14:20]
    narrow, wide, sems, in_sems, out_sems = refs[20:]
    rows = narrow.shape[0] // 4
    loads = [pltpu.make_async_copy(ins[6].at[pl.ds(i * rows, rows)], narrow.at[pl.ds(i * rows, rows)], in_sems.at[i])
             for i in range(4)]
    for cp in loads:
        cp.start()
    arrays = [pltpu.make_async_copy(ins[i], held[i], sems.at[i]) for i in range(6)]
    for cp in arrays:
        cp.start()
    copies = []
    for i in range(4):
        here = pl.ds(i * rows, rows)
        loads[i].wait()
        wide[here] = narrow[here].astype(f32)
        cp = pltpu.make_async_copy(wide.at[here], outs[6].at[here], out_sems.at[i])
        cp.start()
        copies.append(cp)
    for i in range(6):
        arrays[i].wait()
        cp = pltpu.make_async_copy(held[i], outs[i], sems.at[6 + i])
        cp.start()
        copies.append(cp)
    for cp in copies:
        cp.wait()


def shards(xs, z_gate, b_proj, c_proj, dt_raw, a_log, dt_bias, d_skip, norm_gain, w_out, cotangent):
    rows = xs.shape[1]
    width = cotangent.shape[2]
    shard = w_out.shape[0]
    wide = ((rows, E), bf16)
    outs = [((rows, width), bf16), wide, wide, ((rows, G * N), bf16), ((rows, G * N), bf16), ((H, rows), bf16),
            ((shard, width), bf16)]
    state = ((N, E), bf16)
    ext = ((EXT, E), bf16)
    share = ((NCTX, EXT, SHARE), bf16)
    linked = ((NCTX, N, SHARE), bf16)
    per_group = ((G, rows, HG), f32)
    group_cols = ((G, rows, N), bf16)
    quad = ((NX, rows, E // NX), bf16)
    block = ((NDP // 2, 256, width // 2), bf16)
    scratch = [
        wide, wide, ((rows, width), bf16), wide,
        ((NDP, shard, width), bf16), ((NX * rows, width), bf16), quad, ((NX * rows, E // NX), bf16), wide, wide, ((rows, E), f32),
        ((rows, E), f32), wide, wide, wide,
        ((rows, width), f32), ((rows, rows), f32),
        ((2 * G, rows, HG), f32), ((G, rows, N), f32), group_cols,
        per_group, per_group, ((H, rows), f32), group_cols, group_cols, ((rows, 128), f32), ((G, 1, HG), f32),
        ext, share, linked, state, state, linked, state,
        ((2, NZ, 128, width // 2), bf16), block, block, ((4, NZ, 64, 3 * width // 16), bf16), ((NZ, 2, 128, 5 * width // 16), bf16),
        ((NZ, 64, 3 * width // 16), bf16), ((4, 64, 5 * width // 16), bf16), ((64, width // 2), bf16),
    ]
    sems = [9, 36, 36, 8, 8, 3, 3] + [NCTX - 1] * 8 + [NDP // 2, NDP // 2, 24, 24] + [4 * NX] * 4
    vmem = pl.BlockSpec(memory_space=pltpu.VMEM)
    hbm = pl.BlockSpec(memory_space=pl.ANY)
    layer_out, dx, dz, db, dc, ddt, gw = pl.pallas_call(
        layer_kernel,
        out_shape=[jax.ShapeDtypeStruct(s, d) for s, d in outs],
        in_specs=[hbm] * 2 + [vmem] * 7 + [hbm] * 2,
        out_specs=[hbm] * 3 + [vmem] * 3 + [hbm],
        scratch_shapes=[pltpu.VMEM(s, d) for s, d in scratch] + [pltpu.SemaphoreType.DMA((n,)) for n in sems],
        compiler_params=pltpu.CompilerParams(
            collective_id=0, has_side_effects=True, vmem_limit_bytes=VMEM_LIMIT),
    )(xs[0], z_gate[0], b_proj[0], c_proj[0], dt_raw[0].T, a_log[None], dt_bias[None],
      d_skip[None], norm_gain[None], w_out, cotangent[0])
    layer_out, dx, dz, db, dc, ddt, gw = pl.pallas_call(
        result_kernel,
        out_shape=[jax.ShapeDtypeStruct(s, d) for s, d in outs[:6]] + [jax.ShapeDtypeStruct((shard, width), f32)],
        in_specs=[hbm] * 7,
        out_specs=[hbm] * 7,
        scratch_shapes=[pltpu.VMEM(s, d) for s, d in outs[:6]]
        + [pltpu.VMEM((shard, width), bf16), pltpu.VMEM((shard, width), f32), pltpu.SemaphoreType.DMA((12,)), pltpu.SemaphoreType.DMA((4,)),
           pltpu.SemaphoreType.DMA((4,))],
        compiler_params=pltpu.CompilerParams(vmem_limit_bytes=VMEM_LIMIT),
    )(layer_out, dx, dz, db, dc, ddt, gw)
    return layer_out[None], dx[None], dz[None], db[None], dc[None], ddt.T[None], gw


def solution(mesh):
    rows = P("dp", "ctx", None)
    in_specs = (rows,) * 5 + (P(),) * 4 + (P("dp", None), rows)
    out_specs = (rows,) * 6 + (P("dp", None),)
    return jax.shard_map(shards, mesh=mesh, in_specs=in_specs, out_specs=out_specs, check_vma=False)
```

```python
import math

import jax
import jax.numpy as jnp
from jax import lax
from jax.experimental import pallas as pl
from jax.experimental.pallas import tpu as pltpu
from jax.sharding import PartitionSpec as P

H = 64
P_SIZE = 64
N = 64
G = 4
E = 4096
HG = H // G
EG = E // G
EPSILON = 1e-05
LOG2E = math.log2(math.e)
EXT = 80
bf16 = jnp.bfloat16
f32 = jnp.float32
VMEM_LIMIT = 63 * 1024 * 1024
MESH = pl.DeviceIdType.MESH


def dot(a, b):
    return lax.dot_general(a, b, (((1,), (0,)), ((), ())), preferred_element_type=f32)


def dot_nt(a, b):
    return lax.dot_general(a, b, (((1,), (1,)), ((), ())), preferred_element_type=f32)


def dot_tn(a, b):
    return lax.dot_general(a, b, (((0,), (0,)), ((), ())), preferred_element_type=f32)


def split3(v):
    a = v.astype(bf16)
    rest = v - a.astype(f32)
    b = rest.astype(bf16)
    c = (rest - b.astype(f32)).astype(bf16)
    return a, b, c


def mask_dot(mask, v):
    a, b, c = split3(v)
    return dot(mask, a) + dot(mask, b) + dot(mask, c)


def low_half(rows):
    return lax.broadcasted_iota(jnp.int32, (rows, 128), 1) < P_SIZE


def pair(values, p, low):
    return jnp.where(low, values[:, 2 * p : 2 * p + 1], values[:, 2 * p + 1 : 2 * p + 2])


NZ = 4
NX = 4
NDP = 2 * NZ
NCTX = 4 * NX
SHARE = E // NCTX


def layer_kernel(x_in, z_in, b_ref, c_ref, dt_ref, al_ref, bias_ref, skips_ref, gain_ref, w_ref, cot_ref,
                 layer_ref, dx_ref, dz_out, db_ref, dc_ref, ddt_ref, gw_ref,
                 x_ref, z_ref, out_ref, dz_ref, w_all, cot_all, nb, nrecv, xr_ref, xw_ref, y_ref, wide_ref, dn_ref, dy_ref, dyel_ref,
                 lay_ref, dcb_ref, qs_ref, dbg_ref, dcg_ref,
                 lg_ref, rg_ref, lt_ref, bg_ref, cg_ref, acc_ref, skip_ref,
                 ext_ref, mine_ref, link_ref, sin_ref, gext_ref, gmine_ref, reach_ref,
                 own_ref, other_ref, sib_ref, ra1_ref, rb1_ref, ra2_ref, rb2_ref, piece_ref,
                 local_sem, w_send, w_recv, c_send, c_recv, n_send, n_recv,
                 a_send, a_recv, o_send, o_recv, ga_send, ga_recv, go_send, go_recv,
                 b_send, b_recv, r_send, r_recv, p_send, p_recv, f_send, f_recv):
    rows = x_ref.shape[0]
    width = cot_ref.shape[1]
    half_width = width // 2
    shard = w_ref.shape[0]
    half = shard // 2
    quarter = shard // 4
    dp = lax.axis_index("dp")
    ctx = lax.axis_index("ctx")
    yh, z = dp // NZ, dp % NZ
    x, yl, core = ctx // 4, (ctx // 2) % 2, ctx % 2
    z_up, z_down = (z + 1) % NZ, (z + NZ - 1) % NZ
    z_far = (z + 2) % NZ

    def dev(yh_=yh, z_=z, x_=x, yl_=yl, core_=core):
        return {"dp": yh_ * NZ + z_, "ctx": x_ * 4 + yl_ * 2 + core_}

    up, down = dev(z_=z_up), dev(z_=z_down)
    cross = dev(yh_=1 - yh, yl_=1 - yl)
    sibling = dev(core_=1 - core)

    def remote(src, dst, send, recv, target):
        return pltpu.make_async_remote_copy(
            src_ref=src, dst_ref=dst, send_sem=send, recv_sem=recv, device_id=target, device_id_type=MESH)

    x_copy = pltpu.make_async_copy(x_in, x_ref, local_sem.at[4])
    x_copy.start()
    z_copy = pltpu.make_async_copy(z_in, z_ref, local_sem.at[5])
    z_copy.start()

    def tokens(x_, start=0, count=rows):
        return pl.ds(pl.multiple_of(x_ * rows + start, 16), count)

    barrier = pltpu.get_barrier_semaphore()

    def greet_ctx(k, _):
        pl.semaphore_signal(barrier, inc=1, device_id={"dp": dp, "ctx": (ctx + k) % NCTX}, device_id_type=MESH)
        return 0

    for other in [dev(z_=(z + k) % NZ) for k in (1, 2, 3)] + [dev(yh_=1 - yh, yl_=k) for k in (0, 1)]:
        pl.semaphore_signal(barrier, inc=1, device_id=other, device_id_type=MESH)
    lax.fori_loop(1, NCTX, greet_ctx, 0)
    rate = jax.nn.softplus(dt_ref[...].astype(f32).T + bias_ref[...])
    steps = rate * (-LOG2E * jnp.exp(al_ref[...]))
    row_pos = lax.broadcasted_iota(jnp.int32, (rows, rows), 0)
    col_pos = lax.broadcasted_iota(jnp.int32, (rows, rows), 1)
    causal = row_pos >= col_pos
    anticausal = col_pos >= row_pos
    log = mask_dot(causal.astype(bf16), steps)
    lt_ref[...] = log.T
    last = log[rows - 1 : rows, :]
    to_end = jnp.exp2(last - log)
    low = low_half(rows)
    low1 = low_half(1)
    for g in range(G):
        lg_ref[g] = log[:, g * HG : (g + 1) * HG]
        rg_ref[g] = rate[:, g * HG : (g + 1) * HG]
        skip_ref[g] = skips_ref[:, g * HG : (g + 1) * HG]
        bg_ref[g] = b_ref[:, g * N : (g + 1) * N]
        cg_ref[g] = c_ref[:, g * N : (g + 1) * N]
    own_w = pltpu.make_async_copy(w_ref, w_all.at[dp], local_sem.at[0])
    own_w.start()
    own_cot = pltpu.make_async_copy(cot_ref, cot_all.at[tokens(x)], local_sem.at[1])
    own_cot.start()
    pl.semaphore_wait(barrier, NCTX - 1 + 5)

    up_y = dev(yl_=1 - yl)
    mine, theirs = yl, 1 - yl

    def unit(yh_, z_, q, part=None):
        start = core * half + q * quarter + (0 if part is None else part * (quarter // 2))
        count = quarter if part is None else quarter // 2
        return w_all.at[yh_ * NZ + z_, pl.ds(pl.multiple_of(start, quarter // 2), count)]

    waits = {}
    sent = []

    def send_w(name, src, target, dst=None):
        i = len(waits)
        cp = remote(src, src if dst is None else dst, w_send.at[i], w_recv.at[i], target)
        cp.start()
        waits[name] = cp
        sent.append(cp)

    def arrived(*names):
        for name in names:
            waits[name].wait_recv()

    def own_unit(q, part=None):
        start = core * half + q * quarter + (0 if part is None else part * (quarter // 2))
        count = quarter if part is None else quarter // 2
        return w_ref.at[pl.ds(pl.multiple_of(start, quarter // 2), count)]

    def share(name, yh_, z_, q):
        send_w(name, unit(yh_, z_, q), sibling)

    def send_cot(k, part):
        here = pl.ds(part * (rows // 2), rows // 2)
        i = k - 1 + part
        return remote(cot_ref.at[here], cot_all.at[tokens(x, part * (rows // 2), rows // 2)], c_send.at[i], c_recv.at[i], dev(x_=(x + k) % NX))

    def hand_cot(part, side):
        k = 1 + 2 * side
        there = cot_all.at[tokens((x + NX - k) % NX, part * (rows // 2) + side * (rows // 4), rows // 4)]
        i = 4 + 2 * part + side
        return remote(there, there, c_send.at[i], c_recv.at[i], dev(x_=(x + k) % NX))

    def pass_cot(part):
        for k in (1, 3):
            send_cot(k, part).wait_recv()
        for side in range(2):
            hand_cot(part, side).start()

    def send_normed(k):
        return remote(nb.at[(x + k) % NX], nrecv.at[tokens(x)], n_send.at[k - 1], n_recv.at[k - 1], dev(x_=(x + k) % NX))

    send_w("a1", own_unit(mine), up, unit(yh, z, mine))
    send_w("a2", own_unit(mine), down, unit(yh, z, mine))
    send_w("b1", own_unit(theirs), cross, unit(yh, z, theirs))
    send_w("e1", own_unit(theirs, 1), up, unit(yh, z, theirs, 1))
    send_w("e2", own_unit(theirs, 1), down, unit(yh, z, theirs, 1))
    send_w("b2", own_unit(mine), cross, unit(yh, z, mine))
    for k in (1, 3):
        send_cot(k, 0).start()
    x_copy.wait()
    for p in range(H // 2):
        lanes = slice(p * 128, (p + 1) * 128)
        xr = x_ref[:, lanes].astype(f32) * pair(rate, p, low)
        xr_ref[:, lanes] = xr.astype(bf16)
        xw_ref[:, lanes] = (xr * pair(to_end, p, low)).astype(bf16)
        hi, mid, lo = split3(pair(last, p, low1))
        tail = jnp.concatenate([hi, mid, lo, jnp.zeros((EXT - N - 3, 128), bf16)], axis=0)
        ext_ref[N:EXT, lanes] = tail
    for g in range(G):
        lanes = slice(g * EG, (g + 1) * EG)
        state = dot_tn(bg_ref[g], xw_ref[:, lanes])
        ext_ref[0:N, lanes] = state.astype(bf16)

    def lanes_of(j):
        return pl.ds(pl.multiple_of(j * SHARE, SHARE), SHARE)

    def along(k):
        return (ctx + k) % NCTX

    def spread(ext, into, sends, recvs, k):
        return remote(ext.at[:, lanes_of(along(k))], into.at[ctx], sends.at[k - 1], recvs.at[k - 1],
                      {"dp": dp, "ctx": along(k)})

    def back(linked, into, sends, recvs, k):
        return remote(linked.at[along(k)], into.at[:, lanes_of(ctx)], sends.at[k - 1], recvs.at[k - 1],
                      {"dp": dp, "ctx": along(k)})

    def start_all(make):
        lax.fori_loop(1, NCTX, lambda k, _: (make(k).start(), 0)[1], 0)

    def wait_recv_all(make):
        lax.fori_loop(1, NCTX, lambda k, _: (make(k).wait_recv(), 0)[1], 0)

    def wait_send_all(make):
        lax.fori_loop(1, NCTX, lambda k, _: (make(k).wait_send(), 0)[1], 0)

    def link(reverse, gathered, linked, into):
        acc = jnp.zeros((N, SHARE), f32)
        for step in range(NCTX):
            j = NCTX - 1 - step if reverse else step
            linked[j] = acc.astype(bf16)
            tail = mine_ref[j, N:EXT, :].astype(f32)
            total = tail[0:1] + tail[1:2] + tail[2:3]
            acc = jnp.exp2(total) * acc + gathered[j, 0:N, :].astype(f32)
        into[:, lanes_of(ctx)] = linked[ctx]

    fwd_out = lambda k: spread(ext_ref, mine_ref, a_send, a_recv, k)
    fwd_back = lambda k: back(link_ref, sin_ref, o_send, o_recv, k)
    rev_out = lambda k: spread(gext_ref, gmine_ref, ga_send, ga_recv, k)
    rev_back = lambda k: back(link_ref, reach_ref, go_send, go_recv, k)
    start_all(fwd_out)
    mine_ref[ctx] = ext_ref[:, lanes_of(ctx)]

    def within(g, _):
        base = pl.multiple_of(g * EG, EG)
        log = lg_ref[g]
        log_t = lt_ref[pl.ds(pl.multiple_of(g * HG, HG), HG), :]
        cb = dot_nt(cg_ref[g], bg_ref[g])
        for p in range(HG // 2):
            lanes = pl.ds(pl.multiple_of(base + p * 128, 128), 128)
            parts = []
            for h in (2 * p, 2 * p + 1):
                gap = jnp.where(causal, log[:, h : h + 1] - log_t[h : h + 1, :], -1e30)
                parts.append((cb * jnp.exp2(gap)).astype(bf16))
            both = dot(jnp.concatenate(parts, axis=0), xr_ref[:, lanes])
            y_ref[:, lanes] = jnp.where(low, both[:rows], both[rows:])
        return 0

    lax.fori_loop(0, G, within, 0)
    wait_recv_all(fwd_out)
    link(False, mine_ref, link_ref, sin_ref)
    start_all(fwd_back)

    arrived("b1")
    send_w("c1", unit(1 - yh, z, mine), up)
    send_w("c2", unit(1 - yh, z, mine), down)
    arrived("a1", "a2")
    for name, z_ in (("n1", z_down), ("n2", z_up)):
        send_w(name, unit(yh, z_, mine, 0), up_y)
    for name, z_ in (("m1", z_down), ("m2", z_up)):
        send_w(name, unit(yh, z_, mine), cross)
    share("s1", yh, z_down, mine)
    share("s2", yh, z_up, mine)
    share("s3", 1 - yh, z, mine)
    pass_cot(0)
    for k in (1, 3):
        send_cot(k, 1).start()

    wait_recv_all(fwd_back)

    z_copy.wait()
    acc_ref[...] = jnp.zeros_like(acc_ref)

    def gate(g, _):
        base = pl.multiple_of(g * EG, EG)
        grown = jnp.exp2(lg_ref[g])
        c_blk = cg_ref[g]
        total = acc_ref[...]
        for p in range(HG // 2):
            lanes = pl.ds(pl.multiple_of(base + p * 128, 128), 128)
            y = y_ref[:, lanes] + pair(grown, p, low) * dot(c_blk, sin_ref[:, lanes])
            y_ref[:, lanes] = y
            out = y + pair(skip_ref[g], p, low1) * x_ref[:, lanes].astype(f32)
            zf = z_ref[:, lanes].astype(f32)
            gated = out * (zf * jax.nn.sigmoid(zf))
            wide_ref[:, lanes] = gated
            total = total + gated * gated
        acc_ref[...] = total
        return 0

    lax.fori_loop(0, G, gate, 0)
    r = lax.rsqrt(jnp.sum(acc_ref[...], axis=1, keepdims=True) * (1.0 / E) + EPSILON)

    def norm(i, _):
        for q in range(NX):
            lanes = pl.ds(pl.multiple_of(i * 512 + q * 128, 128), 128)
            nb[q, :, pl.ds(pl.multiple_of(i * 128, 128), 128)] = (
                wide_ref[:, lanes] * r * gain_ref[:, lanes]).astype(bf16)
        return 0

    lax.fori_loop(0, NDP, norm, 0)
    for k in (1, 3, 2):
        send_normed(k).start()
    nrecv[tokens(x)] = nb[x]

    own_w.wait()
    own_cot.wait()
    lay_ref[...] = jnp.zeros_like(lay_ref)

    acc_ref[...] = jnp.zeros_like(acc_ref)

    def project_back(yh_, z_):
        k = yh_ * NZ + z_
        acc = acc_ref[...]
        for q in range(NX):
            lanes = pl.ds(pl.multiple_of(k * shard + q * 128, 128), 128)
            dn = dot_nt(cot_all[tokens(x)], w_all[k, q * 128 : (q + 1) * 128, :]).astype(bf16)
            dn_ref[:, lanes] = dn
            acc = acc + dn.astype(f32) * gain_ref[:, lanes] * wide_ref[:, lanes]
        acc_ref[...] = acc

    def project_out(yh_, z_):
        k = yh_ * NZ + z_
        block = jnp.concatenate([nb[q, :, pl.ds(pl.multiple_of(k * 128, 128), 128)] for q in range(NX)], axis=1)

        def tile(n, _):
            cols = pl.ds(pl.multiple_of(n * (width // 4), width // 4), width // 4)
            lay_ref[:, cols] += dot(block, w_all[k, :, cols])
            return 0

        lax.fori_loop(0, 4, tile, 0)

    def project(yh_, z_):
        project_back(yh_, z_)
        project_out(yh_, z_)

    project(yh, z)

    arrived("c1", "c2")
    send_w("g1", unit(1 - yh, z_down, mine, 0), up)
    send_w("g2", unit(1 - yh, z_up, mine, 1), down)
    send_w("f1", unit(yh, z_down, mine, 0), up)
    send_w("f2", unit(yh, z_up, mine, 1), down)
    arrived("e2")
    send_w("f4", unit(yh, z_up, theirs, 1), down)
    share("s6", 1 - yh, z_down, mine)
    share("s7", 1 - yh, z_up, mine)
    arrived("b2")
    share("s5", 1 - yh, z, theirs)
    pass_cot(1)
    arrived("n1")
    send_w("f3", unit(yh, z_down, theirs, 0), up)
    arrived("n2", "e1")
    share("s8", yh, z_down, theirs)
    share("s9", yh, z_up, theirs)
    arrived("s3", "s5")
    project(1 - yh, z)
    arrived("g1", "g2")
    send_w("n4", unit(1 - yh, z_far, mine), up_y)
    share("s10", 1 - yh, z_far, mine)
    arrived("s1", "s8")
    project(yh, z_down)
    arrived("s2", "s9")
    project(yh, z_up)

    arrived("m1", "m2")
    share("s11", 1 - yh, z_down, theirs)
    share("s12", 1 - yh, z_up, theirs)
    arrived("f1", "f2")
    share("s4", yh, z_far, mine)
    arrived("s6", "s11")
    project(1 - yh, z_down)
    arrived("f3", "f4")
    share("s13", yh, z_far, theirs)
    arrived("s7", "s12")
    project(1 - yh, z_up)
    arrived("s4", "s13")
    project(yh, z_far)
    arrived("n4")
    share("s14", 1 - yh, z_far, theirs)

    arrived("s10", "s14")
    project_back(1 - yh, z_far)

    inner = jnp.sum(acc_ref[...], axis=1, keepdims=True) * (1.0 / E)
    scaled = r * r * inner

    def gate_back(g, _):
        base = pl.multiple_of(g * EG, EG)
        grown = jnp.exp2(lg_ref[g])
        for p in range(HG // 2):
            lanes = pl.ds(pl.multiple_of(base + p * 128, 128), 128)
            zf = z_ref[:, lanes].astype(f32)
            sig = jax.nn.sigmoid(zf)
            silu = zf * sig
            out = y_ref[:, lanes] + pair(skip_ref[g], p, low1) * x_ref[:, lanes].astype(f32)
            dg = dn_ref[:, lanes].astype(f32) * gain_ref[:, lanes]
            d_gated = r * (dg - wide_ref[:, lanes] * scaled)
            dz_ref[:, lanes] = (d_gated * out * (sig * (1.0 + zf * (1.0 - sig)))).astype(bf16)
            dy = d_gated * silu
            dy_ref[:, lanes] = dy.astype(bf16)
            dyel_ref[:, lanes] = (dy * pair(grown, p, low)).astype(bf16)
        lanes = pl.ds(base, EG)
        gext_ref[:, lanes] = dot_tn(cg_ref[g], dyel_ref[:, lanes]).astype(bf16)
        return 0

    lax.fori_loop(0, G, gate_back, 0)
    dz_copy = pltpu.make_async_copy(dz_ref, dz_out, local_sem.at[7])
    dz_copy.start()
    start_all(rev_out)
    gmine_ref[ctx] = gext_ref[:, lanes_of(ctx)]

    for part in range(2):
        for side in range(2):
            hand_cot(part, side).wait_recv()
    for k in (1, 3, 2):
        send_normed(k).wait_recv()

    def send_half(j):
        return remote(other_ref.at[j], sib_ref.at[j], b_send.at[j], b_recv.at[j], sibling)

    def product(j, side):
        cols = pl.ds(pl.multiple_of(side * half_width, half_width), half_width)
        return dot_tn(nrecv[:, pl.ds(pl.multiple_of(j * 256, 256), 256)], cot_all[:, cols]).astype(bf16)

    def weigh_other(j, _):
        other_ref[j] = product(j, 1 - core)
        send_half(j).start()
        return 0

    def weigh_own(j, _):
        part = product(j, core)
        own_ref[j // 2, 2 * (j % 2)] = part[0:128]
        own_ref[j // 2, 2 * (j % 2) + 1] = part[128:256]
        return 0

    def combine(j, _):
        send_half(j).wait_recv()
        for i in range(2):
            here = (j // 2, 2 * (j % 2) + i)
            got = sib_ref[j, i * 128 : (i + 1) * 128, :]
            own_ref[here] = (own_ref[here].astype(f32) + got.astype(f32)).astype(bf16)
        return 0

    lax.fori_loop(0, NDP // 2, weigh_other, 0)
    lax.fori_loop(0, NDP // 2, weigh_own, 0)
    lax.fori_loop(0, NDP // 2, combine, 0)

    y = 2 * yh + yl
    part_width = half_width // 2
    y_spans = (part_width // 4, part_width // 2)
    z_spans = tuple(part_width - n for n in y_spans)

    def y_first(part, whole=False):
        return pl.ds(part * part_width if whole else part * y_spans[0], y_spans[part])

    def z_first(part, whole=False):
        return pl.ds(part * part_width + y_spans[part] if whole else part * z_spans[0], z_spans[part])

    def rows_of(yl_):
        return pl.ds(pl.multiple_of(yl_ * 64, 64), 64)

    def reduce_copy(i, src, dst, target):
        return remote(src, dst, r_send.at[i], r_recv.at[i], target)

    def along_y(k):
        there = (y + k) % 4
        return there // 2, there % 2

    def first_step(part):
        copies = []
        for k in (1, 3, 2):
            yh_, yl_ = along_y(k)
            copies.append(reduce_copy(12 * part + k - 1, own_ref.at[yh_, :, rows_of(yl_), y_first(part, True)],
                                      ra1_ref.at[y, :, :, y_first(part)], dev(yh_=yh_, yl_=yl_)))
            z_ = (z + k) % NZ
            copies.append(reduce_copy(12 * part + k + 2, own_ref.at[:, z_, :, z_first(part, True)],
                                      rb1_ref.at[z, :, :, z_first(part)], dev(z_=z_)))
        for cp in copies:
            cp.start()
        return copies

    def total_of(ref, here):
        total = ref[(0, Ellipsis, here)].astype(f32)
        for q in range(1, 4):
            total = total + ref[(q, Ellipsis, here)].astype(f32)
        return total.astype(bf16)

    def second_step(part):
        for cp in step1[part]:
            cp.wait_recv()
        ya, za = y_first(part), z_first(part)
        ra1_ref[y, :, :, ya] = total_of(ra1_ref, ya)
        rb1_ref[z, :, :, za] = total_of(rb1_ref, za)
        copies = []
        for k in (1, 3, 2):
            yh_, yl_ = along_y(k)
            z_ = (z + k) % NZ
            copies.append(reduce_copy(12 * part + k + 5, ra1_ref.at[y, z_, :, ya], ra2_ref.at[z, :, ya],
                                      dev(z_=z_)))
            copies.append(reduce_copy(12 * part + k + 8, rb1_ref.at[z, yh_, rows_of(yl_), za],
                                      rb2_ref.at[y, :, za], dev(yh_=yh_, yl_=yl_)))
        for cp in copies:
            cp.start()
        ra2_ref[z, :, ya] = ra1_ref[y, z, :, ya]
        rb2_ref[y, :, za] = rb1_ref[z, yh, rows_of(yl), za]
        return copies

    def place(x_, yl_, part):
        rows_here = pl.ds(pl.multiple_of(x_ * 128 + yl_ * 64, 64), 64)
        start = core * half_width + part * (half_width // 2)
        return gw_ref.at[rows_here, pl.ds(pl.multiple_of(start, half_width // 2), half_width // 2)]

    def own_cols(part):
        return piece_ref.at[:, pl.ds(part * (half_width // 2), half_width // 2)]

    def send_sum(k, part):
        i = 8 * part + k
        if k % 2 and k > 1:
            src = place(x, 1 - yl, part)
            return remote(src, src, p_send.at[i], p_recv.at[i], dev(x_=(x + k // 2) % NX))
        target = sibling if k == 0 else dev(x_=(x + k // 2) % NX, yl_=(yl + k) % 2)
        return remote(own_cols(part), place(x, yl, part), p_send.at[i], p_recv.at[i], target)

    def hand_on(k, part):
        src = place((x + NX - k // 2) % NX, (yl + k) % 2, part)
        i = 8 * part + k
        return remote(src, src, f_send.at[i], f_recv.at[i], sibling)

    def own_piece(part):
        return pltpu.make_async_copy(own_cols(part), place(x, yl, part), local_sem.at[2 + 6 * part])

    def spread_sum(part):
        for cp in step2[part]:
            cp.wait_recv()
        piece_ref[:, y_first(part, True)] = total_of(ra2_ref, y_first(part))
        piece_ref[:, z_first(part, True)] = total_of(rb2_ref, z_first(part))
        for k in (1, 2, 6, 4, 0):
            send_sum(k, part).start()
        own_piece(part).start()

    def pass_sum(part):
        send_sum(1, part).wait_recv()
        for k in (3, 7, 5):
            send_sum(k, part).start()

    def hand_all(part):
        for k in (1, 2, 6, 4, 3, 7, 5):
            if k > 1:
                send_sum(k, part).wait_recv()
            hand_on(k, part).start()

    step1 = [first_step(0), first_step(1)]
    for part in range(2):
        ra1_ref[y, :, :, y_first(part)] = own_ref[yh, :, rows_of(yl), y_first(part, True)]
        rb1_ref[z, :, :, z_first(part)] = own_ref[:, z, :, z_first(part, True)]

    project_out(1 - yh, z_far)
    out_ref[...] = lay_ref[...].astype(bf16)
    layer_copy = pltpu.make_async_copy(out_ref, layer_ref, local_sem.at[6])
    layer_copy.start()

    e_pos = lax.broadcasted_iota(jnp.int32, (EG, HG), 0)
    h_pos = lax.broadcasted_iota(jnp.int32, (EG, HG), 1)
    heads = ((e_pos // P_SIZE) == h_pos).astype(bf16)

    def within_back(g, _):
        base = pl.multiple_of(g * EG, EG)
        log = lg_ref[g]
        log_t = lt_ref[pl.ds(pl.multiple_of(g * HG, HG), HG), :]
        cbt = dot_nt(bg_ref[g], cg_ref[g])
        for p in range(HG // 2):
            lanes = pl.ds(pl.multiple_of(base + p * 128, 128), 128)
            dy = dy_ref[:, lanes]
            xr = xr_ref[:, lanes]
            decays = []
            parts = []
            for h in (2 * p, 2 * p + 1):
                gap = jnp.where(anticausal, log_t[h : h + 1, :] - log[:, h : h + 1], -1e30)
                decay = jnp.exp2(gap)
                decays.append(decay)
                parts.append((cbt * decay).astype(bf16))
            both = dot(jnp.concatenate(parts, axis=0), dy)
            dxr = jnp.where(low, both[:rows], both[rows:])
            wide_ref[:, lanes] = dxr
            q1 = dy.astype(f32) * y_ref[:, lanes] - xr.astype(f32) * dxr
            hi = q1.astype(bf16)
            dn_ref[:, slice(p * 128, (p + 1) * 128)] = hi
            dn_ref[:, slice(EG + p * 128, EG + (p + 1) * 128)] = (q1 - hi.astype(f32)).astype(bf16)
            dn_ref[:, slice(2 * EG + p * 128, 2 * EG + (p + 1) * 128)] = (
                x_ref[:, lanes].astype(f32) * dxr).astype(bf16)
            zero = jnp.zeros_like(xr)
            halves = jnp.concatenate([jnp.where(low, xr, zero), jnp.where(low, zero, xr)], axis=0)
            dm = dot_nt(halves, dy)
            add = dm[:rows] * decays[0] + dm[rows:] * decays[1]
            if p == 0:
                dcb_ref[...] = add
            else:
                dcb_ref[...] += add
        wide = pl.ds(base, EG)
        dcb = dcb_ref[...].astype(bf16)
        dbg_ref[g] = dot(dcb, cg_ref[g])
        qs_ref[g] = dot(dn_ref[:, 0:EG], heads) + dot(dn_ref[:, EG : 2 * EG], heads)
        qs_ref[G + g] = dot(dn_ref[:, 2 * EG : 3 * EG], heads)
        dcg_ref[g] = (dot_tn(dcb, bg_ref[g]) + dot_nt(dyel_ref[:, wide], sin_ref[:, wide])).astype(bf16)
        return 0

    lax.fori_loop(0, G // 2, within_back, 0)
    wait_recv_all(rev_out)
    wait_send_all(fwd_back)
    link(True, gmine_ref, link_ref, reach_ref)
    start_all(rev_back)
    lax.fori_loop(G // 2, G, within_back, 0)
    step2 = [second_step(0)]

    wait_recv_all(rev_back)

    def finish(g, _):
        base = pl.multiple_of(g * EG, EG)
        wide = pl.ds(base, EG)
        log = lg_ref[g]
        rate = rg_ref[g]
        b_blk = bg_ref[g]
        last = log[rows - 1 : rows, :]
        to_end = jnp.exp2(last - log)
        for p in range(HG // 2):
            here = slice(p * 128, (p + 1) * 128)
            lanes = pl.ds(pl.multiple_of(base + p * 128, 128), 128)
            dyf = dy_ref[:, lanes].astype(f32)
            late = pair(to_end, p, low) * dot(b_blk, reach_ref[:, lanes])
            dxr = wide_ref[:, lanes] + late
            dy_ref[:, lanes] = (dxr * pair(rate, p, low) + pair(skip_ref[g], p, low1) * dyf).astype(bf16)
            q2 = x_ref[:, lanes].astype(f32) * late
            hi = q2.astype(bf16)
            dn_ref[:, here] = hi
            dn_ref[:, slice(EG + p * 128, EG + (p + 1) * 128)] = (q2 - hi.astype(f32)).astype(bf16)
        reach = reach_ref[:, wide]
        dbg_ref[g] += dot_nt(xw_ref[:, wide], reach)
        sums = []
        for v in (sin_ref[:, wide].astype(f32), ext_ref[0:N, wide].astype(f32)):
            v = jnp.sum(v * reach.astype(f32), axis=0, keepdims=True)
            a, b, _ = split3(jnp.broadcast_to(v, (16, EG)))
            sums.append((dot(a, heads) + dot(b, heads))[0:1])
        at_end = jnp.exp2(last) * sums[0] + sums[1]
        q2 = dot(dn_ref[:, 0:EG], heads) + dot(dn_ref[:, EG : 2 * EG], heads)
        qs_ref[g] = mask_dot(anticausal.astype(bf16), qs_ref[g] - rate * q2) + at_end
        qs_ref[G + g] += q2
        return 0

    step2.append(second_step(1))
    spread_sum(0)
    lax.fori_loop(0, G // 2, finish, 0)
    pass_sum(0)
    spread_sum(1)
    lax.fori_loop(G // 2, G, finish, 0)
    pass_sum(1)
    hand_all(0)
    dx_out = pltpu.make_async_copy(dy_ref, dx_ref, local_sem.at[3])
    dx_out.start()
    a_neg = -jnp.exp(al_ref[...])
    slope = jax.nn.sigmoid(dt_ref[...].astype(f32).T + bias_ref[...])
    for g in range(G):
        here = slice(g * HG, (g + 1) * HG)
        d_rate = a_neg[:, here] * qs_ref[g] + qs_ref[G + g]
        ddt_ref[here, :] = (d_rate * slope[:, here]).T.astype(bf16)
        db_ref[:, g * N : (g + 1) * N] = dbg_ref[g].astype(bf16)
        dc_ref[:, g * N : (g + 1) * N] = dcg_ref[g]

    hand_all(1)

    dx_out.wait()
    layer_copy.wait()
    dz_copy.wait()
    for part in range(2):
        own_piece(part).wait()
        send_sum(0, part).wait()
        for k in range(1, 2 * NX):
            send_sum(k, part).wait_send()
            hand_on(k, part).wait()
    for cp in sent:
        cp.wait_send()
    for part in range(2):
        for k in (1, 3):
            send_cot(k, part).wait_send()
        for side in range(2):
            hand_cot(part, side).wait_send()
    for k in (1, 3, 2):
        send_normed(k).wait_send()
    for make in (fwd_out, rev_out, rev_back):
        wait_send_all(make)
    for k in range(NDP // 2):
        send_half(k).wait_send()
    for copies in step1 + step2:
        for cp in copies:
            cp.wait_send()


def result_kernel(*refs):
    ins, outs = refs[:7], refs[7:14]
    held = refs[14:20]
    narrow, wide, sems, in_sems, out_sems = refs[20:]
    rows = narrow.shape[0] // 4
    loads = [pltpu.make_async_copy(ins[6].at[pl.ds(i * rows, rows)], narrow.at[pl.ds(i * rows, rows)], in_sems.at[i])
             for i in range(4)]
    for cp in loads:
        cp.start()
    arrays = [pltpu.make_async_copy(ins[i], held[i], sems.at[i]) for i in range(6)]
    for cp in arrays:
        cp.start()
    copies = []
    for i in range(4):
        here = pl.ds(i * rows, rows)
        loads[i].wait()
        wide[here] = narrow[here].astype(f32)
        cp = pltpu.make_async_copy(wide.at[here], outs[6].at[here], out_sems.at[i])
        cp.start()
        copies.append(cp)
    for i in range(6):
        arrays[i].wait()
        cp = pltpu.make_async_copy(held[i], outs[i], sems.at[6 + i])
        cp.start()
        copies.append(cp)
    for cp in copies:
        cp.wait()


def shards(xs, z_gate, b_proj, c_proj, dt_raw, a_log, dt_bias, d_skip, norm_gain, w_out, cotangent):
    rows = xs.shape[1]
    width = cotangent.shape[2]
    shard = w_out.shape[0]
    wide = ((rows, E), bf16)
    outs = [((rows, width), bf16), wide, wide, ((rows, G * N), bf16), ((rows, G * N), bf16), ((H, rows), bf16),
            ((shard, width), bf16)]
    state = ((N, E), bf16)
    ext = ((EXT, E), bf16)
    share = ((NCTX, EXT, SHARE), bf16)
    linked = ((NCTX, N, SHARE), bf16)
    per_group = ((G, rows, HG), f32)
    group_cols = ((G, rows, N), bf16)
    quad = ((NX, rows, E // NX), bf16)
    block = ((NDP // 2, 256, width // 2), bf16)
    scratch = [
        wide, wide, ((rows, width), bf16), wide,
        ((NDP, shard, width), bf16), ((NX * rows, width), bf16), quad, ((NX * rows, E // NX), bf16), wide, wide, ((rows, E), f32),
        ((rows, E), f32), wide, wide, wide,
        ((rows, width), f32), ((rows, rows), f32),
        ((2 * G, rows, HG), f32), ((G, rows, N), f32), group_cols,
        per_group, per_group, ((H, rows), f32), group_cols, group_cols, ((rows, 128), f32), ((G, 1, HG), f32),
        ext, share, linked, state, state, linked, state,
        ((2, NZ, 128, width // 2), bf16), block, block, ((4, NZ, 64, 3 * width // 16), bf16), ((NZ, 2, 128, 5 * width // 16), bf16),
        ((NZ, 64, 3 * width // 16), bf16), ((4, 64, 5 * width // 16), bf16), ((64, width // 2), bf16),
    ]
    sems = [9, 36, 36, 8, 8, 3, 3] + [NCTX - 1] * 8 + [NDP // 2, NDP // 2, 24, 24] + [4 * NX] * 4
    vmem = pl.BlockSpec(memory_space=pltpu.VMEM)
    hbm = pl.BlockSpec(memory_space=pl.ANY)
    layer_out, dx, dz, db, dc, ddt, gw = pl.pallas_call(
        layer_kernel,
        out_shape=[jax.ShapeDtypeStruct(s, d) for s, d in outs],
        in_specs=[hbm] * 2 + [vmem] * 7 + [hbm] * 2,
        out_specs=[hbm] * 3 + [vmem] * 3 + [hbm],
        scratch_shapes=[pltpu.VMEM(s, d) for s, d in scratch] + [pltpu.SemaphoreType.DMA((n,)) for n in sems],
        compiler_params=pltpu.CompilerParams(
            collective_id=0, has_side_effects=True, vmem_limit_bytes=VMEM_LIMIT),
    )(xs[0], z_gate[0], b_proj[0], c_proj[0], dt_raw[0].T, a_log[None], dt_bias[None],
      d_skip[None], norm_gain[None], w_out, cotangent[0])
    layer_out, dx, dz, db, dc, ddt, gw = pl.pallas_call(
        result_kernel,
        out_shape=[jax.ShapeDtypeStruct(s, d) for s, d in outs[:6]] + [jax.ShapeDtypeStruct((shard, width), f32)],
        in_specs=[hbm] * 7,
        out_specs=[hbm] * 7,
        scratch_shapes=[pltpu.VMEM(s, d) for s, d in outs[:6]]
        + [pltpu.VMEM((shard, width), bf16), pltpu.VMEM((shard, width), f32), pltpu.SemaphoreType.DMA((12,)), pltpu.SemaphoreType.DMA((4,)),
           pltpu.SemaphoreType.DMA((4,))],
        compiler_params=pltpu.CompilerParams(vmem_limit_bytes=VMEM_LIMIT),
    )(layer_out, dx, dz, db, dc, ddt, gw)
    return layer_out[None], dx[None], dz[None], db[None], dc[None], ddt.T[None], gw


def solution(mesh):
    rows = P("dp", "ctx", None)
    in_specs = (rows,) * 5 + (P(),) * 4 + (P("dp", None), rows)
    out_specs = (rows,) * 6 + (P("dp", None),)
    return jax.shard_map(shards, mesh=mesh, in_specs=in_specs, out_specs=out_specs, check_vma=False)
```

```python
import math

import jax
import jax.numpy as jnp
from jax import lax
from jax.experimental import pallas as pl
from jax.experimental.pallas import tpu as pltpu
from jax.sharding import PartitionSpec as P

H = 64
P_SIZE = 64
N = 64
G = 4
E = 4096
HG = H // G
EG = E // G
EPSILON = 1e-05
LOG2E = math.log2(math.e)
EXT = 80
bf16 = jnp.bfloat16
f32 = jnp.float32
VMEM_LIMIT = 63 * 1024 * 1024
MESH = pl.DeviceIdType.MESH


def dot(a, b):
    return lax.dot_general(a, b, (((1,), (0,)), ((), ())), preferred_element_type=f32)


def dot_nt(a, b):
    return lax.dot_general(a, b, (((1,), (1,)), ((), ())), preferred_element_type=f32)


def dot_tn(a, b):
    return lax.dot_general(a, b, (((0,), (0,)), ((), ())), preferred_element_type=f32)


def split3(v):
    a = v.astype(bf16)
    rest = v - a.astype(f32)
    b = rest.astype(bf16)
    c = (rest - b.astype(f32)).astype(bf16)
    return a, b, c


def mask_dot(mask, v):
    a, b, c = split3(v)
    return dot(mask, a) + dot(mask, b) + dot(mask, c)


def low_half(rows):
    return lax.broadcasted_iota(jnp.int32, (rows, 128), 1) < P_SIZE


def pair(values, p, low):
    return jnp.where(low, values[:, 2 * p : 2 * p + 1], values[:, 2 * p + 1 : 2 * p + 2])


NZ = 4
NX = 4
NDP = 2 * NZ
NCTX = 4 * NX
SHARE = E // NCTX


def layer_kernel(x_in, z_in, b_ref, c_ref, dt_ref, al_ref, bias_ref, skips_ref, gain_ref, w_ref, cot_ref,
                 layer_ref, dx_ref, dz_out, db_ref, dc_ref, ddt_ref, gw_ref,
                 x_ref, z_ref, out_ref, dz_ref, w_all, cot_all, nb, nrecv, xr_ref, xw_ref, y_ref, wide_ref, dn_ref, dy_ref, dyel_ref,
                 lay_ref, dcb_ref, qs_ref, dbg_ref, dcg_ref,
                 lg_ref, rg_ref, lt_ref, bg_ref, cg_ref, acc_ref, skip_ref,
                 ext_ref, mine_ref, link_ref, sin_ref, gext_ref, gmine_ref, reach_ref,
                 own_ref, other_ref, sib_ref, ra1_ref, rb1_ref, ra2_ref, rb2_ref, piece_ref,
                 local_sem, w_send, w_recv, c_send, c_recv, n_send, n_recv,
                 a_send, a_recv, o_send, o_recv, ga_send, ga_recv, go_send, go_recv,
                 b_send, b_recv, r_send, r_recv, p_send, p_recv, f_send, f_recv):
    rows = x_ref.shape[0]
    width = cot_ref.shape[1]
    half_width = width // 2
    shard = w_ref.shape[0]
    half = shard // 2
    quarter = shard // 4
    dp = lax.axis_index("dp")
    ctx = lax.axis_index("ctx")
    yh, z = dp // NZ, dp % NZ
    x, yl, core = ctx // 4, (ctx // 2) % 2, ctx % 2
    z_up, z_down = (z + 1) % NZ, (z + NZ - 1) % NZ
    z_far = (z + 2) % NZ

    def dev(yh_=yh, z_=z, x_=x, yl_=yl, core_=core):
        return {"dp": yh_ * NZ + z_, "ctx": x_ * 4 + yl_ * 2 + core_}

    up, down = dev(z_=z_up), dev(z_=z_down)
    cross = dev(yh_=1 - yh, yl_=1 - yl)
    sibling = dev(core_=1 - core)

    def remote(src, dst, send, recv, target):
        return pltpu.make_async_remote_copy(
            src_ref=src, dst_ref=dst, send_sem=send, recv_sem=recv, device_id=target, device_id_type=MESH)

    x_copy = pltpu.make_async_copy(x_in, x_ref, local_sem.at[4])
    x_copy.start()
    z_copy = pltpu.make_async_copy(z_in, z_ref, local_sem.at[5])
    z_copy.start()

    def tokens(x_, start=0, count=rows):
        return pl.ds(pl.multiple_of(x_ * rows + start, 16), count)

    barrier = pltpu.get_barrier_semaphore()

    def greet_ctx(k, _):
        pl.semaphore_signal(barrier, inc=1, device_id={"dp": dp, "ctx": (ctx + k) % NCTX}, device_id_type=MESH)
        return 0

    for other in [dev(z_=(z + k) % NZ) for k in (1, 2, 3)] + [dev(yh_=1 - yh, yl_=k) for k in (0, 1)]:
        pl.semaphore_signal(barrier, inc=1, device_id=other, device_id_type=MESH)
    lax.fori_loop(1, NCTX, greet_ctx, 0)
    rate = jax.nn.softplus(dt_ref[...].astype(f32).T + bias_ref[...])
    steps = rate * (-LOG2E * jnp.exp(al_ref[...]))
    row_pos = lax.broadcasted_iota(jnp.int32, (rows, rows), 0)
    col_pos = lax.broadcasted_iota(jnp.int32, (rows, rows), 1)
    causal = row_pos >= col_pos
    anticausal = col_pos >= row_pos
    log = mask_dot(causal.astype(bf16), steps)
    lt_ref[...] = log.T
    last = log[rows - 1 : rows, :]
    to_end = jnp.exp2(last - log)
    low = low_half(rows)
    low1 = low_half(1)
    for g in range(G):
        lg_ref[g] = log[:, g * HG : (g + 1) * HG]
        rg_ref[g] = rate[:, g * HG : (g + 1) * HG]
        skip_ref[g] = skips_ref[:, g * HG : (g + 1) * HG]
        bg_ref[g] = b_ref[:, g * N : (g + 1) * N]
        cg_ref[g] = c_ref[:, g * N : (g + 1) * N]
    own_w = pltpu.make_async_copy(w_ref, w_all.at[dp], local_sem.at[0])
    own_w.start()
    own_cot = pltpu.make_async_copy(cot_ref, cot_all.at[tokens(x)], local_sem.at[1])
    own_cot.start()
    pl.semaphore_wait(barrier, NCTX - 1 + 5)

    up_y = dev(yl_=1 - yl)
    mine, theirs = yl, 1 - yl

    def unit(yh_, z_, q, part=None):
        start = core * half + q * quarter + (0 if part is None else part * (quarter // 2))
        count = quarter if part is None else quarter // 2
        return w_all.at[yh_ * NZ + z_, pl.ds(pl.multiple_of(start, quarter // 2), count)]

    waits = {}
    sent = []

    def send_w(name, src, target, dst=None):
        i = len(waits)
        cp = remote(src, src if dst is None else dst, w_send.at[i], w_recv.at[i], target)
        cp.start()
        waits[name] = cp
        sent.append(cp)

    def arrived(*names):
        for name in names:
            waits[name].wait_recv()

    def own_unit(q, part=None):
        start = core * half + q * quarter + (0 if part is None else part * (quarter // 2))
        count = quarter if part is None else quarter // 2
        return w_ref.at[pl.ds(pl.multiple_of(start, quarter // 2), count)]

    def share(name, yh_, z_, q):
        send_w(name, unit(yh_, z_, q), sibling)

    def send_cot(k, part):
        here = pl.ds(part * (rows // 2), rows // 2)
        i = k - 1 + part
        return remote(cot_ref.at[here], cot_all.at[tokens(x, part * (rows // 2), rows // 2)], c_send.at[i], c_recv.at[i], dev(x_=(x + k) % NX))

    def hand_cot(part, side):
        k = 1 + 2 * side
        there = cot_all.at[tokens((x + NX - k) % NX, part * (rows // 2) + side * (rows // 4), rows // 4)]
        i = 4 + 2 * part + side
        return remote(there, there, c_send.at[i], c_recv.at[i], dev(x_=(x + k) % NX))

    def pass_cot(part):
        for k in (1, 3):
            send_cot(k, part).wait_recv()
        for side in range(2):
            hand_cot(part, side).start()

    def send_normed(k):
        return remote(nb.at[(x + k) % NX], nrecv.at[tokens(x)], n_send.at[k - 1], n_recv.at[k - 1], dev(x_=(x + k) % NX))

    send_w("a1", own_unit(mine), up, unit(yh, z, mine))
    send_w("a2", own_unit(mine), down, unit(yh, z, mine))
    send_w("b1", own_unit(theirs), cross, unit(yh, z, theirs))
    send_w("e1", own_unit(theirs, 1), up, unit(yh, z, theirs, 1))
    send_w("e2", own_unit(theirs, 1), down, unit(yh, z, theirs, 1))
    send_w("b2", own_unit(mine), cross, unit(yh, z, mine))
    for k in (1, 3):
        send_cot(k, 0).start()
    x_copy.wait()
    for p in range(H // 2):
        lanes = slice(p * 128, (p + 1) * 128)
        xr = x_ref[:, lanes].astype(f32) * pair(rate, p, low)
        xr_ref[:, lanes] = xr.astype(bf16)
        xw_ref[:, lanes] = (xr * pair(to_end, p, low)).astype(bf16)
        hi, mid, lo = split3(pair(last, p, low1))
        tail = jnp.concatenate([hi, mid, lo, jnp.zeros((EXT - N - 3, 128), bf16)], axis=0)
        ext_ref[N:EXT, lanes] = tail
    for g in range(G):
        lanes = slice(g * EG, (g + 1) * EG)
        state = dot_tn(bg_ref[g], xw_ref[:, lanes])
        ext_ref[0:N, lanes] = state.astype(bf16)

    def lanes_of(j):
        return pl.ds(pl.multiple_of(j * SHARE, SHARE), SHARE)

    def along(k):
        return (ctx + k) % NCTX

    def spread(ext, into, sends, recvs, k):
        return remote(ext.at[:, lanes_of(along(k))], into.at[ctx], sends.at[k - 1], recvs.at[k - 1],
                      {"dp": dp, "ctx": along(k)})

    def back(linked, into, sends, recvs, k):
        return remote(linked.at[along(k)], into.at[:, lanes_of(ctx)], sends.at[k - 1], recvs.at[k - 1],
                      {"dp": dp, "ctx": along(k)})

    def start_all(make):
        lax.fori_loop(1, NCTX, lambda k, _: (make(k).start(), 0)[1], 0)

    def wait_recv_all(make):
        lax.fori_loop(1, NCTX, lambda k, _: (make(k).wait_recv(), 0)[1], 0)

    def wait_send_all(make):
        lax.fori_loop(1, NCTX, lambda k, _: (make(k).wait_send(), 0)[1], 0)

    def link(reverse, gathered, linked, into):
        acc = jnp.zeros((N, SHARE), f32)
        for step in range(NCTX):
            j = NCTX - 1 - step if reverse else step
            linked[j] = acc.astype(bf16)
            tail = mine_ref[j, N:EXT, :].astype(f32)
            total = tail[0:1] + tail[1:2] + tail[2:3]
            acc = jnp.exp2(total) * acc + gathered[j, 0:N, :].astype(f32)
        into[:, lanes_of(ctx)] = linked[ctx]

    fwd_out = lambda k: spread(ext_ref, mine_ref, a_send, a_recv, k)
    fwd_back = lambda k: back(link_ref, sin_ref, o_send, o_recv, k)
    rev_out = lambda k: spread(gext_ref, gmine_ref, ga_send, ga_recv, k)
    rev_back = lambda k: back(link_ref, reach_ref, go_send, go_recv, k)
    start_all(fwd_out)
    mine_ref[ctx] = ext_ref[:, lanes_of(ctx)]

    def within(g, _):
        base = pl.multiple_of(g * EG, EG)
        log = lg_ref[g]
        log_t = lt_ref[pl.ds(pl.multiple_of(g * HG, HG), HG), :]
        cb = dot_nt(cg_ref[g], bg_ref[g])
        for p in range(HG // 2):
            lanes = pl.ds(pl.multiple_of(base + p * 128, 128), 128)
            parts = []
            for h in (2 * p, 2 * p + 1):
                gap = jnp.where(causal, log[:, h : h + 1] - log_t[h : h + 1, :], -1e30)
                parts.append((cb * jnp.exp2(gap)).astype(bf16))
            both = dot(jnp.concatenate(parts, axis=0), xr_ref[:, lanes])
            y_ref[:, lanes] = jnp.where(low, both[:rows], both[rows:])
        return 0

    lax.fori_loop(0, G, within, 0)
    wait_recv_all(fwd_out)
    link(False, mine_ref, link_ref, sin_ref)
    start_all(fwd_back)

    arrived("b1")
    send_w("c1", unit(1 - yh, z, mine), up)
    send_w("c2", unit(1 - yh, z, mine), down)
    arrived("a1", "a2")
    for name, z_ in (("n1", z_down), ("n2", z_up)):
        send_w(name, unit(yh, z_, mine, 0), up_y)
    for name, z_ in (("m1", z_down), ("m2", z_up)):
        send_w(name, unit(yh, z_, mine), cross)
    share("s1", yh, z_down, mine)
    share("s2", yh, z_up, mine)
    share("s3", 1 - yh, z, mine)
    pass_cot(0)
    for k in (1, 3):
        send_cot(k, 1).start()

    wait_recv_all(fwd_back)

    z_copy.wait()
    acc_ref[...] = jnp.zeros_like(acc_ref)

    def gate(g, _):
        base = pl.multiple_of(g * EG, EG)
        grown = jnp.exp2(lg_ref[g])
        c_blk = cg_ref[g]
        total = acc_ref[...]
        for p in range(HG // 2):
            lanes = pl.ds(pl.multiple_of(base + p * 128, 128), 128)
            y = y_ref[:, lanes] + pair(grown, p, low) * dot(c_blk, sin_ref[:, lanes])
            y_ref[:, lanes] = y
            out = y + pair(skip_ref[g], p, low1) * x_ref[:, lanes].astype(f32)
            zf = z_ref[:, lanes].astype(f32)
            gated = out * (zf * jax.nn.sigmoid(zf))
            wide_ref[:, lanes] = gated
            total = total + gated * gated
        acc_ref[...] = total
        return 0

    lax.fori_loop(0, G, gate, 0)
    r = lax.rsqrt(jnp.sum(acc_ref[...], axis=1, keepdims=True) * (1.0 / E) + EPSILON)

    def norm(i, _):
        for q in range(NX):
            lanes = pl.ds(pl.multiple_of(i * 512 + q * 128, 128), 128)
            nb[q, :, pl.ds(pl.multiple_of(i * 128, 128), 128)] = (
                wide_ref[:, lanes] * r * gain_ref[:, lanes]).astype(bf16)
        return 0

    lax.fori_loop(0, NDP, norm, 0)
    for k in (1, 3, 2):
        send_normed(k).start()
    nrecv[tokens(x)] = nb[x]

    own_w.wait()
    own_cot.wait()
    lay_ref[...] = jnp.zeros_like(lay_ref)

    acc_ref[...] = jnp.zeros_like(acc_ref)

    def project_back(yh_, z_):
        k = yh_ * NZ + z_
        acc = acc_ref[...]
        for q in range(NX):
            lanes = pl.ds(pl.multiple_of(k * shard + q * 128, 128), 128)
            dn = dot_nt(cot_all[tokens(x)], w_all[k, q * 128 : (q + 1) * 128, :]).astype(bf16)
            dn_ref[:, lanes] = dn
            acc = acc + dn.astype(f32) * gain_ref[:, lanes] * wide_ref[:, lanes]
        acc_ref[...] = acc

    def project_out(yh_, z_):
        k = yh_ * NZ + z_
        block = jnp.concatenate([nb[q, :, pl.ds(pl.multiple_of(k * 128, 128), 128)] for q in range(NX)], axis=1)

        def tile(n, _):
            cols = pl.ds(pl.multiple_of(n * (width // 4), width // 4), width // 4)
            lay_ref[:, cols] += dot(block, w_all[k, :, cols])
            return 0

        lax.fori_loop(0, 4, tile, 0)

    def project(yh_, z_):
        project_back(yh_, z_)
        project_out(yh_, z_)

    project(yh, z)

    arrived("c1", "c2")
    send_w("g1", unit(1 - yh, z_down, mine, 0), up)
    send_w("g2", unit(1 - yh, z_up, mine, 1), down)
    send_w("f1", unit(yh, z_down, mine, 0), up)
    send_w("f2", unit(yh, z_up, mine, 1), down)
    arrived("e2")
    send_w("f4", unit(yh, z_up, theirs, 1), down)
    share("s6", 1 - yh, z_down, mine)
    share("s7", 1 - yh, z_up, mine)
    arrived("b2")
    share("s5", 1 - yh, z, theirs)
    pass_cot(1)
    arrived("n1")
    send_w("f3", unit(yh, z_down, theirs, 0), up)
    arrived("n2", "e1")
    share("s8", yh, z_down, theirs)
    share("s9", yh, z_up, theirs)
    arrived("s3", "s5")
    project(1 - yh, z)
    arrived("g1", "g2")
    send_w("n4", unit(1 - yh, z_far, mine), up_y)
    share("s10", 1 - yh, z_far, mine)
    arrived("s1", "s8")
    project(yh, z_down)
    arrived("s2", "s9")
    project(yh, z_up)

    arrived("m1", "m2")
    share("s11", 1 - yh, z_down, theirs)
    share("s12", 1 - yh, z_up, theirs)
    arrived("f1", "f2")
    share("s4", yh, z_far, mine)
    arrived("s6", "s11")
    project(1 - yh, z_down)
    arrived("f3", "f4")
    share("s13", yh, z_far, theirs)
    arrived("s7", "s12")
    project(1 - yh, z_up)
    arrived("s4", "s13")
    project(yh, z_far)
    arrived("n4")
    share("s14", 1 - yh, z_far, theirs)

    for part in range(2):
        for side in range(2):
            hand_cot(part, side).wait_recv()
    for k in (1, 3, 2):
        send_normed(k).wait_recv()

    def send_half(j):
        return remote(other_ref.at[j], sib_ref.at[j], b_send.at[j], b_recv.at[j], sibling)

    def product(j, side):
        cols = pl.ds(pl.multiple_of(side * half_width, half_width), half_width)
        return dot_tn(nrecv[:, pl.ds(pl.multiple_of(j * 256, 256), 256)], cot_all[:, cols]).astype(bf16)

    def weigh_other(j, _):
        other_ref[j] = product(j, 1 - core)
        send_half(j).start()
        return 0

    def weigh_own(j, _):
        part = product(j, core)
        own_ref[j // 2, 2 * (j % 2)] = part[0:128]
        own_ref[j // 2, 2 * (j % 2) + 1] = part[128:256]
        return 0

    def combine(j, _):
        send_half(j).wait_recv()
        for i in range(2):
            here = (j // 2, 2 * (j % 2) + i)
            got = sib_ref[j, i * 128 : (i + 1) * 128, :]
            own_ref[here] = (own_ref[here].astype(f32) + got.astype(f32)).astype(bf16)
        return 0

    lax.fori_loop(0, NDP // 2, weigh_other, 0)
    lax.fori_loop(0, NDP // 2, weigh_own, 0)
    lax.fori_loop(0, NDP // 2, combine, 0)

    y = 2 * yh + yl
    part_width = half_width // 2
    y_span = part_width // 4
    z_span = part_width - y_span

    def y_first(part, start=0):
        return pl.ds(part * start + part * (0 if start else y_span), y_span)

    def z_first(part, start=0):
        return pl.ds(part * start + (y_span if start else part * z_span), z_span)

    def rows_of(yl_):
        return pl.ds(pl.multiple_of(yl_ * 64, 64), 64)

    def reduce_copy(i, src, dst, target):
        return remote(src, dst, r_send.at[i], r_recv.at[i], target)

    def along_y(k):
        there = (y + k) % 4
        return there // 2, there % 2

    def first_step(part):
        copies = []
        for k in (1, 3, 2):
            yh_, yl_ = along_y(k)
            copies.append(reduce_copy(12 * part + k - 1, own_ref.at[yh_, :, rows_of(yl_), y_first(part, part_width)],
                                      ra1_ref.at[y, :, :, y_first(part)], dev(yh_=yh_, yl_=yl_)))
            z_ = (z + k) % NZ
            copies.append(reduce_copy(12 * part + k + 2, own_ref.at[:, z_, :, z_first(part, part_width)],
                                      rb1_ref.at[z, :, :, z_first(part)], dev(z_=z_)))
        for cp in copies:
            cp.start()
        return copies

    def total_of(ref, here):
        total = ref[(0, Ellipsis, here)].astype(f32)
        for q in range(1, 4):
            total = total + ref[(q, Ellipsis, here)].astype(f32)
        return total.astype(bf16)

    def second_step(part):
        for cp in step1[part]:
            cp.wait_recv()
        ya, za = y_first(part), z_first(part)
        ra1_ref[y, :, :, ya] = total_of(ra1_ref, ya)
        rb1_ref[z, :, :, za] = total_of(rb1_ref, za)
        copies = []
        for k in (1, 3, 2):
            yh_, yl_ = along_y(k)
            z_ = (z + k) % NZ
            copies.append(reduce_copy(12 * part + k + 5, ra1_ref.at[y, z_, :, ya], ra2_ref.at[z, :, ya],
                                      dev(z_=z_)))
            copies.append(reduce_copy(12 * part + k + 8, rb1_ref.at[z, yh_, rows_of(yl_), za],
                                      rb2_ref.at[y, :, za], dev(yh_=yh_, yl_=yl_)))
        for cp in copies:
            cp.start()
        ra2_ref[z, :, ya] = ra1_ref[y, z, :, ya]
        rb2_ref[y, :, za] = rb1_ref[z, yh, rows_of(yl), za]
        return copies

    def place(x_, yl_, part):
        rows_here = pl.ds(pl.multiple_of(x_ * 128 + yl_ * 64, 64), 64)
        start = core * half_width + part * (half_width // 2)
        return gw_ref.at[rows_here, pl.ds(pl.multiple_of(start, half_width // 2), half_width // 2)]

    def own_cols(part):
        return piece_ref.at[:, pl.ds(part * (half_width // 2), half_width // 2)]

    def send_sum(k, part):
        i = 8 * part + k
        if part == 0 and k in (3, 5, 7):
            src = place(x, 1 - yl, part)
            return remote(src, src, p_send.at[i], p_recv.at[i], dev(x_=(x + k // 2) % NX))
        target = sibling if k == 0 else dev(x_=(x + k // 2) % NX, yl_=(yl + k) % 2)
        return remote(own_cols(part), place(x, yl, part), p_send.at[i], p_recv.at[i], target)

    def hand_on(k, part):
        src = place((x + NX - k // 2) % NX, (yl + k) % 2, part)
        i = 8 * part + k
        return remote(src, src, f_send.at[i], f_recv.at[i], sibling)

    def own_piece(part):
        return pltpu.make_async_copy(own_cols(part), place(x, yl, part), local_sem.at[2 + 6 * part])

    def spread_sum(part):
        for cp in step2[part]:
            cp.wait_recv()
        piece_ref[:, y_first(part, part_width)] = total_of(ra2_ref, y_first(part))
        piece_ref[:, z_first(part, part_width)] = total_of(rb2_ref, z_first(part))
        for k in (1, 2, 6, 4, 0) if part == 0 else (2, 6, 4, 1, 3, 7, 5, 0):
            send_sum(k, part).start()
        own_piece(part).start()

    def pass_sum():
        send_sum(1, 0).wait_recv()
        for k in (3, 7, 5):
            send_sum(k, 0).start()

    def hand_all(part):
        for k in (2, 6, 1, 3, 7, 4, 5):
            if part == 1 or k != 1:
                send_sum(k, part).wait_recv()
            hand_on(k, part).start()

    step1 = [first_step(0), first_step(1)]
    for part in range(2):
        ra1_ref[y, :, :, y_first(part)] = own_ref[yh, :, rows_of(yl), y_first(part, part_width)]
        rb1_ref[z, :, :, z_first(part)] = own_ref[:, z, :, z_first(part, part_width)]

    arrived("s10", "s14")
    project_back(1 - yh, z_far)

    inner = jnp.sum(acc_ref[...], axis=1, keepdims=True) * (1.0 / E)
    scaled = r * r * inner

    def gate_back(g, _):
        base = pl.multiple_of(g * EG, EG)
        grown = jnp.exp2(lg_ref[g])
        for p in range(HG // 2):
            lanes = pl.ds(pl.multiple_of(base + p * 128, 128), 128)
            zf = z_ref[:, lanes].astype(f32)
            sig = jax.nn.sigmoid(zf)
            silu = zf * sig
            out = y_ref[:, lanes] + pair(skip_ref[g], p, low1) * x_ref[:, lanes].astype(f32)
            dg = dn_ref[:, lanes].astype(f32) * gain_ref[:, lanes]
            d_gated = r * (dg - wide_ref[:, lanes] * scaled)
            dz_ref[:, lanes] = (d_gated * out * (sig * (1.0 + zf * (1.0 - sig)))).astype(bf16)
            dy = d_gated * silu
            dy_ref[:, lanes] = dy.astype(bf16)
            dyel_ref[:, lanes] = (dy * pair(grown, p, low)).astype(bf16)
        lanes = pl.ds(base, EG)
        gext_ref[:, lanes] = dot_tn(cg_ref[g], dyel_ref[:, lanes]).astype(bf16)
        return 0

    lax.fori_loop(0, G, gate_back, 0)
    dz_copy = pltpu.make_async_copy(dz_ref, dz_out, local_sem.at[7])
    dz_copy.start()
    start_all(rev_out)
    gmine_ref[ctx] = gext_ref[:, lanes_of(ctx)]
    project_out(1 - yh, z_far)
    out_ref[...] = lay_ref[...].astype(bf16)
    layer_copy = pltpu.make_async_copy(out_ref, layer_ref, local_sem.at[6])
    layer_copy.start()

    e_pos = lax.broadcasted_iota(jnp.int32, (EG, HG), 0)
    h_pos = lax.broadcasted_iota(jnp.int32, (EG, HG), 1)
    heads = ((e_pos // P_SIZE) == h_pos).astype(bf16)

    def within_back(g, _):
        base = pl.multiple_of(g * EG, EG)
        log = lg_ref[g]
        log_t = lt_ref[pl.ds(pl.multiple_of(g * HG, HG), HG), :]
        cbt = dot_nt(bg_ref[g], cg_ref[g])
        for p in range(HG // 2):
            lanes = pl.ds(pl.multiple_of(base + p * 128, 128), 128)
            dy = dy_ref[:, lanes]
            xr = xr_ref[:, lanes]
            decays = []
            parts = []
            for h in (2 * p, 2 * p + 1):
                gap = jnp.where(anticausal, log_t[h : h + 1, :] - log[:, h : h + 1], -1e30)
                decay = jnp.exp2(gap)
                decays.append(decay)
                parts.append((cbt * decay).astype(bf16))
            both = dot(jnp.concatenate(parts, axis=0), dy)
            dxr = jnp.where(low, both[:rows], both[rows:])
            wide_ref[:, lanes] = dxr
            q1 = dy.astype(f32) * y_ref[:, lanes] - xr.astype(f32) * dxr
            hi = q1.astype(bf16)
            dn_ref[:, slice(p * 128, (p + 1) * 128)] = hi
            dn_ref[:, slice(EG + p * 128, EG + (p + 1) * 128)] = (q1 - hi.astype(f32)).astype(bf16)
            dn_ref[:, slice(2 * EG + p * 128, 2 * EG + (p + 1) * 128)] = (
                x_ref[:, lanes].astype(f32) * dxr).astype(bf16)
            zero = jnp.zeros_like(xr)
            halves = jnp.concatenate([jnp.where(low, xr, zero), jnp.where(low, zero, xr)], axis=0)
            dm = dot_nt(halves, dy)
            add = dm[:rows] * decays[0] + dm[rows:] * decays[1]
            if p == 0:
                dcb_ref[...] = add
            else:
                dcb_ref[...] += add
        wide = pl.ds(base, EG)
        dcb = dcb_ref[...].astype(bf16)
        dbg_ref[g] = dot(dcb, cg_ref[g])
        qs_ref[g] = dot(dn_ref[:, 0:EG], heads) + dot(dn_ref[:, EG : 2 * EG], heads)
        qs_ref[G + g] = dot(dn_ref[:, 2 * EG : 3 * EG], heads)
        dcg_ref[g] = (dot_tn(dcb, bg_ref[g]) + dot_nt(dyel_ref[:, wide], sin_ref[:, wide])).astype(bf16)
        return 0

    lax.fori_loop(0, G // 2, within_back, 0)
    step2 = [second_step(0)]
    lax.fori_loop(G // 2, G, within_back, 0)
    wait_recv_all(rev_out)
    wait_send_all(fwd_back)
    link(True, gmine_ref, link_ref, reach_ref)
    start_all(rev_back)

    step2.append(second_step(1))
    spread_sum(0)
    wait_recv_all(rev_back)

    def finish(g, _):
        base = pl.multiple_of(g * EG, EG)
        wide = pl.ds(base, EG)
        log = lg_ref[g]
        rate = rg_ref[g]
        b_blk = bg_ref[g]
        last = log[rows - 1 : rows, :]
        to_end = jnp.exp2(last - log)
        for p in range(HG // 2):
            here = slice(p * 128, (p + 1) * 128)
            lanes = pl.ds(pl.multiple_of(base + p * 128, 128), 128)
            dyf = dy_ref[:, lanes].astype(f32)
            late = pair(to_end, p, low) * dot(b_blk, reach_ref[:, lanes])
            dxr = wide_ref[:, lanes] + late
            dy_ref[:, lanes] = (dxr * pair(rate, p, low) + pair(skip_ref[g], p, low1) * dyf).astype(bf16)
            q2 = x_ref[:, lanes].astype(f32) * late
            hi = q2.astype(bf16)
            dn_ref[:, here] = hi
            dn_ref[:, slice(EG + p * 128, EG + (p + 1) * 128)] = (q2 - hi.astype(f32)).astype(bf16)
        reach = reach_ref[:, wide]
        dbg_ref[g] += dot_nt(xw_ref[:, wide], reach)
        sums = []
        for v in (sin_ref[:, wide].astype(f32), ext_ref[0:N, wide].astype(f32)):
            v = jnp.sum(v * reach.astype(f32), axis=0, keepdims=True)
            a, b, _ = split3(jnp.broadcast_to(v, (16, EG)))
            sums.append((dot(a, heads) + dot(b, heads))[0:1])
        at_end = jnp.exp2(last) * sums[0] + sums[1]
        q2 = dot(dn_ref[:, 0:EG], heads) + dot(dn_ref[:, EG : 2 * EG], heads)
        qs_ref[g] = mask_dot(anticausal.astype(bf16), qs_ref[g] - rate * q2) + at_end
        qs_ref[G + g] += q2
        return 0

    lax.fori_loop(0, G // 2, finish, 0)
    pass_sum()
    spread_sum(1)
    lax.fori_loop(G // 2, G, finish, 0)
    hand_all(0)
    dx_out = pltpu.make_async_copy(dy_ref, dx_ref, local_sem.at[3])
    dx_out.start()
    a_neg = -jnp.exp(al_ref[...])
    slope = jax.nn.sigmoid(dt_ref[...].astype(f32).T + bias_ref[...])
    for g in range(G):
        here = slice(g * HG, (g + 1) * HG)
        d_rate = a_neg[:, here] * qs_ref[g] + qs_ref[G + g]
        ddt_ref[here, :] = (d_rate * slope[:, here]).T.astype(bf16)
        db_ref[:, g * N : (g + 1) * N] = dbg_ref[g].astype(bf16)
        dc_ref[:, g * N : (g + 1) * N] = dcg_ref[g]

    hand_all(1)

    dx_out.wait()
    layer_copy.wait()
    dz_copy.wait()
    for part in range(2):
        own_piece(part).wait()
        send_sum(0, part).wait()
        for k in range(1, 2 * NX):
            send_sum(k, part).wait_send()
            hand_on(k, part).wait()
    for cp in sent:
        cp.wait_send()
    for part in range(2):
        for k in (1, 3):
            send_cot(k, part).wait_send()
        for side in range(2):
            hand_cot(part, side).wait_send()
    for k in (1, 3, 2):
        send_normed(k).wait_send()
    for make in (fwd_out, rev_out, rev_back):
        wait_send_all(make)
    for k in range(NDP // 2):
        send_half(k).wait_send()
    for copies in step1 + step2:
        for cp in copies:
            cp.wait_send()


def result_kernel(*refs):
    ins, outs = refs[:7], refs[7:14]
    held = refs[14:20]
    narrow, wide, sems, in_sems, out_sems = refs[20:]
    rows = narrow.shape[0] // 4
    loads = [pltpu.make_async_copy(ins[6].at[pl.ds(i * rows, rows)], narrow.at[pl.ds(i * rows, rows)], in_sems.at[i])
             for i in range(4)]
    for cp in loads:
        cp.start()
    arrays = [pltpu.make_async_copy(ins[i], held[i], sems.at[i]) for i in range(6)]
    for cp in arrays:
        cp.start()
    copies = []
    for i in range(4):
        here = pl.ds(i * rows, rows)
        loads[i].wait()
        wide[here] = narrow[here].astype(f32)
        cp = pltpu.make_async_copy(wide.at[here], outs[6].at[here], out_sems.at[i])
        cp.start()
        copies.append(cp)
    for i in range(6):
        arrays[i].wait()
        cp = pltpu.make_async_copy(held[i], outs[i], sems.at[6 + i])
        cp.start()
        copies.append(cp)
    for cp in copies:
        cp.wait()


def shards(xs, z_gate, b_proj, c_proj, dt_raw, a_log, dt_bias, d_skip, norm_gain, w_out, cotangent):
    rows = xs.shape[1]
    width = cotangent.shape[2]
    shard = w_out.shape[0]
    wide = ((rows, E), bf16)
    outs = [((rows, width), bf16), wide, wide, ((rows, G * N), bf16), ((rows, G * N), bf16), ((H, rows), bf16),
            ((shard, width), bf16)]
    state = ((N, E), bf16)
    ext = ((EXT, E), bf16)
    share = ((NCTX, EXT, SHARE), bf16)
    linked = ((NCTX, N, SHARE), bf16)
    per_group = ((G, rows, HG), f32)
    group_cols = ((G, rows, N), bf16)
    quad = ((NX, rows, E // NX), bf16)
    block = ((NDP // 2, 256, width // 2), bf16)
    scratch = [
        wide, wide, ((rows, width), bf16), wide,
        ((NDP, shard, width), bf16), ((NX * rows, width), bf16), quad, ((NX * rows, E // NX), bf16), wide, wide, ((rows, E), f32),
        ((rows, E), f32), wide, wide, wide,
        ((rows, width), f32), ((rows, rows), f32),
        ((2 * G, rows, HG), f32), ((G, rows, N), f32), group_cols,
        per_group, per_group, ((H, rows), f32), group_cols, group_cols, ((rows, 128), f32), ((G, 1, HG), f32),
        ext, share, linked, state, state, linked, state,
        ((2, NZ, 128, width // 2), bf16), block, block, ((4, NZ, 64, width // 8), bf16), ((NZ, 2, 128, 3 * width // 8), bf16),
        ((NZ, 64, width // 8), bf16), ((4, 64, 3 * width // 8), bf16), ((64, width // 2), bf16),
    ]
    sems = [9, 36, 36, 8, 8, 3, 3] + [NCTX - 1] * 8 + [NDP // 2, NDP // 2, 24, 24] + [4 * NX] * 4
    vmem = pl.BlockSpec(memory_space=pltpu.VMEM)
    hbm = pl.BlockSpec(memory_space=pl.ANY)
    layer_out, dx, dz, db, dc, ddt, gw = pl.pallas_call(
        layer_kernel,
        out_shape=[jax.ShapeDtypeStruct(s, d) for s, d in outs],
        in_specs=[hbm] * 2 + [vmem] * 7 + [hbm] * 2,
        out_specs=[hbm] * 3 + [vmem] * 3 + [hbm],
        scratch_shapes=[pltpu.VMEM(s, d) for s, d in scratch] + [pltpu.SemaphoreType.DMA((n,)) for n in sems],
        compiler_params=pltpu.CompilerParams(
            collective_id=0, has_side_effects=True, vmem_limit_bytes=VMEM_LIMIT),
    )(xs[0], z_gate[0], b_proj[0], c_proj[0], dt_raw[0].T, a_log[None], dt_bias[None],
      d_skip[None], norm_gain[None], w_out, cotangent[0])
    layer_out, dx, dz, db, dc, ddt, gw = pl.pallas_call(
        result_kernel,
        out_shape=[jax.ShapeDtypeStruct(s, d) for s, d in outs[:6]] + [jax.ShapeDtypeStruct((shard, width), f32)],
        in_specs=[hbm] * 7,
        out_specs=[hbm] * 7,
        scratch_shapes=[pltpu.VMEM(s, d) for s, d in outs[:6]]
        + [pltpu.VMEM((shard, width), bf16), pltpu.VMEM((shard, width), f32), pltpu.SemaphoreType.DMA((12,)), pltpu.SemaphoreType.DMA((4,)),
           pltpu.SemaphoreType.DMA((4,))],
        compiler_params=pltpu.CompilerParams(vmem_limit_bytes=VMEM_LIMIT),
    )(layer_out, dx, dz, db, dc, ddt, gw)
    return layer_out[None], dx[None], dz[None], db[None], dc[None], ddt.T[None], gw


def solution(mesh):
    rows = P("dp", "ctx", None)
    in_specs = (rows,) * 5 + (P(),) * 4 + (P("dp", None), rows)
    out_specs = (rows,) * 6 + (P("dp", None),)
    return jax.shard_map(shards, mesh=mesh, in_specs=in_specs, out_specs=out_specs, check_vma=False)
```
